32 devices in a mesh: ctx: 8 (over y, x, core), fsdp: 4 (over z).
Axes of the slice: x: 2, y: 2, z: 4, core: 2. Of those that a mesh axis runs over, the one named last changes fastest.
Arguments:
- tokens: bfloat16 [4, 2, 1024, 1024], P('fsdp', None, 'ctx'), may hold values from -6 to 6
- doc_ids: int32 [4, 2, 1024], P('fsdp', None, 'ctx'), may hold values from 0 to 3, as said below
- alibi_slopes: float32 [16], replicated, may hold values from 2.4414063e-05 to 0.05
- ln1_gain: bfloat16 [1024], P('fsdp'), may hold values from 0.5 to 1.5
- ln1_shift: bfloat16 [1024], P('fsdp'), may hold values from -1.75 to 1.75
- qkv_weight: bfloat16 [3072, 1024], P('fsdp'), may hold values from -0.1875 to 0.1875
- qkv_bias: bfloat16 [2048], P('fsdp'), may hold values from -1.75 to 1.75
- out_weight: bfloat16 [1024, 1024], P('fsdp'), may hold values from -0.75 to 0.75
- out_bias: bfloat16 [1024], P('fsdp'), may hold values from -1.75 to 1.75
- ln2_gain: bfloat16 [1024], P('fsdp'), may hold values from 0.5 to 1.5
- ln2_shift: bfloat16 [1024], P('fsdp'), may hold values from -1.75 to 1.75
- up_weight: bfloat16 [4096, 1024], P('fsdp'), may hold values from -0.1875 to 0.1875
- up_bias: bfloat16 [4096], P('fsdp'), may hold values from -1.75 to 1.75
- down_weight: bfloat16 [4096, 1024], P('fsdp'), may hold values from -0.09375 to 0.09375
- down_bias: bfloat16 [1024], P('fsdp'), may hold values from -1.75 to 1.75
- cotangent: bfloat16 [4, 2, 1024, 1024], P('fsdp', None, 'ctx'), may hold values from -6 to 6
Outputs:
- layer_out: bfloat16 [4, 2, 1024, 1024], P('fsdp', None, 'ctx')
- input_grad: bfloat16 [4, 2, 1024, 1024], P('fsdp', None, 'ctx')
- ln1_gain_grad: float32 [1024], P('fsdp')
- ln1_shift_grad: float32 [1024], P('fsdp')
- qkv_weight_grad: float32 [3072, 1024], P('fsdp')
- qkv_bias_grad: float32 [2048], P('fsdp')
- out_weight_grad: float32 [1024, 1024], P('fsdp')
- out_bias_grad: float32 [1024], P('fsdp')
- ln2_gain_grad: float32 [1024], P('fsdp')
- ln2_shift_grad: float32 [1024], P('fsdp')
- up_weight_grad: float32 [4096, 1024], P('fsdp')
- up_bias_grad: float32 [4096], P('fsdp')
- down_weight_grad: float32 [4096, 1024], P('fsdp')
- down_bias_grad: float32 [1024], P('fsdp')
The draws below stay inside these ranges and needn't reach their ends.
Inputs may be any that keep to these rules, and one draw needn't show every extreme that they name: `doc_ids`: taken in position order, the ids of a sequence start at 0, never fall and rise by at most one from a position to the next; every sequence ends with id 1024 // 512 + 1, in a document that runs from position 1024 or earlier to position 2047.
All inputs are finite; a program needn't handle non-finite values.
Results may differ from the reference program's by a relative error of at most 0.033.
Values may be sent and summed in bfloat16 or wider, within the bound.
No kernel may reach another device: no remote copies, remote signals or barrier semaphores. Data moves between devices by JAX's collectives and lax.ppermute only.
A program may use at most 256 MiB of HBM per device.

```python
import math
import jax
import jax.numpy as jnp
from jax import lax

D = 1024
HEADS = 16
FF = 4096
DOCLEN = 512
SEQS = 4
LEN = 2048
HALF = 1024


def draw_doc_ids(key, part):
    key = jax.random.fold_in(key, 11)
    usable = HALF - HALF // 4 - 1
    starts_count = HALF // DOCLEN

    def one_sequence(seq_key):
        start_key, cut_key = jax.random.split(seq_key)
        start = HALF - jax.random.randint(start_key, (), 0, HALF // 4 + 1)
        place = jnp.arange(LEN, dtype=jnp.int32)
        chosen = (jax.random.permutation(cut_key, usable) + 1)[:starts_count]
        cuts = jnp.zeros((LEN,), jnp.int32).at[chosen].set(1) > 0
        flags = cuts | (place == start)
        numbers = jnp.cumsum(flags.astype(jnp.int32)).astype(jnp.int32)
        return jnp.stack([numbers[:HALF], jnp.flip(numbers[HALF:])])
    return jax.vmap(one_sequence)(jax.random.split(key, SEQS))


def block_scale(key, extent, pieces, low, top_value):
    level, own = 1.0, jax.random.fold_in(key, 6)
    for axis_at, blocks in pieces:
        steps = jnp.exp(jax.random.uniform(jax.random.fold_in(own, axis_at), (blocks,), jnp.float32, low / len(pieces), top_value / len(pieces)))
        level = level * jnp.repeat(steps, extent[axis_at] // blocks).reshape([-1 if axis == axis_at else 1 for axis in range(len(extent))])
    return level


def scatter_about(key, dims, scale, reach, cuts=(), kind=jnp.bfloat16):
    factor_of = block_scale(key, dims, cuts, -0.22, 0.18) if cuts else 1.0
    values = jax.random.normal(key, dims, jnp.float32) * scale * factor_of
    return jnp.minimum(jnp.maximum(values, -reach), reach).astype(kind)


def setup_inputs(seed: int = 0) -> dict:
    key_of = jax.random.split(jax.random.key(seed), 17)
    tokens = scatter_about(key_of[0], (SEQS, 2, HALF, D), 1.0, 6.0, ((0, 4), (2, 8)))
    doc_ids = draw_doc_ids(jax.random.fold_in(key_of[16], 71), 0)
    alibi_slopes = jnp.clip(jnp.exp(jax.random.uniform(key_of[2], (HEADS,), jnp.float32, math.log(2.441406286379788e-05), math.log(0.05))), 2.441406286379788e-05, 0.05)
    ln1_gain = jnp.clip(1.0 + 0.1 * jax.random.normal(key_of[3], (D,), jnp.float32), 0.5, 1.5).astype(jnp.bfloat16)
    ln1_shift = scatter_about(key_of[4], (D,), 0.3, 1.75, ((0, 4),))
    qkv_weight = scatter_about(key_of[5], (3 * D, D), D ** -0.5, 0.1875, ((0, 4),))
    qkv_bias = scatter_about(key_of[6], (2 * D,), 0.3, 1.75, ((0, 4),))
    out_weight = scatter_about(key_of[7], (D, D), (D // 16) ** -0.5, 0.75, ((0, 4),))
    out_bias = scatter_about(key_of[8], (D,), 0.3, 1.75, ((0, 4),))
    ln2_gain = jnp.clip(1.0 + 0.1 * jax.random.normal(key_of[9], (D,), jnp.float32), 0.5, 1.5).astype(jnp.bfloat16)
    ln2_shift = scatter_about(key_of[10], (D,), 0.3, 1.75, ((0, 4),))
    up_weight = scatter_about(key_of[11], (FF, D), D ** -0.5, 0.1875, ((0, 4),))
    up_bias = scatter_about(key_of[12], (FF,), 0.3, 1.75, ((0, 4),))
    down_weight = scatter_about(key_of[13], (FF, D), FF ** -0.5, 0.09375, ((0, 4),))
    down_bias = scatter_about(key_of[14], (D,), 0.3, 1.75, ((0, 4),))
    cotangent = scatter_about(key_of[15], (SEQS, 2, HALF, D), 1.0, 6.0, ((0, 4), (2, 8)))
    return dict(tokens=tokens, doc_ids=doc_ids, alibi_slopes=alibi_slopes, ln1_gain=ln1_gain, ln1_shift=ln1_shift, qkv_weight=qkv_weight, qkv_bias=qkv_bias, out_weight=out_weight, out_bias=out_bias, ln2_gain=ln2_gain, ln2_shift=ln2_shift, up_weight=up_weight, up_bias=up_bias, down_weight=down_weight, down_bias=down_bias, cotangent=cotangent)


EPS = 1e-05
MASKED = -1e+30
HIGH = lax.Precision.HIGHEST

@jax.custom_vjp
def low(v):
    return lax.optimization_barrier(v.astype(jnp.bfloat16)).astype(jnp.float32)

@jax.custom_vjp
def low_back(v):
    return v

def low_keep(v):
    return (low(v), None)

def low_pass(kept, grad):
    return (grad,)

def back_keep(v):
    return (v, None)

def back_low(kept, grad):
    return (low(grad),)
low.defvjp(low_keep, low_pass)
low_back.defvjp(back_keep, back_low)

def layer_norm(v, gain, shift):
    mean = lax.optimization_barrier(jnp.mean(v, axis=-1, keepdims=True))
    centered = v - mean
    spread = lax.optimization_barrier(jnp.mean(centered * centered, axis=-1, keepdims=True))
    return centered * lax.rsqrt(spread + EPS) * gain + shift

def to_positions(stored):
    return jnp.concatenate([stored[:, 0], jnp.flip(stored[:, 1], axis=1)], axis=1)

def to_storage(natural):
    middle = natural.shape[1] // 2
    return jnp.stack([natural[:, :middle], jnp.flip(natural[:, middle:], axis=1)], axis=1)

def attend(query3, start, keys3, values3, docs, slopes):
    seq_len = keys3.shape[0]
    rows = 512 if seq_len % 512 == 0 else seq_len
    scale = keys3.shape[2] ** (-0.5)
    block = lax.dynamic_slice_in_dim(query3, start, rows)
    query_pos = start + jnp.arange(rows, dtype=jnp.int32)
    key_pos = jnp.arange(seq_len, dtype=jnp.int32)
    query_doc = lax.dynamic_slice_in_dim(docs, start, rows)
    raw = jnp.einsum('qhe,khe->hqk', block, keys3, precision=HIGH) * scale
    distance = (query_pos[:, None] - key_pos[None, :]).astype(jnp.float32)
    scores = low_back(raw - slopes[:, None, None] * distance[None])
    allowed = ((key_pos[None, :] <= query_pos[:, None]) & (docs[None, :] == query_doc[:, None]))[None]
    masked = jnp.where(allowed, scores, MASKED)
    top = lax.optimization_barrier(jnp.max(masked, axis=2, keepdims=True))
    weights = jnp.where(allowed, jnp.exp(masked - top), 0.0)
    probs = low(weights / lax.optimization_barrier(jnp.sum(weights, axis=2, keepdims=True)))
    return jnp.einsum('hqk,khe->qhe', probs, values3, precision=HIGH)

def forward(rows_in, params, slopes, docs):
    ln1_gain, ln1_shift, qkv_weight, qkv_bias, out_weight, out_bias, ln2_gain, ln2_shift, up_weight, up_bias, down_weight, down_bias = params
    seq_len, width = rows_in.shape
    heads = slopes.shape[0]
    head = width // heads
    h_one = low(layer_norm(rows_in, ln1_gain, ln1_shift))
    joined = jnp.einsum('ti,oi->to', h_one, qkv_weight, precision=HIGH)
    query = low(low_back(joined[:, :width] + qkv_bias[:width]))
    keys = low(low_back(joined[:, width:2 * width]))
    values = low(low_back(joined[:, 2 * width:] + qkv_bias[width:]))
    query3 = query.reshape(seq_len, heads, head)
    keys3 = keys.reshape(seq_len, heads, head)
    values3 = values.reshape(seq_len, heads, head)
    rows = 512 if seq_len % 512 == 0 else seq_len
    starts = jnp.arange(seq_len // rows, dtype=jnp.int32) * rows
    checked = jax.checkpoint(attend)
    blocks = lax.map(lambda start: checked(query3, start, keys3, values3, docs, slopes), starts)
    mixed = low(low_back(blocks.reshape(seq_len, width)))
    branch = low_back(jnp.einsum('ti,oi->to', mixed, out_weight, precision=HIGH) + out_bias)
    resid = rows_in + branch
    h_two = low(layer_norm(resid, ln2_gain, ln2_shift))
    up = low_back(jnp.einsum('ti,fi->tf', h_two, up_weight, precision=HIGH) + up_bias)
    act = low(jax.nn.gelu(up, approximate=True))
    return resid + jnp.einsum('tf,fo->to', act, down_weight, precision=HIGH) + down_bias

def reference(tokens, doc_ids, alibi_slopes, ln1_gain, ln1_shift, qkv_weight, qkv_bias, out_weight, out_bias, ln2_gain, ln2_shift, up_weight, up_bias, down_weight, down_bias, cotangent):
    params = (ln1_gain.astype(jnp.float32), ln1_shift.astype(jnp.float32), qkv_weight.astype(jnp.float32), qkv_bias.astype(jnp.float32), out_weight.astype(jnp.float32), out_bias.astype(jnp.float32), ln2_gain.astype(jnp.float32), ln2_shift.astype(jnp.float32), up_weight.astype(jnp.float32), up_bias.astype(jnp.float32), down_weight.astype(jnp.float32), down_bias.astype(jnp.float32))
    slopes = alibi_slopes.astype(jnp.float32)
    inputs = to_positions(tokens.astype(jnp.float32))
    grads_in = to_positions(cotangent.astype(jnp.float32))
    documents = to_positions(doc_ids)

    def one_sequence(sums, item):
        rows_in, rows_grad, docs = item
        result, pull = jax.vjp(lambda values_in, weights: forward(values_in, weights, slopes, docs), rows_in, params)
        input_grad, weight_grads = pull(rows_grad)
        sums = jax.tree.map(lambda left, right: left + right, sums, weight_grads)
        return (sums, (result, input_grad))
    zeros = jax.tree.map(jnp.zeros_like, params)
    sums, (results, input_grads) = lax.scan(one_sequence, zeros, (inputs, grads_in, documents))
    return (to_storage(results).astype(jnp.bfloat16), to_storage(input_grads).astype(jnp.bfloat16), sums[0], sums[1], sums[2], sums[3], sums[4], sums[5], sums[6], sums[7], sums[8], sums[9], sums[10], sums[11])
```

```python
import functools

import jax
import jax.numpy as jnp
import numpy as np
from jax import lax
from jax.experimental import pallas as pl
from jax.experimental.pallas import tpu as pltpu
from jax.sharding import PartitionSpec as P

EPS = 1e-05
MASKED = -1e30


def layer_norm(v, gain, shift):
    mean = jnp.mean(v, axis=-1, keepdims=True)
    centered = v - mean
    spread = jnp.mean(centered * centered, axis=-1, keepdims=True)
    return centered * lax.rsqrt(spread + EPS) * gain + shift


def gelu_tanh(v):
    return jax.nn.gelu(v, approximate=True)


def project_rows(values_in, weight):
    return lax.dot_general(
        values_in, weight, (((1,), (1,)), ((), ())), preferred_element_type=jnp.float32
    )


def cross_rows(left, right):
    return lax.dot_general(
        left, right, (((0,), (0,)), ((), ())), preferred_element_type=jnp.float32
    )


def token_positions(index, half_block, seq_len):
    owner = index // (2 * half_block)
    inside = index % (2 * half_block)
    return jnp.where(
        inside < half_block,
        owner * half_block + inside,
        seq_len - 1 - (owner * half_block + inside - half_block),
    )


def score_block(query3, keys3, query_pos, query_doc, key_pos, key_doc, slopes, scale):
    raw = jnp.einsum("qhe,khe->hqk", query3, keys3, preferred_element_type=jnp.float32) * scale
    distance = (query_pos[:, None] - key_pos[None, :]).astype(jnp.float32)
    scores = raw - slopes[:, None, None] * distance[None]
    allowed = ((key_pos[None, :] <= query_pos[:, None]) & (key_doc[None, :] == query_doc[:, None]))[
        None
    ]
    return (jnp.where(allowed, scores, MASKED), allowed)


def block_loop(total, size, visit, state):

    def turn_body(turn, inner):
        return visit(inner, turn * size, size)

    return lax.fori_loop(0, total // size, turn_body, state)


def gathered_device(
    tokens,
    doc_ids,
    alibi_slopes,
    ln1_gain,
    ln1_shift,
    qkv_weight,
    qkv_bias,
    out_weight,
    out_bias,
    ln2_gain,
    ln2_shift,
    up_weight,
    up_bias,
    down_weight,
    down_bias,
    cotangent,
):
    half_block = tokens.shape[2]
    width = tokens.shape[3]
    count = 2 * half_block
    heads = alibi_slopes.shape[0]
    head = width // heads
    scale = head ** (-0.5)
    seq_len = count * lax.axis_size("ctx")
    rows_in = tokens.reshape(count, width).astype(jnp.float32)
    doc_rows = doc_ids.reshape(count)
    grad_low = cotangent.reshape(count, width)
    grad_full = grad_low.astype(jnp.float32)
    own_pos = token_positions(
        lax.axis_index("ctx") * count + jnp.arange(count, dtype=jnp.int32), half_block, seq_len
    )
    gain_one, shift_one, w_qkv, b_qkv, w_out, b_out, gain_two, shift_two, b_down = (
        lax.all_gather(ln1_gain, "fsdp", axis=0, tiled=True),
        lax.all_gather(ln1_shift, "fsdp", axis=0, tiled=True),
        lax.all_gather(qkv_weight, "fsdp", axis=0, tiled=True),
        lax.all_gather(qkv_bias, "fsdp", axis=0, tiled=True),
        lax.all_gather(out_weight, "fsdp", axis=0, tiled=True),
        lax.all_gather(out_bias, "fsdp", axis=0, tiled=True),
        lax.all_gather(ln2_gain, "fsdp", axis=0, tiled=True),
        lax.all_gather(ln2_shift, "fsdp", axis=0, tiled=True),
        lax.all_gather(down_bias, "fsdp", axis=0, tiled=True),
    )
    norm_one, norm_one_pull = jax.vjp(
        layer_norm, rows_in, gain_one.astype(jnp.float32), shift_one.astype(jnp.float32)
    )
    h_one = norm_one.astype(jnp.bfloat16)
    joined = project_rows(h_one, w_qkv)
    bias_full = b_qkv.astype(jnp.float32)
    query = (joined[:, :width] + bias_full[:width]).astype(jnp.bfloat16)
    keys = joined[:, width : 2 * width].astype(jnp.bfloat16)
    values = (joined[:, 2 * width :] + bias_full[width:]).astype(jnp.bfloat16)
    query3 = query.reshape(count, heads, head)
    keys3 = keys.reshape(count, heads, head)
    values3 = values.reshape(count, heads, head)
    doc_all = lax.all_gather(doc_rows, "ctx", axis=0, tiled=True)
    start_state = (
        jnp.full((heads, count), MASKED, jnp.float32),
        jnp.zeros((heads, count), jnp.float32),
        jnp.zeros((count, heads, head), jnp.float32),
    )
    key_piece = lax.all_gather(keys, "ctx", axis=0, tiled=True)
    value_piece = lax.all_gather(values, "ctx", axis=0, tiled=True)

    def visit(state, offset, size):
        top, total, accum = state
        key_part = lax.dynamic_slice_in_dim(key_piece, offset, size).reshape(size, heads, head)
        value_part = lax.dynamic_slice_in_dim(value_piece, offset, size).reshape(size, heads, head)
        key_pos = token_positions(offset + jnp.arange(size, dtype=jnp.int32), half_block, seq_len)
        key_doc = lax.dynamic_slice_in_dim(doc_all, offset, size)
        scores, allowed = score_block(
            query3, key_part, own_pos, doc_rows, key_pos, key_doc, alibi_slopes, scale
        )
        new_top = jnp.maximum(top, jnp.max(scores, axis=2))
        weights = jnp.where(allowed, jnp.exp(scores - new_top[:, :, None]), 0.0)
        factor = jnp.exp(top - new_top)
        total = total * factor + jnp.sum(weights, axis=2)
        accum = accum * jnp.transpose(factor)[:, :, None] + jnp.einsum(
            "hqk,khe->qhe",
            weights.astype(jnp.bfloat16),
            value_part,
            preferred_element_type=jnp.float32,
        )
        return (new_top, total, accum)

    top, total, accum = block_loop(key_piece.shape[0], 512, visit, start_state)
    log_total = top + jnp.log(total)
    attended = accum / jnp.transpose(total)[:, :, None]
    mixed = attended.reshape(count, width).astype(jnp.bfloat16)
    resid = rows_in + project_rows(mixed, w_out) + b_out.astype(jnp.float32)
    norm_two, norm_two_pull = jax.vjp(
        layer_norm, resid, gain_two.astype(jnp.float32), shift_two.astype(jnp.float32)
    )
    h_two = norm_two.astype(jnp.bfloat16)
    w_up, b_up, w_down = (
        lax.all_gather(up_weight, "fsdp", axis=0, tiled=True),
        lax.all_gather(up_bias, "fsdp", axis=0, tiled=True),
        lax.all_gather(down_weight, "fsdp", axis=0, tiled=True),
    )
    up = project_rows(h_two, w_up) + b_up.astype(jnp.float32)
    act, gelu_pull = jax.vjp(gelu_tanh, up)
    act_low = act.astype(jnp.bfloat16)
    branch = jnp.dot(act_low, w_down, preferred_element_type=jnp.float32)
    layer_out = resid + branch + b_down.astype(jnp.float32)
    dup = gelu_pull(project_rows(grad_low, w_down))[0].astype(jnp.bfloat16)
    stacked = lax.psum_scatter(
        jnp.concatenate([cross_rows(dup, h_two), cross_rows(act_low, grad_low)], axis=1).astype(
            jnp.bfloat16
        ),
        "fsdp",
        scatter_dimension=0,
        tiled=True,
    ).astype(jnp.float32)
    up_rows_grad = stacked[:, :width]
    down_rows_grad = stacked[:, width:]
    up_bias_term = jnp.sum(dup, axis=0, dtype=jnp.float32)
    dnorm_two = jnp.dot(dup, w_up, preferred_element_type=jnp.float32)
    dresid_norm, gain_two_grad, shift_two_grad = norm_two_pull(dnorm_two)
    dresid = grad_full + dresid_norm
    dbranch = dresid.astype(jnp.bfloat16)
    out_bias_grad = jnp.sum(dbranch, axis=0, dtype=jnp.float32)
    out_weight_grad = cross_rows(dbranch, mixed)
    dmixed = jnp.dot(dbranch, w_out, preferred_element_type=jnp.float32).astype(jnp.bfloat16)
    dmixed3 = dmixed.reshape(count, heads, head)
    delta = jnp.transpose(jnp.sum(dmixed3.astype(jnp.float32) * attended, axis=2))
    query_key_piece = lax.all_gather(keys, "ctx", axis=0, tiled=True)
    query_value_piece = lax.all_gather(values, "ctx", axis=0, tiled=True)

    def visit(accum_grad, offset, size):
        key_part = lax.dynamic_slice_in_dim(query_key_piece, offset, size).reshape(
            size, heads, head
        )
        value_part = lax.dynamic_slice_in_dim(query_value_piece, offset, size).reshape(
            size, heads, head
        )
        key_pos = token_positions(offset + jnp.arange(size, dtype=jnp.int32), half_block, seq_len)
        key_doc = lax.dynamic_slice_in_dim(doc_all, offset, size)
        scores, allowed = score_block(
            query3, key_part, own_pos, doc_rows, key_pos, key_doc, alibi_slopes, scale
        )
        probs = jnp.where(allowed, jnp.exp(scores - log_total[:, :, None]), 0.0)
        dprobs = jnp.einsum("qhe,khe->hqk", dmixed3, value_part, preferred_element_type=jnp.float32)
        dscores = (probs * (dprobs - delta[:, :, None])).astype(jnp.bfloat16)
        return accum_grad + jnp.einsum(
            "hqk,khe->qhe", dscores, key_part, preferred_element_type=jnp.float32
        )

    query_sum = block_loop(
        query_key_piece.shape[0], 512, visit, jnp.zeros((count, heads, head), jnp.float32)
    )
    dquery = (query_sum * scale).reshape(count, width).astype(jnp.bfloat16)
    total_all, delta_all = (
        lax.all_gather(
            jnp.transpose(log_total).astype(jnp.bfloat16), "ctx", axis=0, tiled=True
        ).astype(jnp.float32),
        lax.all_gather(jnp.transpose(delta).astype(jnp.bfloat16), "ctx", axis=0, tiled=True).astype(
            jnp.float32
        ),
    )
    empty = jnp.zeros((count, heads, head), jnp.float32)
    query_piece = lax.all_gather(query, "ctx", axis=0, tiled=True)
    grad_piece = lax.all_gather(dmixed, "ctx", axis=0, tiled=True)

    def visit(state, offset, size):
        dkeys, dvalues = state
        query_part = lax.dynamic_slice_in_dim(query_piece, offset, size).reshape(size, heads, head)
        grad_part = lax.dynamic_slice_in_dim(grad_piece, offset, size).reshape(size, heads, head)
        query_pos = token_positions(offset + jnp.arange(size, dtype=jnp.int32), half_block, seq_len)
        query_doc = lax.dynamic_slice_in_dim(doc_all, offset, size)
        total_part = jnp.transpose(lax.dynamic_slice_in_dim(total_all, offset, size))
        delta_part = jnp.transpose(lax.dynamic_slice_in_dim(delta_all, offset, size))
        scores, allowed = score_block(
            query_part, keys3, query_pos, query_doc, own_pos, doc_rows, alibi_slopes, scale
        )
        probs = jnp.where(allowed, jnp.exp(scores - total_part[:, :, None]), 0.0)
        dvalues = dvalues + jnp.einsum(
            "hqk,qhe->khe",
            probs.astype(jnp.bfloat16),
            grad_part,
            preferred_element_type=jnp.float32,
        )
        dprobs = jnp.einsum("qhe,khe->hqk", grad_part, values3, preferred_element_type=jnp.float32)
        dscores = (probs * (dprobs - delta_part[:, :, None])).astype(jnp.bfloat16)
        dkeys = dkeys + jnp.einsum(
            "hqk,qhe->khe", dscores, query_part, preferred_element_type=jnp.float32
        )
        return (dkeys, dvalues)

    dkeys, dvalues = block_loop(query_piece.shape[0], 512, visit, (empty, empty))
    dkeys_low = (dkeys * scale).reshape(count, width).astype(jnp.bfloat16)
    dvalues_low = dvalues.reshape(count, width).astype(jnp.bfloat16)
    dfused = jnp.concatenate([dquery, dkeys_low, dvalues_low], axis=1)
    qkv_weight_grad = cross_rows(dfused, h_one)
    qkv_bias_grad = jnp.concatenate(
        [
            jnp.sum(dquery, axis=0, dtype=jnp.float32),
            jnp.sum(dvalues_low, axis=0, dtype=jnp.float32),
        ]
    )
    dnorm_one = jnp.dot(dfused, w_qkv, preferred_element_type=jnp.float32)
    dinput_norm, gain_one_grad, shift_one_grad = norm_one_pull(dnorm_one)
    input_grad = (dresid + dinput_norm).astype(jnp.bfloat16).reshape(tokens.shape)
    down_bias_grad = jnp.sum(grad_full, axis=0)
    shares = (
        lax.psum_scatter(
            qkv_weight_grad.astype(jnp.bfloat16), "fsdp", scatter_dimension=0, tiled=True
        ).astype(jnp.float32),
        lax.psum_scatter(
            out_weight_grad.astype(jnp.bfloat16), "fsdp", scatter_dimension=0, tiled=True
        ).astype(jnp.float32),
        lax.psum_scatter(
            qkv_bias_grad.astype(jnp.bfloat16), "fsdp", scatter_dimension=0, tiled=True
        ).astype(jnp.float32),
        lax.psum_scatter(
            out_bias_grad.astype(jnp.bfloat16), "fsdp", scatter_dimension=0, tiled=True
        ).astype(jnp.float32),
        lax.psum_scatter(
            gain_one_grad.astype(jnp.bfloat16), "fsdp", scatter_dimension=0, tiled=True
        ).astype(jnp.float32),
        lax.psum_scatter(
            shift_one_grad.astype(jnp.bfloat16), "fsdp", scatter_dimension=0, tiled=True
        ).astype(jnp.float32),
        lax.psum_scatter(
            gain_two_grad.astype(jnp.bfloat16), "fsdp", scatter_dimension=0, tiled=True
        ).astype(jnp.float32),
        lax.psum_scatter(
            shift_two_grad.astype(jnp.bfloat16), "fsdp", scatter_dimension=0, tiled=True
        ).astype(jnp.float32),
        lax.psum_scatter(
            up_bias_term.astype(jnp.bfloat16), "fsdp", scatter_dimension=0, tiled=True
        ).astype(jnp.float32),
        lax.psum_scatter(
            down_bias_grad.astype(jnp.bfloat16), "fsdp", scatter_dimension=0, tiled=True
        ).astype(jnp.float32),
    )
    totals = (
        lax.psum(shares[0].astype(jnp.bfloat16), "ctx").astype(jnp.float32),
        lax.psum(shares[1].astype(jnp.bfloat16), "ctx").astype(jnp.float32),
        lax.psum(up_rows_grad.astype(jnp.bfloat16), "ctx").astype(jnp.float32),
        lax.psum(down_rows_grad.astype(jnp.bfloat16), "ctx").astype(jnp.float32),
        lax.psum(shares[2].astype(jnp.bfloat16), "ctx").astype(jnp.float32),
        lax.psum(shares[3].astype(jnp.bfloat16), "ctx").astype(jnp.float32),
        lax.psum(shares[4].astype(jnp.bfloat16), "ctx").astype(jnp.float32),
        lax.psum(shares[5].astype(jnp.bfloat16), "ctx").astype(jnp.float32),
        lax.psum(shares[6].astype(jnp.bfloat16), "ctx").astype(jnp.float32),
        lax.psum(shares[7].astype(jnp.bfloat16), "ctx").astype(jnp.float32),
        lax.psum(shares[8].astype(jnp.bfloat16), "ctx").astype(jnp.float32),
        lax.psum(shares[9].astype(jnp.bfloat16), "ctx").astype(jnp.float32),
    )
    return (
        layer_out.astype(jnp.bfloat16).reshape(tokens.shape),
        input_grad,
        totals[6],
        totals[7],
        totals[0],
        totals[4],
        totals[1],
        totals[5],
        totals[8],
        totals[9],
        totals[2],
        totals[10],
        totals[3],
        totals[11],
    )

F32 = jnp.float32
BF16 = jnp.bfloat16
LOG2E = 1.4426950408889634
LN2 = 0.6931471805599453
TILE = 256
DOC_LANES = 48
GELU_A = 0.7978845608028654
GELU_B = 0.044715


def dot_nt(a, b):
    return lax.dot_general(a, b, (((1,), (1,)), ((), ())), preferred_element_type=F32)


def dot_nn(a, b):
    return lax.dot_general(a, b, (((1,), (0,)), ((), ())), preferred_element_type=F32)


def dot_tn(a, b):
    return lax.dot_general(a, b, (((0,), (0,)), ((), ())), preferred_element_type=F32)


def kernel_call(body, outs, ins, scratch=(), scalars=1, flops=0, mib=40):
    size = sum(int(np.prod(x.shape)) * x.dtype.itemsize for x in list(ins) + list(outs))
    specs = [
        pl.BlockSpec(memory_space=pltpu.SMEM if at < scalars else pltpu.VMEM)
        for at in range(len(ins))
    ]
    return pl.pallas_call(
        body,
        out_shape=list(outs),
        in_specs=specs,
        out_specs=[pl.BlockSpec(memory_space=pltpu.VMEM)] * len(outs),
        scratch_shapes=list(scratch),
        compiler_params=pltpu.CompilerParams(vmem_limit_bytes=mib * 1024 * 1024),
        cost_estimate=pl.CostEstimate(flops=int(flops), bytes_accessed=size, transcendentals=0),
    )(*ins)


def shaped(shape, dtype):
    return jax.ShapeDtypeStruct(shape, dtype)


def lanes_of(shape):
    return lax.broadcasted_iota(jnp.int32, shape, len(shape) - 1)


def three_pieces(v):
    high = v.astype(BF16).astype(F32)
    mid = (v - high).astype(BF16).astype(F32)
    return high, mid, v - high - mid


def normed(v):
    mean = jnp.mean(v, axis=-1, keepdims=True)
    centered = v - mean
    spread = jnp.mean(centered * centered, axis=-1, keepdims=True)
    root = lax.rsqrt(spread + EPS)
    return centered * root, root


def norm_back(dout, unit, root, gain):
    dn = dout * gain
    first = jnp.mean(dn, axis=-1, keepdims=True)
    second = jnp.mean(dn * unit, axis=-1, keepdims=True)
    return root * (dn - first - unit * second)


def block_rows(index, half_block):
    return pl.ds(pl.multiple_of(index * half_block, half_block), half_block)


def project_kernel(ids, slopes, *refs):
    chunks, packs = refs[:8], refs[8:12]
    q_out, k_out, v_out, w_out, par_out, doc_out, small = refs[12:]
    c, f = ids[0], ids[1]
    for k in range(4):
        plane = lax.rem(f + (4 - k), 4)
        small[plane] = packs[k][128:144, :].astype(F32)
        for kind in range(3):

            @pl.when(ids[2 + kind] == k)
            def _():
                w_out[kind * 128 : (kind + 1) * 128, :] = packs[k][0:128, :]

    rows = [small[p] for p in range(4)]

    def whole(row, start, stop, planes=(0, 1, 2, 3)):
        return jnp.concatenate([rows[p][row : row + 1, start:stop] for p in planes], axis=1)

    par_out[0:1, :] = whole(0, 0, 256)
    par_out[1:2, :] = whole(0, 256, 512)
    par_out[2:3, :] = whole(0, 512, 768)
    par_out[3:4, :] = whole(0, 768, 1024)
    par_out[4:5, :] = whole(1, 0, 256)
    par_out[5:6, :] = whole(1, 256, 512)
    par_out[6:7, :] = whole(1, 512, 1024, (0, 1))
    par_out[7:8, :] = whole(1, 512, 1024, (2, 3))
    mine = pl.ds(pl.multiple_of(c * 128, 128), 128)
    bias_q = par_out[6:7, mine]
    bias_v = par_out[7:8, mine]
    gain, shift = par_out[0:1, :], par_out[1:2, :]
    weight = w_out[...]
    lane = lanes_of((256, 128))
    row = lax.broadcasted_iota(jnp.int32, (256, 128), 0)
    eye = (
        lax.broadcasted_iota(jnp.int32, (128, 128), 0) == lanes_of((128, 128))
    ).astype(BF16)
    sub = lax.broadcasted_iota(jnp.int32, (128, 256), 0).astype(F32) - 67.0
    is_doc = (lane >= 67) & (lane < 67 + DOC_LANES)
    low = lane < 64
    for d in range(8):
        cc = c ^ d
        h = (normed(chunks[d][0:256, :].astype(F32))[0] * gain + shift).astype(BF16)
        joined = dot_nt(h, weight)
        query = (joined[:, 0:128] + bias_q) * (LOG2E * 0.125)
        keys = joined[:, 128:256]
        values = joined[:, 256:384] + bias_v
        doc_row = chunks[d][256:272, 0:256].astype(F32)[0:1, :]
        doc_out[pl.ds(cc, 1), :] = doc_row[:, 0:128]
        doc_out[pl.ds(8 + cc, 1), :] = doc_row[:, 128:256]
        one_hot = dot_tn((sub == doc_row).astype(BF16), eye)
        pos = jnp.where(row < 128, cc * 128 + row, 2175 - cc * 128 - row).astype(F32)
        q_aug = jnp.where(lane < 67, 1.0, jnp.where(is_doc, one_hot, 0.0))
        k_tail = jnp.where(is_doc, (1.0 - one_hot) * MASKED, jnp.where(lane < 118, 1.0, 0.0))
        for hh in range(2):
            if hh == 1:
                query, keys, values = (pltpu.roll(t, 64, 1) for t in (query, keys, values))
            high, mid, rest = three_pieces(pos * (slopes[2 * c + hh] * LOG2E))
            k_aug = jnp.where(
                lane == 64, high, jnp.where(lane == 65, mid, jnp.where(lane == 66, rest, k_tail))
            )
            parts = (
                (q_out, jnp.where(low, query, q_aug).astype(BF16)),
                (k_out, jnp.where(low, keys, k_aug).astype(BF16)),
                (v_out, jnp.where(low, values, 1.0).astype(BF16)),
            )
            for ref, value in parts:
                ref[hh, block_rows(cc, 128), :] = value[0:128]
                ref[hh, block_rows(8 + cc, 128), :] = value[128:256]


def tile_start(i):
    return i * TILE if i < 4 else 1024 + (7 - i) * TILE


def tile_rows(i):
    start = jnp.where(i < 4, i * TILE, 1024 + (7 - i) * TILE)
    return pl.ds(pl.multiple_of(start, TILE), TILE)


def tile_docs(docs, i):
    at = tile_start(i) // 128
    return docs[at : at + 2, :]


def count_tiles(flags):
    total = jnp.sum(jnp.where(flags, 1.0, 0.0)).astype(jnp.int32)
    return lax.shift_right_logical(total, 8)


def attend_kernel(docs_ref, q_ref, k_ref, v_ref, q_out, mixed_out, full_out):
    docs = docs_ref[...]
    lane = lanes_of((TILE, 128))
    low = lane < 64
    down, right = lax.broadcasted_iota(jnp.int32, (TILE, TILE), 0), lanes_of((TILE, TILE))
    for i in range(8):
        rows = slice(tile_start(i), tile_start(i) + TILE)
        first = count_tiles(docs < jnp.min(tile_docs(docs, i)))
        allowed = (down >= right) if i < 4 else (down <= right)
        queries = [q_ref[hh, rows, :] for hh in range(2)]
        state = []
        for hh in range(2):
            scores = jnp.where(allowed, dot_nt(queries[hh], k_ref[hh, rows, :]), MASKED)
            top = jnp.max(scores, axis=1, keepdims=True)
            weights = jnp.exp2(scores - top).astype(BF16)
            state += [top, dot_nn(weights, v_ref[hh, rows, :])]

        def step(j, carry):
            out = []
            at = tile_rows(j)
            for hh in range(2):
                top, accum = carry[2 * hh], carry[2 * hh + 1]
                scores = dot_nt(queries[hh], k_ref[hh, at, :])
                new_top = jnp.maximum(top, jnp.max(scores, axis=1, keepdims=True))
                weights = jnp.exp2(scores - new_top).astype(BF16)
                accum = accum * jnp.exp2(top - new_top) + dot_nn(weights, v_ref[hh, at, :])
                out += [new_top, accum]
            return tuple(out)

        state = lax.fori_loop(first, i, step, tuple(state))
        outs = []
        for hh in range(2):
            top, accum = state[2 * hh], state[2 * hh + 1]
            total = accum[:, 64:65]
            outs.append(accum / total)
            high, mid, rest = three_pieces(-(top + jnp.log2(total)))
            tail = jnp.where(
                lane == 115,
                high,
                jnp.where(lane == 116, mid, jnp.where(lane == 117, rest, queries[hh].astype(F32))),
            )
            q_out[hh, rows, :] = tail.astype(BF16)
        both = jnp.where(low, outs[0], pltpu.roll(outs[1], 64, 1))
        full_out[rows, :] = both
        half, at = divmod(tile_start(i) // 128, 8)
        for piece in range(2):
            mixed_out[at + piece, half * 128 : (half + 1) * 128, :] = both[
                piece * 128 : (piece + 1) * 128
            ].astype(BF16)


def attend_back_kernel(docs_ref, q_ref, k_ref, v_ref, full_ref, grad_ref, out, grads, dq, dk, dv):
    docs = docs_ref[...]
    lane = lanes_of((256, 128))
    low = lane < 64
    for at in range(8):
        piece = grad_ref[at].astype(F32)
        other = jnp.concatenate(
            [
                full_ref[at * 128 : (at + 1) * 128, :],
                full_ref[1024 + at * 128 : 1024 + (at + 1) * 128, :],
            ],
            axis=0,
        )
        product = piece * other
        for hh in range(2):
            delta = jnp.sum(jnp.where(low == (hh == 0), product, 0.0), axis=1, keepdims=True)
            high, mid, rest = three_pieces(-delta)
            tail = jnp.where(
                lane == 64, high, jnp.where(lane == 65, mid, jnp.where(lane == 66, rest, 0.0))
            )
            moved = piece if hh == 0 else pltpu.roll(piece, 64, 1)
            value = jnp.where(low, moved, tail).astype(BF16)
            grads[hh, at * 128 : (at + 1) * 128, :] = value[0:128]
            grads[hh, 1024 + at * 128 : 1024 + (at + 1) * 128, :] = value[128:256]
    dq[...] = jnp.zeros_like(dq)
    down, right = lax.broadcasted_iota(jnp.int32, (TILE, TILE), 0), lanes_of((TILE, TILE))
    for j in range(8):
        rows = slice(tile_start(j), tile_start(j) + TILE)
        last = count_tiles(docs <= jnp.max(tile_docs(docs, j)))
        stop = jnp.where(
            jnp.sum(jnp.where(docs <= jnp.max(tile_docs(docs, j)), 1.0, 0.0)).astype(jnp.int32)
            == last * TILE,
            last,
            last + 1,
        )
        allowed = (down <= right) if j < 4 else (down >= right)
        keys = [k_ref[hh, rows, :] for hh in range(2)]
        values = [v_ref[hh, rows, :] for hh in range(2)]

        def visit(hh, at, masked):
            query, grad = q_ref[hh, at, :], grads[hh, at, :]
            probs = jnp.exp2(dot_nt(keys[hh], query))
            if masked:
                probs = jnp.where(allowed, probs, 0.0)
            dscores = (probs * dot_nt(values[hh], grad)).astype(BF16)
            dq[hh, at, :] += dot_tn(dscores, keys[hh])
            return dot_nn(dscores, query), dot_nn(probs.astype(BF16), grad)

        state = []
        for hh in range(2):
            state += list(visit(hh, rows, True))

        def step(i, carry):
            at = tile_rows(i)
            got = []
            for hh in range(2):
                got += list(visit(hh, at, False))
            return tuple(a + b for a, b in zip(carry, got))

        state = lax.fori_loop(j + 1, stop, step, tuple(state))
        dk[rows, :] = jnp.where(low, state[0], pltpu.roll(state[2], 64, 1)) * LN2
        dv[rows, :] = jnp.where(low, state[1], pltpu.roll(state[3], 64, 1))
    for at in range(8):
        rows = slice(at * 256, (at + 1) * 256)
        both = jnp.where(low, dq[0, rows, :], pltpu.roll(dq[1, rows, :], 64, 1)) * 0.125
        out[rows, 0:128] = both.astype(BF16)
        out[rows, 128:256] = dk[rows, :].astype(BF16)
        out[rows, 256:384] = dv[rows, :].astype(BF16)


def branch_kernel(ids, chunk, mixed_in, par, *refs):
    pieces = refs[:8]
    w_out, mixed_out, resid_out, h_out = refs[8:]
    c, f = ids[0], ids[1]
    for d in range(8):
        for k in range(4):
            plane = lax.rem(f + (4 - k), 4)
            at = pl.multiple_of(plane * 256 + (c ^ d) * 32, 32)
            w_out[pl.ds(at, 32), :] = pieces[d][k * 32 : (k + 1) * 32, :]
    for at in range(8):
        mixed_out[:, at * 128 : (at + 1) * 128] = mixed_in[at]
    resid = chunk[0:256, :].astype(F32) + dot_nt(mixed_out[...], w_out[...]) + par[2:3, :]
    resid_out[...] = resid
    h_out[...] = (normed(resid)[0] * par[3:4, :] + par[4:5, :]).astype(BF16)


def feed_kernel(h_ref, cot_ref, up_ref, bias_ref, down_ref, branch, dh, act_out, dup_out, acc, dacc):
    h, cot = h_ref[...], cot_ref[...]
    for t in range(4):
        at = slice(t * 256, (t + 1) * 256)
        up_w, down_w = up_ref[at, :], down_ref[at, :]
        u = dot_nt(h, up_w) + bias_ref[0:1, at]
        grad = dot_nt(cot, down_w)
        square = u * u
        th = jnp.tanh(GELU_A * u * (1.0 + GELU_B * square))
        half = 0.5 * (1.0 + th)
        act = (u * half).astype(BF16)
        slope = half + 0.5 * u * (1.0 - th * th) * (GELU_A * (1.0 + 3.0 * GELU_B * square))
        dup = (grad * slope).astype(BF16)
        act_out[:, at] = act
        dup_out[:, at] = dup
        if t == 0:
            acc[...] = dot_nn(act, down_w)
            dacc[...] = dot_nn(dup, up_w)
        else:
            acc[...] += dot_nn(act, down_w)
            dacc[...] += dot_nn(dup, up_w)
    branch[...] = acc[...].astype(BF16)
    dh[...] = dacc[...].astype(BF16)


def middle_kernel(d0, d1, d2, d3, resid_ref, cot_ref, par, w_ref, dresid_out, dbranch_out, dmixed_out, sums):
    dh = sum(r[...].astype(F32) for r in (d0, d1, d2, d3))
    unit, root = normed(resid_ref[...])
    cot = cot_ref[...].astype(F32)
    dresid = cot + norm_back(dh, unit, root, par[3:4, :])
    dresid_out[...] = dresid
    dbranch = dresid.astype(BF16)
    dbranch_out[...] = dbranch
    dmixed = dot_nn(dbranch, w_ref[...]).astype(BF16)
    for at in range(8):
        dmixed_out[at] = dmixed[:, at * 128 : (at + 1) * 128]
    sums[...] = jnp.zeros_like(sums)
    sums[0:1, :] = jnp.sum(dbranch.astype(F32), axis=0, keepdims=True)
    sums[1:2, :] = jnp.sum(dh * unit, axis=0, keepdims=True)
    sums[2:3, :] = jnp.sum(dh, axis=0, keepdims=True)
    sums[3:4, :] = jnp.sum(cot, axis=0, keepdims=True)


def weights_kernel(ids, *refs):
    dups, hs, acts, cots = refs[0:4], refs[4:8], refs[8:12], refs[12:16]
    dbranch, mixed = refs[16:18]
    keep, send, bias = refs[18:21]
    up_all, down_all, out_all = refs[21:]
    c = ids[0]
    bias[...] = jnp.zeros_like(bias)
    for t in range(4):
        at = slice(t * 256, (t + 1) * 256)
        up_sum = down_sum = bias_sum = 0.0
        for k in range(4):
            dup = dups[k][:, at]
            up_sum += dot_tn(dup, hs[k][...])
            down_sum += dot_tn(acts[k][:, at], cots[k][...])
            bias_sum += jnp.sum(dup.astype(F32), axis=0, keepdims=True)
        up_all[at, :] = up_sum.astype(BF16)
        down_all[at, :] = down_sum.astype(BF16)
        out_all[at, :] = dot_tn(dbranch[:, at], mixed[...]).astype(BF16)
        bias[0:1, at] = bias_sum
    for d in range(8):
        cc = c ^ d
        target = send if d % 2 else keep
        e = d // 2
        target[e, 0:128, :] = up_all[block_rows(cc, 128), :]
        target[e, 128:256, :] = down_all[block_rows(cc, 128), :]
        for plane in range(4):
            at = pl.multiple_of(plane * 256 + cc * 32, 32)
            target[e, 256 + plane * 32 : 256 + (plane + 1) * 32, :] = out_all[pl.ds(at, 32), :]


def unproject_kernel(ids, *refs):
    chunks = refs[:8]
    dqkv, w_ref, par, sums, keep, send, slots, wsum, small = refs[8:]
    c, f = ids[0], ids[1]
    gain, shift = par[0:1, :], par[1:2, :]
    weight = w_ref[...]
    gain_grad = shift_grad = bias_grad = 0.0
    for d in range(8):
        cc = c ^ d
        grads = jnp.concatenate(
            [dqkv[block_rows(cc, 128), :], dqkv[block_rows(8 + cc, 128), :]], axis=0
        )
        unit = normed(chunks[d][0:256, :].astype(F32))[0]
        h = (unit * gain + shift).astype(BF16)
        share = dot_nn(grads, weight)
        (send if d % 2 else keep)[d // 2] = share.astype(BF16)
        gain_grad += jnp.sum(share * unit, axis=0, keepdims=True)
        shift_grad += jnp.sum(share, axis=0, keepdims=True)
        bias_grad += jnp.sum(grads.astype(F32), axis=0, keepdims=True)
        if d == 0:
            wsum[...] = dot_tn(grads, h)
        else:
            wsum[...] += dot_tn(grads, h)
    small[...] = jnp.zeros_like(small)
    for p in range(4):
        at = slice(p * 256, (p + 1) * 256)
        small[p, 0:1, 0:256] = gain_grad[:, at]
        small[p, 0:1, 256:512] = shift_grad[:, at]
        small[p, 0:1, 512:768] = sums[0:1, at]
        small[p, 0:1, 768:1024] = sums[1:2, at]
        small[p, 1:2, 0:256] = sums[2:3, at]
        small[p, 1:2, 256:512] = sums[3:4, at]
        small[p, 1:2, 512:640] = bias_grad[:, 0:128] if p < 2 else bias_grad[:, 256:384]
    for k in range(4):
        start = pl.multiple_of(ids[6 + k] * 128, 128)
        slots[k, 0:128, :] = wsum[pl.ds(start, 128), :].astype(BF16)
        slots[k, 128:144, :] = small[lax.rem(f + k, 4)].astype(BF16)


def input_kernel(s0, s1, s2, s3, chunk, par, dresid, out):
    dh = sum(r[...].astype(F32) for r in (s0, s1, s2, s3))
    unit, root = normed(chunk[0:256, :].astype(F32))
    out[...] = (dresid[...] + norm_back(dh, unit, root, par[0:1, :])).astype(BF16)


def feed_grads_kernel(ids, *refs):
    pieces, (up_out, down_out) = refs[:8], refs[8:]
    for d in range(8):
        rows = block_rows(ids[0] ^ d, 128)
        up_out[rows, :] = pieces[d][0:128, :].astype(F32)
        down_out[rows, :] = pieces[d][128:256, :].astype(F32)


def last_grads_kernel(ids, *refs):
    pieces = refs[:8]
    qkv_out, out_out, vec_out, bias_out = refs[8:]
    c, f = ids[0], ids[1]
    total = 0.0
    for d in range(8):
        cc = c ^ d
        place = lax.rem(cc + 24 - 6 * f, 8)

        @pl.when(place < 6)
        def _():
            qkv_out[block_rows(place, 128), :] = pieces[d][0:128, :].astype(F32)

        out_out[pl.ds(pl.multiple_of(cc * 32, 32), 32), :] = pieces[d][144:176, :].astype(F32)
        rows = pieces[d][128:144, :].astype(F32)
        total += rows

        @pl.when(lax.div(cc, 4) == lax.rem(f, 2))
        def _():
            at = pl.multiple_of(lax.rem(cc, 4) * 128, 128)
            bias_out[0:1, pl.ds(at, 128)] = rows[1:2, 512:640]

    vec_out[...] = total


def per_device(
    tokens,
    doc_ids,
    alibi_slopes,
    ln1_gain,
    ln1_shift,
    qkv_weight,
    qkv_bias,
    out_weight,
    out_bias,
    ln2_gain,
    ln2_shift,
    up_weight,
    up_bias,
    down_weight,
    down_bias,
    cotangent,
):
    c, f = lax.axis_index("ctx"), lax.axis_index("fsdp")
    width = 1024

    def swap(v, d):
        return lax.ppermute(v, "ctx", [(i, i ^ d) for i in range(8)])

    def shift(v, k):
        return lax.ppermute(v, "fsdp", [(i, (i + k) % 4) for i in range(4)])

    def spread(v):
        got = {0: v}
        for d in (2, 4, 6):
            got[d] = swap(v, d)
        for d in (0, 2, 4, 6):
            got[d + 1] = swap(got[d], 1)
        return [got[d] for d in range(8)]

    def add_up(parts):
        return sum(p.astype(F32) for p in parts).astype(BF16)

    table = np.zeros((32, 16), np.int32)
    for ci in range(8):
        for fi in range(4):
            at = ci * 4 + fi
            table[at, 0:2] = ci, fi
            planes = [(8 * kind + ci) // 6 for kind in range(3)]
            table[at, 2:5] = [(fi - p) % 4 for p in planes]
            for kind in range(3):
                if planes[kind] == fi:
                    table[at, 5] = (8 * kind + ci) % 6
            for k in range(4):
                if (fi + k) % 4 in planes:
                    table[at, 6 + k] = planes.index((fi + k) % 4)
    ids = lax.dynamic_index_in_dim(jnp.asarray(table), c * 4 + f, 0, keepdims=False)

    own = tokens.reshape(256, width)
    cot = cotangent.reshape(256, width)
    doc_row = jnp.pad(doc_ids.reshape(1, 256).astype(BF16), ((0, 15), (0, width - 256)))
    chunk = jnp.concatenate([own, doc_row], axis=0)
    chunks = spread(chunk)
    small = jnp.concatenate(
        [ln1_gain, ln1_shift, out_bias, ln2_gain, ln2_shift, down_bias, qkv_bias]
    ).reshape(2, width)
    pack = jnp.concatenate(
        [
            lax.dynamic_slice_in_dim(qkv_weight, ids[5] * 128, 128),
            jnp.pad(small, ((0, 14), (0, 0))),
            lax.dynamic_slice_in_dim(out_weight, c * 32, 32),
        ],
        axis=0,
    )
    packs = [pack] + [shift(pack, k) for k in (1, 2, 3)]

    heads = shaped((2, 2048, 128), BF16)
    q_one, keys, values, w_heads, par, docs = kernel_call(
        project_kernel,
        [heads, heads, heads, shaped((384, width), BF16), shaped((8, width), F32), shaped((16, 128), F32)],
        [ids, alibi_slopes, *chunks, *packs],
        [pltpu.VMEM((4, 16, width), F32)],
        scalars=2,
        flops=2 * 2048 * 384 * 1024,
    )
    q_two, mixed_heads, full = kernel_call(
        attend_kernel,
        [heads, shaped((8, 256, 128), BF16), shaped((2048, 128), F32)],
        [docs, q_one, keys, values],
        scalars=0,
        flops=2 * 2 * 2 * 2048 * 1024 * 128,
    )
    w_pieces = spread(jnp.concatenate([p[144:176] for p in packs], axis=0))
    mixed_in = lax.all_to_all(mixed_heads, "ctx", 0, 0, tiled=True)
    w_out, mixed, resid, h_two = kernel_call(
        branch_kernel,
        [
            shaped((width, width), BF16),
            shaped((256, width), BF16),
            shaped((256, width), F32),
            shaped((256, width), BF16),
        ],
        [ids, chunk, mixed_in, par, *w_pieces],
        flops=2 * 256 * 1024 * 1024,
    )
    late_cot, _ = lax.optimization_barrier((cot, packs[3]))
    cots = [cot] + [shift(late_cot, k) for k in (1, 2, 3)]
    hs = [h_two]
    for _ in range(3):
        hs.append(shift(hs[-1], 1))
    up_row = up_bias.astype(F32).reshape(1, width)
    rows = shaped((256, width), BF16)
    branches, dhs, acts, dups = [], [], [], []
    for k in range(4):
        got = kernel_call(
            feed_kernel,
            [rows, rows, rows, rows],
            [hs[k], cots[k], up_weight, up_row, down_weight],
            [pltpu.VMEM((256, width), F32)] * 2,
            scalars=0,
            flops=8 * 256 * 1024 * 1024,
        )
        for kept, value in zip((branches, dhs, acts, dups), got):
            kept.append(value)
    dh_parts = [dhs[0]] + [shift(dhs[k], 4 - k) for k in (1, 2, 3)]
    dresid, dbranch, dmixed, sums = kernel_call(
        middle_kernel,
        [shaped((256, width), F32), rows, shaped((8, 256, 128), BF16), shaped((8, width), F32)],
        [*dh_parts, resid, cot, par, w_out],
        scalars=0,
        flops=2 * 256 * 1024 * 1024,
    )
    dmixed_heads = lax.all_to_all(dmixed, "ctx", 0, 0, tiled=True)
    late_branches = lax.optimization_barrier((tuple(branches), dmixed))[0]
    parts = [late_branches[0]] + [shift(late_branches[k], 4 - k) for k in (1, 2, 3)]
    layer_out = (resid + par[5:6] + sum(p.astype(F32) for p in parts)).astype(BF16)

    big = shaped((4, 384, width), BF16)
    keep, send, up_sum = kernel_call(
        weights_kernel,
        [big, big, shaped((8, width), F32)],
        [ids, *dups, *hs, *acts, *cots, dbranch, mixed],
        [pltpu.VMEM((width, width), BF16)] * 3,
        flops=2 * 2 * 1024**3 + 2 * 256 * 1024**2,
    )
    mine = add_up([keep, swap(send, 1)])
    owned = add_up([mine[0]] + [swap(mine[e], 2 * e) for e in (1, 2, 3)])
    feed_pieces = spread(owned[0:256])
    up_grad, down_grad = kernel_call(
        feed_grads_kernel,
        [shaped((width, width), F32)] * 2,
        [ids, *feed_pieces],
    )
    out_share = owned[256:384].reshape(4, 32, width)
    out_sum = add_up(
        [lax.dynamic_index_in_dim(out_share, f, 0, keepdims=False)]
        + [
            shift(lax.dynamic_index_in_dim(out_share, (f + k) % 4, 0, keepdims=False), k)
            for k in (1, 2, 3)
        ]
    )

    dqkv = kernel_call(
        attend_back_kernel,
        [shaped((2048, 384), BF16)],
        [docs, q_two, keys, values, full, dmixed_heads],
        [
            pltpu.VMEM((2, 2048, 128), BF16),
            pltpu.VMEM((2, 2048, 128), F32),
            pltpu.VMEM((2048, 128), F32),
            pltpu.VMEM((2048, 128), F32),
        ],
        scalars=0,
        flops=5 * 2 * 2 * 2048 * 1024 * 128,
    )[0]
    quarter = shaped((4, 256, width), BF16)
    keep, send, slots = kernel_call(
        unproject_kernel,
        [quarter, quarter, shaped((4, 144, width), BF16)],
        [ids, *chunks, dqkv, w_heads, par, sums],
        [pltpu.VMEM((384, width), F32), pltpu.VMEM((4, 16, width), F32)],
        flops=4 * 2048 * 384 * 1024,
    )
    mine = add_up([keep, swap(send, 1)])
    shares = [mine[0]] + [swap(mine[e], 2 * e) for e in (1, 2, 3)]
    input_grad = kernel_call(
        input_kernel, [rows], [*shares, chunk, par, dresid], scalars=0
    )[0]
    slot_sum = add_up([slots[0]] + [shift(slots[k], k) for k in (1, 2, 3)])
    slot_sum = jnp.concatenate(
        [slot_sum[0:130], up_sum[0:1].astype(BF16), slot_sum[131:144], out_sum], axis=0
    )
    last_pieces = spread(slot_sum)
    qkv_grad, out_grad, vectors, bias_grad = kernel_call(
        last_grads_kernel,
        [
            shaped((768, width), F32),
            shaped((256, width), F32),
            shaped((16, width), F32),
            shaped((1, 512), F32),
        ],
        [ids, *last_pieces],
    )
    return (
        layer_out.reshape(tokens.shape),
        input_grad.reshape(tokens.shape),
        vectors[0, 0:256],
        vectors[0, 256:512],
        qkv_grad,
        bias_grad.reshape(512),
        out_grad,
        vectors[0, 512:768],
        vectors[0, 768:1024],
        vectors[1, 0:256],
        up_grad,
        vectors[2],
        down_grad,
        vectors[1, 256:512],
    )


def on_small_slice(mesh, tokens, slopes):
    return (
        mesh.shape["ctx"] == 8
        and mesh.shape["fsdp"] == 4
        and tokens.shape == (4, 2, 1024, 1024)
        and slopes.shape == (16,)
    )


def solution(mesh):
    in_specs = (
        P("fsdp", None, "ctx", None),
        P("fsdp", None, "ctx"),
        P(),
        P("fsdp"),
        P("fsdp"),
        P("fsdp", None),
        P("fsdp"),
        P("fsdp", None),
        P("fsdp"),
        P("fsdp"),
        P("fsdp"),
        P("fsdp", None),
        P("fsdp"),
        P("fsdp", None),
        P("fsdp"),
        P("fsdp", None, "ctx", None),
    )
    out_specs = (
        P("fsdp", None, "ctx", None),
        P("fsdp", None, "ctx", None),
        P("fsdp"),
        P("fsdp"),
        P("fsdp", None),
        P("fsdp"),
        P("fsdp", None),
        P("fsdp"),
        P("fsdp"),
        P("fsdp"),
        P("fsdp", None),
        P("fsdp"),
        P("fsdp", None),
        P("fsdp"),
    )
    def layer(*args):
        body = per_device if on_small_slice(mesh, args[0], args[2]) else gathered_device
        return jax.shard_map(
            body, mesh=mesh, in_specs=in_specs, out_specs=out_specs, check_vma=False
        )(*args)

    return layer
```

```python
import functools

import jax
import jax.numpy as jnp
import numpy as np
from jax import lax
from jax.experimental import pallas as pl
from jax.experimental.pallas import tpu as pltpu
from jax.sharding import PartitionSpec as P

EPS = 1e-05
MASKED = -1e30


def layer_norm(v, gain, shift):
    mean = jnp.mean(v, axis=-1, keepdims=True)
    centered = v - mean
    spread = jnp.mean(centered * centered, axis=-1, keepdims=True)
    return centered * lax.rsqrt(spread + EPS) * gain + shift


def gelu_tanh(v):
    return jax.nn.gelu(v, approximate=True)


def project_rows(values_in, weight):
    return lax.dot_general(
        values_in, weight, (((1,), (1,)), ((), ())), preferred_element_type=jnp.float32
    )


def cross_rows(left, right):
    return lax.dot_general(
        left, right, (((0,), (0,)), ((), ())), preferred_element_type=jnp.float32
    )


def token_positions(index, half_block, seq_len):
    owner = index // (2 * half_block)
    inside = index % (2 * half_block)
    return jnp.where(
        inside < half_block,
        owner * half_block + inside,
        seq_len - 1 - (owner * half_block + inside - half_block),
    )


def score_block(query3, keys3, query_pos, query_doc, key_pos, key_doc, slopes, scale):
    raw = jnp.einsum("qhe,khe->hqk", query3, keys3, preferred_element_type=jnp.float32) * scale
    distance = (query_pos[:, None] - key_pos[None, :]).astype(jnp.float32)
    scores = raw - slopes[:, None, None] * distance[None]
    allowed = ((key_pos[None, :] <= query_pos[:, None]) & (key_doc[None, :] == query_doc[:, None]))[
        None
    ]
    return (jnp.where(allowed, scores, MASKED), allowed)


def block_loop(total, size, visit, state):

    def turn_body(turn, inner):
        return visit(inner, turn * size, size)

    return lax.fori_loop(0, total // size, turn_body, state)


def gathered_device(
    tokens,
    doc_ids,
    alibi_slopes,
    ln1_gain,
    ln1_shift,
    qkv_weight,
    qkv_bias,
    out_weight,
    out_bias,
    ln2_gain,
    ln2_shift,
    up_weight,
    up_bias,
    down_weight,
    down_bias,
    cotangent,
):
    half_block = tokens.shape[2]
    width = tokens.shape[3]
    count = 2 * half_block
    heads = alibi_slopes.shape[0]
    head = width // heads
    scale = head ** (-0.5)
    seq_len = count * lax.axis_size("ctx")
    rows_in = tokens.reshape(count, width).astype(jnp.float32)
    doc_rows = doc_ids.reshape(count)
    grad_low = cotangent.reshape(count, width)
    grad_full = grad_low.astype(jnp.float32)
    own_pos = token_positions(
        lax.axis_index("ctx") * count + jnp.arange(count, dtype=jnp.int32), half_block, seq_len
    )
    gain_one, shift_one, w_qkv, b_qkv, w_out, b_out, gain_two, shift_two, b_down = (
        lax.all_gather(ln1_gain, "fsdp", axis=0, tiled=True),
        lax.all_gather(ln1_shift, "fsdp", axis=0, tiled=True),
        lax.all_gather(qkv_weight, "fsdp", axis=0, tiled=True),
        lax.all_gather(qkv_bias, "fsdp", axis=0, tiled=True),
        lax.all_gather(out_weight, "fsdp", axis=0, tiled=True),
        lax.all_gather(out_bias, "fsdp", axis=0, tiled=True),
        lax.all_gather(ln2_gain, "fsdp", axis=0, tiled=True),
        lax.all_gather(ln2_shift, "fsdp", axis=0, tiled=True),
        lax.all_gather(down_bias, "fsdp", axis=0, tiled=True),
    )
    norm_one, norm_one_pull = jax.vjp(
        layer_norm, rows_in, gain_one.astype(jnp.float32), shift_one.astype(jnp.float32)
    )
    h_one = norm_one.astype(jnp.bfloat16)
    joined = project_rows(h_one, w_qkv)
    bias_full = b_qkv.astype(jnp.float32)
    query = (joined[:, :width] + bias_full[:width]).astype(jnp.bfloat16)
    keys = joined[:, width : 2 * width].astype(jnp.bfloat16)
    values = (joined[:, 2 * width :] + bias_full[width:]).astype(jnp.bfloat16)
    query3 = query.reshape(count, heads, head)
    keys3 = keys.reshape(count, heads, head)
    values3 = values.reshape(count, heads, head)
    doc_all = lax.all_gather(doc_rows, "ctx", axis=0, tiled=True)
    start_state = (
        jnp.full((heads, count), MASKED, jnp.float32),
        jnp.zeros((heads, count), jnp.float32),
        jnp.zeros((count, heads, head), jnp.float32),
    )
    key_piece = lax.all_gather(keys, "ctx", axis=0, tiled=True)
    value_piece = lax.all_gather(values, "ctx", axis=0, tiled=True)

    def visit(state, offset, size):
        top, total, accum = state
        key_part = lax.dynamic_slice_in_dim(key_piece, offset, size).reshape(size, heads, head)
        value_part = lax.dynamic_slice_in_dim(value_piece, offset, size).reshape(size, heads, head)
        key_pos = token_positions(offset + jnp.arange(size, dtype=jnp.int32), half_block, seq_len)
        key_doc = lax.dynamic_slice_in_dim(doc_all, offset, size)
        scores, allowed = score_block(
            query3, key_part, own_pos, doc_rows, key_pos, key_doc, alibi_slopes, scale
        )
        new_top = jnp.maximum(top, jnp.max(scores, axis=2))
        weights = jnp.where(allowed, jnp.exp(scores - new_top[:, :, None]), 0.0)
        factor = jnp.exp(top - new_top)
        total = total * factor + jnp.sum(weights, axis=2)
        accum = accum * jnp.transpose(factor)[:, :, None] + jnp.einsum(
            "hqk,khe->qhe",
            weights.astype(jnp.bfloat16),
            value_part,
            preferred_element_type=jnp.float32,
        )
        return (new_top, total, accum)

    top, total, accum = block_loop(key_piece.shape[0], 512, visit, start_state)
    log_total = top + jnp.log(total)
    attended = accum / jnp.transpose(total)[:, :, None]
    mixed = attended.reshape(count, width).astype(jnp.bfloat16)
    resid = rows_in + project_rows(mixed, w_out) + b_out.astype(jnp.float32)
    norm_two, norm_two_pull = jax.vjp(
        layer_norm, resid, gain_two.astype(jnp.float32), shift_two.astype(jnp.float32)
    )
    h_two = norm_two.astype(jnp.bfloat16)
    w_up, b_up, w_down = (
        lax.all_gather(up_weight, "fsdp", axis=0, tiled=True),
        lax.all_gather(up_bias, "fsdp", axis=0, tiled=True),
        lax.all_gather(down_weight, "fsdp", axis=0, tiled=True),
    )
    up = project_rows(h_two, w_up) + b_up.astype(jnp.float32)
    act, gelu_pull = jax.vjp(gelu_tanh, up)
    act_low = act.astype(jnp.bfloat16)
    branch = jnp.dot(act_low, w_down, preferred_element_type=jnp.float32)
    layer_out = resid + branch + b_down.astype(jnp.float32)
    dup = gelu_pull(project_rows(grad_low, w_down))[0].astype(jnp.bfloat16)
    stacked = lax.psum_scatter(
        jnp.concatenate([cross_rows(dup, h_two), cross_rows(act_low, grad_low)], axis=1).astype(
            jnp.bfloat16
        ),
        "fsdp",
        scatter_dimension=0,
        tiled=True,
    ).astype(jnp.float32)
    up_rows_grad = stacked[:, :width]
    down_rows_grad = stacked[:, width:]
    up_bias_term = jnp.sum(dup, axis=0, dtype=jnp.float32)
    dnorm_two = jnp.dot(dup, w_up, preferred_element_type=jnp.float32)
    dresid_norm, gain_two_grad, shift_two_grad = norm_two_pull(dnorm_two)
    dresid = grad_full + dresid_norm
    dbranch = dresid.astype(jnp.bfloat16)
    out_bias_grad = jnp.sum(dbranch, axis=0, dtype=jnp.float32)
    out_weight_grad = cross_rows(dbranch, mixed)
    dmixed = jnp.dot(dbranch, w_out, preferred_element_type=jnp.float32).astype(jnp.bfloat16)
    dmixed3 = dmixed.reshape(count, heads, head)
    delta = jnp.transpose(jnp.sum(dmixed3.astype(jnp.float32) * attended, axis=2))
    query_key_piece = lax.all_gather(keys, "ctx", axis=0, tiled=True)
    query_value_piece = lax.all_gather(values, "ctx", axis=0, tiled=True)

    def visit(accum_grad, offset, size):
        key_part = lax.dynamic_slice_in_dim(query_key_piece, offset, size).reshape(
            size, heads, head
        )
        value_part = lax.dynamic_slice_in_dim(query_value_piece, offset, size).reshape(
            size, heads, head
        )
        key_pos = token_positions(offset + jnp.arange(size, dtype=jnp.int32), half_block, seq_len)
        key_doc = lax.dynamic_slice_in_dim(doc_all, offset, size)
        scores, allowed = score_block(
            query3, key_part, own_pos, doc_rows, key_pos, key_doc, alibi_slopes, scale
        )
        probs = jnp.where(allowed, jnp.exp(scores - log_total[:, :, None]), 0.0)
        dprobs = jnp.einsum("qhe,khe->hqk", dmixed3, value_part, preferred_element_type=jnp.float32)
        dscores = (probs * (dprobs - delta[:, :, None])).astype(jnp.bfloat16)
        return accum_grad + jnp.einsum(
            "hqk,khe->qhe", dscores, key_part, preferred_element_type=jnp.float32
        )

    query_sum = block_loop(
        query_key_piece.shape[0], 512, visit, jnp.zeros((count, heads, head), jnp.float32)
    )
    dquery = (query_sum * scale).reshape(count, width).astype(jnp.bfloat16)
    total_all, delta_all = (
        lax.all_gather(
            jnp.transpose(log_total).astype(jnp.bfloat16), "ctx", axis=0, tiled=True
        ).astype(jnp.float32),
        lax.all_gather(jnp.transpose(delta).astype(jnp.bfloat16), "ctx", axis=0, tiled=True).astype(
            jnp.float32
        ),
    )
    empty = jnp.zeros((count, heads, head), jnp.float32)
    query_piece = lax.all_gather(query, "ctx", axis=0, tiled=True)
    grad_piece = lax.all_gather(dmixed, "ctx", axis=0, tiled=True)

    def visit(state, offset, size):
        dkeys, dvalues = state
        query_part = lax.dynamic_slice_in_dim(query_piece, offset, size).reshape(size, heads, head)
        grad_part = lax.dynamic_slice_in_dim(grad_piece, offset, size).reshape(size, heads, head)
        query_pos = token_positions(offset + jnp.arange(size, dtype=jnp.int32), half_block, seq_len)
        query_doc = lax.dynamic_slice_in_dim(doc_all, offset, size)
        total_part = jnp.transpose(lax.dynamic_slice_in_dim(total_all, offset, size))
        delta_part = jnp.transpose(lax.dynamic_slice_in_dim(delta_all, offset, size))
        scores, allowed = score_block(
            query_part, keys3, query_pos, query_doc, own_pos, doc_rows, alibi_slopes, scale
        )
        probs = jnp.where(allowed, jnp.exp(scores - total_part[:, :, None]), 0.0)
        dvalues = dvalues + jnp.einsum(
            "hqk,qhe->khe",
            probs.astype(jnp.bfloat16),
            grad_part,
            preferred_element_type=jnp.float32,
        )
        dprobs = jnp.einsum("qhe,khe->hqk", grad_part, values3, preferred_element_type=jnp.float32)
        dscores = (probs * (dprobs - delta_part[:, :, None])).astype(jnp.bfloat16)
        dkeys = dkeys + jnp.einsum(
            "hqk,qhe->khe", dscores, query_part, preferred_element_type=jnp.float32
        )
        return (dkeys, dvalues)

    dkeys, dvalues = block_loop(query_piece.shape[0], 512, visit, (empty, empty))
    dkeys_low = (dkeys * scale).reshape(count, width).astype(jnp.bfloat16)
    dvalues_low = dvalues.reshape(count, width).astype(jnp.bfloat16)
    dfused = jnp.concatenate([dquery, dkeys_low, dvalues_low], axis=1)
    qkv_weight_grad = cross_rows(dfused, h_one)
    qkv_bias_grad = jnp.concatenate(
        [
            jnp.sum(dquery, axis=0, dtype=jnp.float32),
            jnp.sum(dvalues_low, axis=0, dtype=jnp.float32),
        ]
    )
    dnorm_one = jnp.dot(dfused, w_qkv, preferred_element_type=jnp.float32)
    dinput_norm, gain_one_grad, shift_one_grad = norm_one_pull(dnorm_one)
    input_grad = (dresid + dinput_norm).astype(jnp.bfloat16).reshape(tokens.shape)
    down_bias_grad = jnp.sum(grad_full, axis=0)
    shares = (
        lax.psum_scatter(
            qkv_weight_grad.astype(jnp.bfloat16), "fsdp", scatter_dimension=0, tiled=True
        ).astype(jnp.float32),
        lax.psum_scatter(
            out_weight_grad.astype(jnp.bfloat16), "fsdp", scatter_dimension=0, tiled=True
        ).astype(jnp.float32),
        lax.psum_scatter(
            qkv_bias_grad.astype(jnp.bfloat16), "fsdp", scatter_dimension=0, tiled=True
        ).astype(jnp.float32),
        lax.psum_scatter(
            out_bias_grad.astype(jnp.bfloat16), "fsdp", scatter_dimension=0, tiled=True
        ).astype(jnp.float32),
        lax.psum_scatter(
            gain_one_grad.astype(jnp.bfloat16), "fsdp", scatter_dimension=0, tiled=True
        ).astype(jnp.float32),
        lax.psum_scatter(
            shift_one_grad.astype(jnp.bfloat16), "fsdp", scatter_dimension=0, tiled=True
        ).astype(jnp.float32),
        lax.psum_scatter(
            gain_two_grad.astype(jnp.bfloat16), "fsdp", scatter_dimension=0, tiled=True
        ).astype(jnp.float32),
        lax.psum_scatter(
            shift_two_grad.astype(jnp.bfloat16), "fsdp", scatter_dimension=0, tiled=True
        ).astype(jnp.float32),
        lax.psum_scatter(
            up_bias_term.astype(jnp.bfloat16), "fsdp", scatter_dimension=0, tiled=True
        ).astype(jnp.float32),
        lax.psum_scatter(
            down_bias_grad.astype(jnp.bfloat16), "fsdp", scatter_dimension=0, tiled=True
        ).astype(jnp.float32),
    )
    totals = (
        lax.psum(shares[0].astype(jnp.bfloat16), "ctx").astype(jnp.float32),
        lax.psum(shares[1].astype(jnp.bfloat16), "ctx").astype(jnp.float32),
        lax.psum(up_rows_grad.astype(jnp.bfloat16), "ctx").astype(jnp.float32),
        lax.psum(down_rows_grad.astype(jnp.bfloat16), "ctx").astype(jnp.float32),
        lax.psum(shares[2].astype(jnp.bfloat16), "ctx").astype(jnp.float32),
        lax.psum(shares[3].astype(jnp.bfloat16), "ctx").astype(jnp.float32),
        lax.psum(shares[4].astype(jnp.bfloat16), "ctx").astype(jnp.float32),
        lax.psum(shares[5].astype(jnp.bfloat16), "ctx").astype(jnp.float32),
        lax.psum(shares[6].astype(jnp.bfloat16), "ctx").astype(jnp.float32),
        lax.psum(shares[7].astype(jnp.bfloat16), "ctx").astype(jnp.float32),
        lax.psum(shares[8].astype(jnp.bfloat16), "ctx").astype(jnp.float32),
        lax.psum(shares[9].astype(jnp.bfloat16), "ctx").astype(jnp.float32),
    )
    return (
        layer_out.astype(jnp.bfloat16).reshape(tokens.shape),
        input_grad,
        totals[6],
        totals[7],
        totals[0],
        totals[4],
        totals[1],
        totals[5],
        totals[8],
        totals[9],
        totals[2],
        totals[10],
        totals[3],
        totals[11],
    )

F32 = jnp.float32
BF16 = jnp.bfloat16
LOG2E = 1.4426950408889634
LN2 = 0.6931471805599453
TILE = 256
DOC_LANES = 48
GELU_A = 0.7978845608028654
GELU_B = 0.044715


def dot_nt(a, b):
    return lax.dot_general(a, b, (((1,), (1,)), ((), ())), preferred_element_type=F32)


def dot_nn(a, b):
    return lax.dot_general(a, b, (((1,), (0,)), ((), ())), preferred_element_type=F32)


def dot_tn(a, b):
    return lax.dot_general(a, b, (((0,), (0,)), ((), ())), preferred_element_type=F32)


def kernel_call(body, outs, ins, scratch=(), scalars=1, tied=(), spare=7, cost=0):
    groups = [x if isinstance(x, tuple) else (x,) for x in ins[scalars:]]
    flat = [x for group in groups for x in group]
    joined = [
        pltpu.VMEM((sum(x.shape[0] for x in group), *group[0].shape[1:]), group[0].dtype)
        for group in groups
        if len(group) > 1
    ]
    scratch = [*joined, *scratch]
    room = sum(int(np.prod(x.shape)) * jnp.dtype(x.dtype).itemsize for x in scratch)

    def run(*refs):
        numbers, refs = refs[:scalars], refs[scalars:]
        sources, refs = refs[: len(flat)], refs[len(flat) + len(tied) :]
        targets, refs = refs[: len(outs)], refs[len(outs) :]
        places, refs = list(refs[: len(joined)]), refs[len(joined) :]
        held, at = [], 0
        for group in groups:
            if len(group) == 1:
                held.append(sources[at])
            else:
                held.append(places.pop(0))
                row = 0
                for source in sources[at : at + len(group)]:
                    held[-1][row : row + source.shape[0], :] = source[...]
                    row += source.shape[0]
            at += len(group)
        body(*numbers, *held, *targets, *refs)

    vmem = pl.BlockSpec(memory_space=pltpu.VMEM)
    return pl.pallas_call(
        run,
        out_shape=list(outs),
        in_specs=[pl.BlockSpec(memory_space=pltpu.SMEM)] * scalars
        + [vmem] * len(flat)
        + [pl.BlockSpec(memory_space=pl.ANY)] * len(tied),
        out_specs=[vmem] * len(outs),
        scratch_shapes=scratch,
        compiler_params=pltpu.CompilerParams(vmem_limit_bytes=room + spare * 1024 * 1024),
        cost_estimate=pl.CostEstimate(
            flops=int(cost * 1e9), bytes_accessed=0, transcendentals=0
        ),
    )(*ins[:scalars], *flat, *tied)


def shaped(shape, dtype):
    return jax.ShapeDtypeStruct(shape, dtype)


def lanes_of(shape):
    return lax.broadcasted_iota(jnp.int32, shape, len(shape) - 1)


def three_pieces(v):
    high = v.astype(BF16).astype(F32)
    mid = (v - high).astype(BF16).astype(F32)
    return high, mid, v - high - mid


def normed(v):
    mean = jnp.mean(v, axis=-1, keepdims=True)
    centered = v - mean
    spread = jnp.mean(centered * centered, axis=-1, keepdims=True)
    root = lax.rsqrt(spread + EPS)
    return centered * root, root


def norm_back(dout, unit, root, gain):
    dn = dout * gain
    first = jnp.mean(dn, axis=-1, keepdims=True)
    second = jnp.mean(dn * unit, axis=-1, keepdims=True)
    return root * (dn - first - unit * second)


def block_rows(index, half_block):
    return pl.ds(pl.multiple_of(index * half_block, half_block), half_block)


def prepare_kernel(ids, *refs):
    own, w_ref, out_ref, up_ref, down_ref = refs[0:5]
    vectors, (chunk, pack, piece), places, sems = refs[5:14], refs[14:17], refs[17:31], refs[31]
    c = ids[0]

    def rows(ref, start, count):
        return ref.at[pl.ds(pl.multiple_of(start * count, count), count)]

    sources = [
        own,
        rows(w_ref, ids[5], 128),
        rows(out_ref, c, 32),
        rows(up_ref, c, 128),
        rows(down_ref, c, 128),
        *vectors,
    ]
    copies = [
        pltpu.make_async_copy(a, b, sems.at[i]) for i, (a, b) in enumerate(zip(sources, places))
    ]
    for copy in copies:
        copy.start()
    for copy in copies:
        copy.wait()
    doc, g1, s1, ob, g2, s2, db, qb, ub = places[5:]
    docs = doc[...].astype(F32)
    row = jnp.concatenate([docs[0:1], docs[1:2]], axis=1)
    chunk[256:272, :] = jnp.zeros((16, 1024), BF16)
    chunk[256:272, 0:256] = jnp.broadcast_to(row, (16, 256)).astype(BF16)

    def wide(ref):
        size = ref.shape[0]
        return jnp.broadcast_to(ref[...].astype(F32).reshape(1, size), (8, size))

    first = jnp.concatenate([wide(r) for r in (g1, s1, ob, g2)], axis=1)
    at = lax.broadcasted_iota(jnp.int32, (8, 1024), 0)
    first = jnp.where(at < 4, first, wide(ub))
    second = jnp.concatenate([wide(r) for r in (s2, db, qb)], axis=1)
    small = jnp.concatenate([first, second], axis=0).astype(BF16)
    chunk[0:256, :] = places[0][...]
    pack[0:128, :] = places[1][...]
    pack[128:144, :] = small
    pack[144:176, :] = places[2][...]
    piece[0:128, :] = places[3][...]
    piece[128:256, :] = places[4][...]


def project_kernel(ids, slopes, *refs):
    chunks, packs = refs[:8], refs[8:12]
    q_out, k_out, v_out, w_out, par_out, doc_out, h_out, out_rows, small = refs[12:]
    c, f = ids[0], ids[1]
    for k in range(4):
        plane = lax.rem(f + (4 - k), 4)
        small[plane] = packs[k][128:144, :].astype(F32)
        at = pl.multiple_of(plane * 32, 32)
        out_rows[pl.ds(at, 32), :] = packs[k][144:176, :]
        for kind in range(3):

            @pl.when(ids[2 + kind] == plane)
            def _():
                w_out[kind * 128 : (kind + 1) * 128, :] = packs[k][0:128, :]

    rows = [small[p] for p in range(4)]

    def whole(row, start, stop, planes=(0, 1, 2, 3)):
        return jnp.concatenate([rows[p][row * 8 : row * 8 + 1, start:stop] for p in planes], axis=1)

    par_out[0:1, :] = whole(0, 0, 256)
    par_out[1:2, :] = whole(0, 256, 512)
    par_out[2:3, :] = whole(0, 512, 768)
    par_out[3:4, :] = whole(0, 768, 1024)
    par_out[4:5, :] = whole(1, 0, 256)
    par_out[5:6, :] = whole(1, 256, 512)
    par_out[6:7, :] = whole(1, 512, 1024, (0, 1))
    par_out[7:8, :] = whole(1, 512, 1024, (2, 3))
    par_out[8:16, :] = small[f ^ 2][0:8, :]
    par_out[8:9, :] = small[f ^ 2][4:5, :]
    mine = pl.ds(pl.multiple_of(c * 128, 128), 128)
    bias_q = par_out[6:7, mine]
    bias_v = par_out[7:8, mine]
    gain, shift = par_out[0:1, :], par_out[1:2, :]
    weight = w_out[...]
    lane = lanes_of((256, 128))
    row = lax.broadcasted_iota(jnp.int32, (256, 128), 0)
    eye = (
        lax.broadcasted_iota(jnp.int32, (128, 128), 0) == lanes_of((128, 128))
    ).astype(BF16)
    sub = lax.broadcasted_iota(jnp.int32, (128, 256), 0).astype(F32) - 67.0
    is_doc = (lane >= 67) & (lane < 67 + DOC_LANES)
    low = lane < 64
    for d in range(8):
        cc = c ^ d
        h = (normed(chunks[d][0:256, :].astype(F32))[0] * gain + shift).astype(BF16)
        h_out[d % 2, d // 2] = h
        joined = dot_nt(h, weight)
        query = (joined[:, 0:128] + bias_q) * (LOG2E * 0.125)
        keys = joined[:, 128:256]
        values = joined[:, 256:384] + bias_v
        doc_row = chunks[d][256:272, 0:256].astype(F32)[0:1, :]
        doc_out[pl.ds(cc, 1), :] = doc_row[:, 0:128]
        doc_out[pl.ds(8 + cc, 1), :] = doc_row[:, 128:256]
        one_hot = dot_tn((sub == doc_row).astype(BF16), eye)
        pos = jnp.where(row < 128, cc * 128 + row, 2175 - cc * 128 - row).astype(F32)
        q_aug = jnp.where(lane < 67, 1.0, jnp.where(is_doc, one_hot, 0.0))
        k_tail = jnp.where(is_doc, (1.0 - one_hot) * MASKED, jnp.where(lane < 118, 1.0, 0.0))
        for hh in range(2):
            if hh == 1:
                query, keys, values = (pltpu.roll(t, 64, 1) for t in (query, keys, values))
            high, mid, rest = three_pieces(pos * (slopes[2 * c + hh] * LOG2E))
            k_aug = jnp.where(
                lane == 64, high, jnp.where(lane == 65, mid, jnp.where(lane == 66, rest, k_tail))
            )
            parts = (
                (q_out, jnp.where(low, query, q_aug).astype(BF16)),
                (k_out, jnp.where(low, keys, k_aug).astype(BF16)),
                (v_out, jnp.where(low, values, 1.0).astype(BF16)),
            )
            for ref, value in parts:
                ref[hh, block_rows(cc, 128), :] = value[0:128]
                ref[hh, block_rows(8 + cc, 128), :] = value[128:256]


def tile_start(i):
    return i * TILE if i < 4 else 1024 + (7 - i) * TILE


def tile_rows(i):
    start = jnp.where(i < 4, i * TILE, 1024 + (7 - i) * TILE)
    return pl.ds(pl.multiple_of(start, TILE), TILE)


def tile_docs(docs, i):
    at = tile_start(i) // 128
    return docs[at : at + 2, :]


def count_tiles(flags):
    total = jnp.sum(jnp.where(flags, 1.0, 0.0)).astype(jnp.int32)
    return lax.shift_right_logical(total, 8)


def attend_kernel(
    ids, docs_ref, q_ref, k_ref, v_ref, q_out, full_out, m0, m1, m2, m3, mixed_out
):
    docs = docs_ref[...]
    lane = lanes_of((TILE, 128))
    low = lane < 64
    down, right = lax.broadcasted_iota(jnp.int32, (TILE, TILE), 0), lanes_of((TILE, TILE))
    for i in range(8):
        rows = slice(tile_start(i), tile_start(i) + TILE)
        first = count_tiles(docs < jnp.min(tile_docs(docs, i)))
        allowed = (down >= right) if i < 4 else (down <= right)
        queries = [q_ref[hh, rows, :] for hh in range(2)]
        state = []
        for hh in range(2):
            scores = jnp.where(allowed, dot_nt(queries[hh], k_ref[hh, rows, :]), MASKED)
            top = jnp.max(scores, axis=1, keepdims=True)
            weights = jnp.exp2(scores - top).astype(BF16)
            state += [top, dot_nn(weights, v_ref[hh, rows, :])]

        def step(j, carry):
            out = []
            at = tile_rows(j)
            for hh in range(2):
                top, accum = carry[2 * hh], carry[2 * hh + 1]
                scores = dot_nt(queries[hh], k_ref[hh, at, :])
                new_top = jnp.maximum(top, jnp.max(scores, axis=1, keepdims=True))
                weights = jnp.exp2(scores - new_top).astype(BF16)
                accum = accum * jnp.exp2(top - new_top) + dot_nn(weights, v_ref[hh, at, :])
                out += [new_top, accum]
            return tuple(out)

        state = lax.fori_loop(first, i, step, tuple(state))
        outs = []
        for hh in range(2):
            top, accum = state[2 * hh], state[2 * hh + 1]
            total = accum[:, 64:65]
            outs.append(accum / total)
            high, mid, rest = three_pieces(-(top + jnp.log2(total)))
            tail = jnp.where(
                lane == 115,
                high,
                jnp.where(lane == 116, mid, jnp.where(lane == 117, rest, queries[hh].astype(F32))),
            )
            q_out[hh, rows, :] = tail.astype(BF16)
        both = jnp.where(low, outs[0], pltpu.roll(outs[1], 64, 1))
        full_out[rows, :] = both
        half, at = divmod(tile_start(i) // 128, 8)
        for piece in range(2):
            mixed_out[at + piece, half * 128 : (half + 1) * 128, :] = both[
                piece * 128 : (piece + 1) * 128
            ].astype(BF16)
    for e, ref in enumerate((m0, m1, m2, m3)):
        for parity in range(2):
            ref[parity * 256 : (parity + 1) * 256, :] = mixed_out[ids[0] ^ (2 * e + parity)]


def heads_far_kernel(g0, g1, g2, g3, out):
    for e, ref in enumerate((g0, g1, g2, g3)):
        out[e] = ref[256:512, :]


def attend_back_kernel(
    ids, docs_ref, q_ref, k_ref, v_ref, full_ref, g0, g1, g2, g3, g_far, keep, send, grads, dq, dk, dv, all_grads
):
    docs = docs_ref[...]
    lane = lanes_of((256, 128))
    low = lane < 64
    for e, ref in enumerate((g0, g1, g2, g3)):
        all_grads[ids[0] ^ (2 * e)] = ref[0:256, :]
        all_grads[ids[0] ^ (2 * e + 1)] = g_far[e]
    for at in range(8):
        piece = all_grads[at].astype(F32)
        other = jnp.concatenate(
            [
                full_ref[at * 128 : (at + 1) * 128, :],
                full_ref[1024 + at * 128 : 1024 + (at + 1) * 128, :],
            ],
            axis=0,
        )
        product = piece * other
        for hh in range(2):
            delta = jnp.sum(jnp.where(low == (hh == 0), product, 0.0), axis=1, keepdims=True)
            high, mid, rest = three_pieces(-delta)
            tail = jnp.where(
                lane == 64, high, jnp.where(lane == 65, mid, jnp.where(lane == 66, rest, 0.0))
            )
            moved = piece if hh == 0 else pltpu.roll(piece, 64, 1)
            value = jnp.where(low, moved, tail).astype(BF16)
            grads[hh, at * 128 : (at + 1) * 128, :] = value[0:128]
            grads[hh, 1024 + at * 128 : 1024 + (at + 1) * 128, :] = value[128:256]
    dq[...] = jnp.zeros_like(dq)
    down, right = lax.broadcasted_iota(jnp.int32, (TILE, TILE), 0), lanes_of((TILE, TILE))
    for j in range(8):
        rows = slice(tile_start(j), tile_start(j) + TILE)
        last = count_tiles(docs <= jnp.max(tile_docs(docs, j)))
        stop = jnp.where(
            jnp.sum(jnp.where(docs <= jnp.max(tile_docs(docs, j)), 1.0, 0.0)).astype(jnp.int32)
            == last * TILE,
            last,
            last + 1,
        )
        allowed = (down <= right) if j < 4 else (down >= right)
        keys = [k_ref[hh, rows, :] for hh in range(2)]
        values = [v_ref[hh, rows, :] for hh in range(2)]

        def visit(hh, at, masked):
            query, grad = q_ref[hh, at, :], grads[hh, at, :]
            probs = jnp.exp2(dot_nt(keys[hh], query))
            if masked:
                probs = jnp.where(allowed, probs, 0.0)
            dscores = (probs * dot_nt(values[hh], grad)).astype(BF16)
            dq[hh, at, :] += dot_tn(dscores, keys[hh])
            return dot_nn(dscores, query), dot_nn(probs.astype(BF16), grad)

        state = []
        for hh in range(2):
            state += list(visit(hh, rows, True))

        def step(i, carry):
            at = tile_rows(i)
            got = []
            for hh in range(2):
                got += list(visit(hh, at, False))
            return tuple(a + b for a, b in zip(carry, got))

        state = lax.fori_loop(j + 1, stop, step, tuple(state))
        dk[rows, :] = jnp.where(low, state[0], pltpu.roll(state[2], 64, 1)) * LN2
        dv[rows, :] = jnp.where(low, state[1], pltpu.roll(state[3], 64, 1))
    for j in range(4):
        for parity, ref in enumerate((keep, send)):
            cc = ids[0] ^ (2 * j + parity)
            for half in range(2):
                rows = block_rows(8 * half + cc, 128)
                at = slice(half * 128, (half + 1) * 128)
                both = jnp.where(low[0:128], dq[0, rows, :], pltpu.roll(dq[1, rows, :], 64, 1))
                ref[j, at, 0:128] = (both * 0.125).astype(BF16)
                ref[j, at, 128:256] = dk[rows, :].astype(BF16)
                ref[j, at, 256:384] = dv[rows, :].astype(BF16)


def branch_kernel(ids, chunk, g0, g1, g2, g3, g_far, par, *refs):
    pieces, (w_out, mixed_out, resid_out, h_out) = refs[:8], refs[8:]
    for d in range(8):
        for plane in range(4):
            at = pl.multiple_of(plane * 256 + (ids[0] ^ d) * 32, 32)
            w_out[pl.ds(at, 32), :] = pieces[d][plane * 32 : (plane + 1) * 32, :]
    for e, ref in enumerate((g0, g1, g2, g3)):
        for parity, value in enumerate((ref[0:256, :], g_far[e])):
            at = pl.multiple_of((ids[0] ^ (2 * e + parity)) * 128, 128)
            mixed_out[:, pl.ds(at, 128)] = value
    resid = chunk[0:256, :].astype(F32) + dot_nt(mixed_out[...], w_out[...]) + par[2:3, :]
    resid_out[...] = resid
    h_out[...] = (normed(resid)[0] * par[3:4, :] + par[4:5, :]).astype(BF16)


def feed_step(h, cot, up_w, down_w, bias):
    u = dot_nt(h, up_w) + bias
    grad = dot_nt(cot, down_w)
    square = u * u
    th = jnp.tanh(GELU_A * u * (1.0 + GELU_B * square))
    half = 0.5 * (1.0 + th)
    act = (u * half).astype(BF16)
    slope = half + 0.5 * u * (1.0 - th * th) * (GELU_A * (1.0 + 3.0 * GELU_B * square))
    return act, (grad * slope).astype(BF16)


def feed_kernel(h_ref, cot_ref, up_ref, bias_ref, down_ref, act_out, dup_out, acc, dacc):
    h, cot = h_ref[...], cot_ref[...]
    for t in range(4):
        at = slice(t * 256, (t + 1) * 256)
        up_w, down_w = up_ref[at, :], down_ref[at, :]
        act, dup = feed_step(h, cot, up_w, down_w, bias_ref[0:1, at])
        act_out[:, at] = act
        dup_out[:, at] = dup
        if t == 0:
            acc[...] = dot_nn(act, down_w)
            dacc[...] = dot_nn(dup, up_w)
        else:
            acc[...] += dot_nn(act, down_w)
            dacc[...] += dot_nn(dup, up_w)


def feed_other_kernel(ids, h_ref, cot_ref, par, acc, dacc, *refs):
    pieces, (act_out, dup_out, branch, dh) = refs[:8], refs[8:]
    h, cot = h_ref[...], cot_ref[...]
    for t in range(4):
        at = slice(t * 256, (t + 1) * 256)
        two = (pieces[2 * t], pieces[2 * t + 1])
        up_w = jnp.concatenate([r[0:128, :] for r in two], axis=0)
        down_w = jnp.concatenate([r[128:256, :] for r in two], axis=0)
        bias = [
            par[8:9, pl.ds(pl.multiple_of((ids[0] ^ (2 * t + p)) * 128, 128), 128)]
            for p in range(2)
        ]
        act, dup = feed_step(h, cot, up_w, down_w, jnp.concatenate(bias, axis=1))
        act_out[:, at] = act
        dup_out[:, at] = dup
        acc[...] += dot_nn(act, down_w)
        dacc[...] += dot_nn(dup, up_w)
    branch[...] = acc[...].astype(BF16)
    dh[...] = dacc[...].astype(BF16)


def middle_kernel(
    ids, d0, d1, resid_ref, cot_ref, par, w_ref, dresid_out, dbranch_out, m0, m1, m2, m3, sums, held
):
    dh = d0[...].astype(F32) + d1[...].astype(F32)
    unit, root = normed(resid_ref[...])
    cot = cot_ref[...].astype(F32)
    dresid = cot + norm_back(dh, unit, root, par[3:4, :])
    dresid_out[...] = dresid
    dbranch = dresid.astype(BF16)
    dbranch_out[...] = dbranch
    held[...] = dot_nn(dbranch, w_ref[...]).astype(BF16)
    for e, ref in enumerate((m0, m1, m2, m3)):
        for parity in range(2):
            at = pl.multiple_of((ids[0] ^ (2 * e + parity)) * 128, 128)
            ref[parity * 256 : (parity + 1) * 256, :] = held[:, pl.ds(at, 128)]
    sums[...] = jnp.zeros_like(sums)
    sums[0:1, :] = jnp.sum(dbranch.astype(F32), axis=0, keepdims=True)
    sums[1:2, :] = jnp.sum(dh * unit, axis=0, keepdims=True)
    sums[2:3, :] = jnp.sum(dh, axis=0, keepdims=True)
    sums[3:4, :] = jnp.sum(cot, axis=0, keepdims=True)


def feed_weights_kernel(ids, *refs):
    hs, cots, dups, acts, dups_far, acts_far = (refs[2 * i : 2 * i + 2] for i in range(6))
    keep, send, bias, all_rows = refs[12:]
    c = ids[0]

    def product(lefts, at, rights):
        return sum(dot_tn(a[:, at], b[...]) for a, b in zip(lefts, rights)).astype(BF16)

    for t in range(4):
        at = slice(t * 256, (t + 1) * 256)
        for which, (lefts, rights) in enumerate(((dups, hs), (acts, cots))):
            all_rows[which, at, :] = product(lefts, at, rights)
        for which, (lefts, rights) in enumerate(((dups_far, hs), (acts_far, cots))):
            both = product(lefts, at, rights)
            for parity, ref in enumerate((keep, send)):
                place = slice(256 + which * 128, 384 + which * 128)
                ref[t, place, :] = both[parity * 128 : (parity + 1) * 128]
    for e in range(4):
        for parity, ref in enumerate((keep, send)):
            rows = block_rows(c ^ (2 * e + parity), 128)
            ref[e, 0:128, :] = all_rows[0, rows, :]
            ref[e, 128:256, :] = all_rows[1, rows, :]

    def total(refs):
        return sum(jnp.sum(r[...].astype(F32), axis=0, keepdims=True) for r in refs)

    bias[0:1, :] = total(dups)
    far = total(dups_far)
    for d in range(8):
        at = pl.ds(pl.multiple_of((c ^ d) * 128, 128), 128)
        bias[8:9, at] = far[:, d * 128 : (d + 1) * 128]


def out_weights_kernel(ids, dbranch, mixed, keep, send, total):
    for t in range(4):
        at = slice(t * 256, (t + 1) * 256)
        total[at, :] = dot_tn(dbranch[:, at], mixed[...]).astype(BF16)
    for e in range(4):
        for parity, ref in enumerate((keep, send)):
            cc = ids[0] ^ (2 * e + parity)
            for plane in range(4):
                at = pl.multiple_of(plane * 256 + cc * 32, 32)
                ref[e, plane * 32 : (plane + 1) * 32, :] = total[pl.ds(at, 32), :]


def added(*values):
    return sum(v.astype(F32) for v in values).astype(BF16)


def pair_sum_kernel(keep, got, x_out, y_out, own_out):
    half = keep.shape[1] // 2
    first, second = slice(0, half), slice(half, 2 * half)
    for e, part in ((1, first), (3, first)):
        x_out[half * (e // 2) : half * (e // 2 + 1), :] = added(keep[e, part], got[e, part])
    for e, part in ((2, second), (3, second)):
        y_out[half * (e - 2) : half * (e - 1), :] = added(keep[e, part], got[e, part])
    own_out[0 : 2 * half, :] = added(keep[0], got[0])
    own_out[2 * half : 3 * half, :] = added(keep[2, first], got[2, first])
    own_out[3 * half : 4 * half, :] = added(keep[1, second], got[1, second])


def relay_kernel(own, from_x, from_y, kept, x_out, y_out):
    half = own.shape[0] // 4
    kept[0:half, :] = added(own[0:half, :], from_x[0:half, :])
    y_out[...] = added(own[2 * half : 3 * half, :], from_x[half:, :])
    kept[half:, :] = added(own[half : 2 * half, :], from_y[0:half, :])
    x_out[...] = added(own[3 * half :, :], from_y[half:, :])


def owned_kernel(kept, from_y, from_x, near, far):
    half = kept.shape[0] // 2
    near[...] = added(kept[0:half, :], from_y[...])
    far[...] = added(kept[half:, :], from_x[...])


def small_sum_kernel(keep, got, *outs):
    for e in range(4):
        outs[e][...] = added(keep[e], got[e])


def sum_kernel(*refs):
    refs[-1][...] = added(*(r[...] for r in refs[:-1]))


def layer_out_kernel(resid, par, one, two, out):
    out[...] = (resid[...] + par[5:6, :] + one[...].astype(F32) + two[...].astype(F32)).astype(BF16)


def head_weights_kernel(keep, send, h_ref, total):
    for parity, ref in enumerate((keep, send)):
        for j in range(4):
            got = dot_tn(ref[j], h_ref[parity, j])
            if parity == 0 and j == 0:
                total[...] = got
            else:
                total[...] += got


def unproject_kernel(ids, *refs):
    chunks, (near, far, bias_far, w_near, w_far, par, sums, up_sums, wsum, out_share) = refs[:4], refs[4:14]
    x_out, y_out, own_out, s0, s1, s2, s3, slots, small = refs[14:]
    c, f = ids[0], ids[1]
    near_w, far_w = w_near[...], w_far[...]
    gain_grad = shift_grad = bias_grad = 0.0
    places = (
        (own_out, 0, own_out, 128),
        (x_out, 0, own_out, 384),
        (own_out, 256, y_out, 0),
        (x_out, 128, y_out, 128),
    )
    for e, chunk in enumerate(chunks):
        grads = near[e]
        unit = normed(chunk[0:256, :].astype(F32))[0]
        share = dot_nn(grads, near_w) + dot_nn(far[e], far_w)
        top, at, bottom, below = places[e]
        top[at : at + 128, :] = share[0:128].astype(BF16)
        bottom[below : below + 128, :] = share[128:256].astype(BF16)
        gain_grad += jnp.sum(share * unit, axis=0, keepdims=True)
        shift_grad += jnp.sum(share, axis=0, keepdims=True)
        bias_grad += jnp.sum(grads.astype(F32) + bias_far[e].astype(F32), axis=0, keepdims=True)
    small[...] = jnp.zeros_like(small)
    for p in range(4):
        at = slice(p * 256, (p + 1) * 256)
        small[p, 0:1, 0:256] = gain_grad[:, at]
        small[p, 0:1, 256:512] = shift_grad[:, at]
        small[p, 0:1, 512:768] = sums[0:1, at]
        small[p, 0:1, 768:1024] = sums[1:2, at]
        small[p, 1:2, 0:256] = sums[2:3, at]
        small[p, 1:2, 256:512] = sums[3:4, at]
        small[p, 1:2, 512:640] = bias_grad[:, 0:128] if p < 2 else bias_grad[:, 256:384]
        up_far = jnp.where(f == p ^ 2, up_sums[8:9, :], 0.0)
        small[p, 2:3, :] = jnp.where(f == p, up_sums[0:1, :], up_far)
        start = pl.multiple_of(ids[6 + p] * 128, 128)
        slots[p, 0:128, :] = wsum[pl.ds(start, 128), :].astype(BF16)
        slots[p, 128:144, :] = small[p].astype(BF16)
        slots[p, 144:176, :] = out_share[p * 32 : (p + 1) * 32, :]
    for k, ref in enumerate((s0, s1, s2, s3)):
        ref[...] = slots[lax.rem(f + k, 4)]


def input_kernel(kept, from_y, from_x, chunk, par, dresid, out):
    moved = jnp.concatenate([from_y[...], from_x[...]], axis=0)
    dh = kept[...].astype(F32) + moved.astype(F32)
    unit, root = normed(chunk[0:256, :].astype(F32))
    out[...] = (dresid[...] + norm_back(dh, unit, root, par[0:1, :])).astype(BF16)


def feed_grads_kernel(ids, *refs):
    pieces, (up_out, down_out) = refs[:8], refs[8:]
    for d in range(8):
        rows = block_rows(ids[0] ^ d, 128)
        up_out[rows, :] = pieces[d][0:128, :].astype(F32)
        down_out[rows, :] = pieces[d][128:256, :].astype(F32)


def last_grads_kernel(ids, *refs):
    pieces, (qkv_out, out_out, vec_out, bias_out) = refs[:8], refs[8:]
    c, f = ids[0], ids[1]
    total = 0.0
    for d in range(8):
        cc = c ^ d
        place = lax.rem(cc + 24 - 6 * f, 8)

        @pl.when(place < 6)
        def _():
            qkv_out[block_rows(place, 128), :] = pieces[d][0:128, :].astype(F32)

        out_out[pl.ds(pl.multiple_of(cc * 32, 32), 32), :] = pieces[d][144:176, :].astype(F32)
        rows = pieces[d][128:144, :].astype(F32)
        total += rows

        @pl.when(lax.div(cc, 4) == lax.rem(f, 2))
        def _():
            at = pl.multiple_of(lax.rem(cc, 4) * 128, 128)
            bias_out[0:1, pl.ds(at, 128)] = rows[1:2, 512:640]

    vec_out[...] = total


def per_device(
    tokens,
    doc_ids,
    alibi_slopes,
    ln1_gain,
    ln1_shift,
    qkv_weight,
    qkv_bias,
    out_weight,
    out_bias,
    ln2_gain,
    ln2_shift,
    up_weight,
    up_bias,
    down_weight,
    down_bias,
    cotangent,
):
    c, f = lax.axis_index("ctx"), lax.axis_index("fsdp")
    width = 1024

    def swap(v, d):
        return lax.ppermute(v, "ctx", [(i, i ^ d) for i in range(8)])

    def shift(v, k):
        return lax.ppermute(v, "fsdp", [(i, (i + k) % 4) for i in range(4)])

    def pair(v):
        return lax.ppermute(v, "fsdp", [(i, i ^ 1) for i in range(4)])

    def after(value, *earlier):
        return lax.optimization_barrier((value, earlier))[0]

    def spread(v):
        near = [v] + [swap(v, d) for d in (2, 4, 6)]
        return [t for e in near for t in (e, swap(e, 1))]

    def spread_relayed(v, cut):
        from_x, from_y = swap(v, 2), swap(v, 4)
        top, bottom = swap(from_x[:cut], 4), swap(from_y[cut:], 2)
        pairs = [(p, swap(p, 1)) for p in (v, from_x, from_y, top, bottom)]
        last = [(pairs[3][side], pairs[4][side]) for side in range(2)]
        return [t for p in pairs[:3] for t in p] + last

    table = np.zeros((32, 16), np.int32)
    for ci in range(8):
        for fi in range(4):
            at = ci * 4 + fi
            table[at, 0:2] = ci, fi
            planes = [(8 * kind + ci) // 6 for kind in range(3)]
            table[at, 2:5] = planes
            for kind in range(3):
                if planes[kind] == fi:
                    table[at, 5] = (8 * kind + ci) % 6
            for k in range(4):
                if k in planes:
                    table[at, 6 + k] = planes.index(k)
    ids = lax.dynamic_index_in_dim(jnp.asarray(table), c * 4 + f, 0, keepdims=False)

    own = tokens.reshape(256, width)
    cot = cotangent.reshape(256, width)
    vectors_in = [ln1_gain, ln1_shift, out_bias, ln2_gain, ln2_shift, down_bias, qkv_bias, up_bias]
    vectors_in = [doc_ids.reshape(2, 128)] + vectors_in
    hbm = pl.BlockSpec(memory_space=pltpu.HBM)
    outs = [shaped((272, width), BF16), shaped((176, width), BF16), shaped((256, width), BF16)]
    sizes = [(size, width) for size in (256, 128, 32, 128, 128)]
    chunk, pack, piece = pl.pallas_call(
        prepare_kernel,
        out_shape=outs,
        in_specs=[pl.BlockSpec(memory_space=pltpu.SMEM)] + [hbm] * 14,
        out_specs=[pl.BlockSpec(memory_space=pltpu.VMEM)] * 3,
        scratch_shapes=[pltpu.VMEM(size, BF16) for size in sizes]
        + [pltpu.VMEM(x.shape, x.dtype) for x in vectors_in]
        + [pltpu.SemaphoreType.DMA((14,))],
        compiler_params=pltpu.CompilerParams(vmem_limit_bytes=58 * 1024 * 1024),
        cost_estimate=pl.CostEstimate(flops=0, bytes_accessed=0, transcendentals=0),
    )(ids, own, qkv_weight, out_weight, up_weight, down_weight, *vectors_in)
    packs = [pack] + [shift(pack, k) for k in (1, 2, 3)]
    chunks = spread_relayed(chunk, 128)

    heads = shaped((2, 2048, 128), BF16)
    q_one, keys, values, w_heads, par, docs, h_one, out_rows = kernel_call(
        project_kernel,
        [
            heads,
            heads,
            heads,
            shaped((384, width), BF16),
            shaped((16, width), F32),
            shaped((16, 128), F32),
            shaped((2, 4, 256, width), BF16),
            shaped((128, width), BF16),
        ],
        [ids, alibi_slopes, *chunks, *packs],
        [pltpu.VMEM((4, 16, width), F32)],
        scalars=2,
        spare=12,
        cost=2,
    )
    out_near = [out_rows] + [swap(out_rows, d) for d in (2, 4, 6)]
    far_piece = shift(after(piece, packs), 2)
    cot_near = pair(after(cot, packs))
    pieces_of_heads = [shaped((512, 128), BF16)] * 4

    def swap_heads(parts):
        got = [parts[0]] + [swap(parts[e], 2 * e) for e in (1, 2, 3)]
        far = kernel_call(heads_far_kernel, [shaped((4, 256, 128), BF16)], got, scalars=0)[0]
        return [*got, swap(far, 1)]

    q_two, full, *mixed_parts = kernel_call(
        attend_kernel,
        [heads, shaped((2048, 128), F32), *pieces_of_heads],
        [ids, docs, q_one, keys, values],
        [pltpu.VMEM((8, 256, 128), BF16)],
        spare=8,
        cost=4,
    )
    out_pieces = [t for v in out_near for t in (v, swap(after(v, full), 1))]
    mixed_in = swap_heads(mixed_parts)
    far_piece = after(far_piece, mixed_in[-1])
    far_near = [far_piece] + [swap(far_piece, d) for d in (2, 4, 6)]
    rows = shaped((256, width), BF16)
    full_rows = shaped((256, width), F32)
    w_out, mixed, resid, h_two = kernel_call(
        branch_kernel,
        [shaped((width, width), BF16), rows, full_rows, rows],
        [ids, chunk, *mixed_in, par, *out_pieces],
    )
    h_near = pair(h_two)
    far_pieces = [t for v in far_near for t in (v, swap(after(v, h_two), 1))]
    up_row = up_bias.astype(F32).reshape(1, width)

    def feed(h, cots):
        return kernel_call(
            feed_kernel,
            [rows, rows, full_rows, full_rows],
            [h, cots, up_weight, up_row, down_weight],
            scalars=0,
            spare=8,
            cost=1,
        )

    def feed_other(h, cots, accs):
        return kernel_call(
            feed_other_kernel,
            [rows, rows, rows, rows],
            [ids, h, cots, par, *accs, *far_pieces],
            spare=8,
            cost=1,
        )

    act_own, dup_own, *accs_own = feed(h_two, cot)
    act_near, dup_near, *accs_near = feed(h_near, cot_near)
    act_near_far, dup_near_far, branch_near, dh_near = feed_other(h_near, cot_near, accs_near)
    dh_got = pair(dh_near)
    act_own_far, dup_own_far, branch_own, dh_own = feed_other(h_two, after(cot, dh_near), accs_own)
    big = shaped((4, 512, width), BF16)
    keep, send, up_sums = kernel_call(
        feed_weights_kernel,
        [big, big, shaped((16, width), F32)],
        [
            ids,
            h_two,
            h_near,
            cot,
            cot_near,
            dup_own,
            dup_near,
            act_own,
            act_near,
            dup_own_far,
            dup_near_far,
            act_own_far,
            act_near_far,
        ],
        [pltpu.VMEM((2, width, width), BF16)],
        spare=8,
        cost=3,
    )
    dresid, dbranch, *dmixed_parts, sums = kernel_call(
        middle_kernel,
        [full_rows, rows, *pieces_of_heads, shaped((8, width), F32)],
        [ids, dh_own, dh_got, resid, cot, par, w_out],
        [pltpu.VMEM((256, width), BF16)],
    )
    dmixed_heads = swap_heads(dmixed_parts)

    def shape(*size):
        return shaped((*size, width), BF16)

    def relay(own_part, x_part, y_part):
        from_x, from_y = swap(x_part, 2), swap(y_part, 4)
        half = own_part.shape[0] // 4
        kept, x_next, y_next = kernel_call(
            relay_kernel,
            [shape(2 * half), shape(half), shape(half)],
            [own_part, from_x, from_y],
            scalars=0,
        )
        return kept, swap(y_next, 4), swap(x_next, 2)

    x_part, y_part, own_part = kernel_call(
        pair_sum_kernel,
        [shape(512), shape(512), shape(1024)],
        [keep, swap(send, 1)],
        scalars=0,
    )
    feed_kept = relay(own_part, x_part, y_part)
    feed_near, feed_far = kernel_call(
        owned_kernel, [shape(256), shape(256)], list(feed_kept), scalars=0
    )
    out_keep, out_send = kernel_call(
        out_weights_kernel,
        [shape(4, 128), shape(4, 128)],
        [ids, dbranch, mixed],
        [pltpu.VMEM((width, width), BF16)],
    )
    out_parts = kernel_call(
        small_sum_kernel, [shape(128)] * 4, [out_keep, swap(out_send, 1)], scalars=0
    )
    out_parts = [out_parts[0]] + [swap(out_parts[e], 2 * e) for e in (1, 2, 3)]
    out_share = kernel_call(sum_kernel, [shape(128)], out_parts, scalars=0)[0]
    branch_got = pair(after(branch_near, dbranch))
    layer_out = kernel_call(
        layer_out_kernel, [rows], [resid, par, branch_own, branch_got], scalars=0
    )[0]

    blocks = shaped((4, 256, 384), BF16)
    near, send = kernel_call(
        attend_back_kernel,
        [blocks, blocks],
        [ids, docs, q_two, keys, values, full, *dmixed_heads],
        [
            pltpu.VMEM((2, 2048, 128), BF16),
            pltpu.VMEM((2, 2048, 128), F32),
            pltpu.VMEM((2048, 128), F32),
            pltpu.VMEM((2048, 128), F32),
            pltpu.VMEM((8, 256, 128), BF16),
        ],
        spare=8,
        cost=6,
        tied=[own_part, out_parts[0]],
    )
    far = swap(send, 1)
    wsum = kernel_call(
        head_weights_kernel,
        [shaped((384, width), F32)],
        [near, send, h_one],
        scalars=0,
        tied=[feed_kept[0], layer_out],
    )[0]
    x_part, y_part, own_part, *slots = kernel_call(
        unproject_kernel,
        [shape(256), shape(256), shape(512), *[shape(176)] * 4],
        [
            ids,
            *chunks[0::2],
            near,
            far,
            send,
            w_heads,
            swap(w_heads, 1),
            par,
            sums,
            up_sums,
            wsum,
            out_share,
        ],
        [pltpu.VMEM((4, 176, width), BF16), pltpu.VMEM((4, 16, width), F32)],
        spare=8,
    )
    slots_got = [slots[0]] + [shift(slots[k], k) for k in (1, 2, 3)]
    input_grad = kernel_call(
        input_kernel, [rows], [*relay(own_part, x_part, y_part), chunk, par, dresid], scalars=0
    )[0]
    feed_sum = kernel_call(
        sum_kernel, [shape(256)], [feed_near, shift(feed_far, 2)], scalars=0
    )[0]
    up_grad, down_grad = kernel_call(
        feed_grads_kernel,
        [shaped((width, width), F32)] * 2,
        [ids, *spread_relayed(feed_sum, 128)],
        spare=18,
    )
    slot_sum = kernel_call(sum_kernel, [shape(176)], slots_got, scalars=0)[0]
    qkv_grad, out_grad, vectors, bias_grad = kernel_call(
        last_grads_kernel,
        [
            shaped((768, width), F32),
            shaped((256, width), F32),
            shaped((16, width), F32),
            shaped((1, 512), F32),
        ],
        [ids, *spread(slot_sum)],
        spare=14,
    )
    return (
        layer_out.reshape(tokens.shape),
        input_grad.reshape(tokens.shape),
        vectors[0, 0:256],
        vectors[0, 256:512],
        qkv_grad,
        bias_grad.reshape(512),
        out_grad,
        vectors[0, 512:768],
        vectors[0, 768:1024],
        vectors[1, 0:256],
        up_grad,
        vectors[2],
        down_grad,
        vectors[1, 256:512],
    )


def on_small_slice(mesh, tokens, slopes):
    return (
        mesh.shape["ctx"] == 8
        and mesh.shape["fsdp"] == 4
        and tokens.shape == (4, 2, 1024, 1024)
        and slopes.shape == (16,)
    )


def solution(mesh):
    in_specs = (
        P("fsdp", None, "ctx", None),
        P("fsdp", None, "ctx"),
        P(),
        P("fsdp"),
        P("fsdp"),
        P("fsdp", None),
        P("fsdp"),
        P("fsdp", None),
        P("fsdp"),
        P("fsdp"),
        P("fsdp"),
        P("fsdp", None),
        P("fsdp"),
        P("fsdp", None),
        P("fsdp"),
        P("fsdp", None, "ctx", None),
    )
    out_specs = (
        P("fsdp", None, "ctx", None),
        P("fsdp", None, "ctx", None),
        P("fsdp"),
        P("fsdp"),
        P("fsdp", None),
        P("fsdp"),
        P("fsdp", None),
        P("fsdp"),
        P("fsdp"),
        P("fsdp"),
        P("fsdp", None),
        P("fsdp"),
        P("fsdp", None),
        P("fsdp"),
    )
    def layer(*args):
        body = per_device if on_small_slice(mesh, args[0], args[2]) else gathered_device
        return jax.shard_map(
            body, mesh=mesh, in_specs=in_specs, out_specs=out_specs, check_vma=False
        )(*args)

    return layer
```

```python
import functools

import jax
import jax.numpy as jnp
import numpy as np
from jax import lax
from jax.experimental import pallas as pl
from jax.experimental.pallas import tpu as pltpu
from jax.sharding import PartitionSpec as P

EPS = 1e-05
MASKED = -1e30


def layer_norm(v, gain, shift):
    mean = jnp.mean(v, axis=-1, keepdims=True)
    centered = v - mean
    spread = jnp.mean(centered * centered, axis=-1, keepdims=True)
    return centered * lax.rsqrt(spread + EPS) * gain + shift


def gelu_tanh(v):
    return jax.nn.gelu(v, approximate=True)


def project_rows(values_in, weight):
    return lax.dot_general(
        values_in, weight, (((1,), (1,)), ((), ())), preferred_element_type=jnp.float32
    )


def cross_rows(left, right):
    return lax.dot_general(
        left, right, (((0,), (0,)), ((), ())), preferred_element_type=jnp.float32
    )


def token_positions(index, half_block, seq_len):
    owner = index // (2 * half_block)
    inside = index % (2 * half_block)
    return jnp.where(
        inside < half_block,
        owner * half_block + inside,
        seq_len - 1 - (owner * half_block + inside - half_block),
    )


def score_block(query3, keys3, query_pos, query_doc, key_pos, key_doc, slopes, scale):
    raw = jnp.einsum("qhe,khe->hqk", query3, keys3, preferred_element_type=jnp.float32) * scale
    distance = (query_pos[:, None] - key_pos[None, :]).astype(jnp.float32)
    scores = raw - slopes[:, None, None] * distance[None]
    allowed = ((key_pos[None, :] <= query_pos[:, None]) & (key_doc[None, :] == query_doc[:, None]))[
        None
    ]
    return (jnp.where(allowed, scores, MASKED), allowed)


def block_loop(total, size, visit, state):

    def turn_body(turn, inner):
        return visit(inner, turn * size, size)

    return lax.fori_loop(0, total // size, turn_body, state)


def gathered_device(
    tokens,
    doc_ids,
    alibi_slopes,
    ln1_gain,
    ln1_shift,
    qkv_weight,
    qkv_bias,
    out_weight,
    out_bias,
    ln2_gain,
    ln2_shift,
    up_weight,
    up_bias,
    down_weight,
    down_bias,
    cotangent,
):
    half_block = tokens.shape[2]
    width = tokens.shape[3]
    count = 2 * half_block
    heads = alibi_slopes.shape[0]
    head = width // heads
    scale = head ** (-0.5)
    seq_len = count * lax.axis_size("ctx")
    rows_in = tokens.reshape(count, width).astype(jnp.float32)
    doc_rows = doc_ids.reshape(count)
    grad_low = cotangent.reshape(count, width)
    grad_full = grad_low.astype(jnp.float32)
    own_pos = token_positions(
        lax.axis_index("ctx") * count + jnp.arange(count, dtype=jnp.int32), half_block, seq_len
    )
    gain_one, shift_one, w_qkv, b_qkv, w_out, b_out, gain_two, shift_two, b_down = (
        lax.all_gather(ln1_gain, "fsdp", axis=0, tiled=True),
        lax.all_gather(ln1_shift, "fsdp", axis=0, tiled=True),
        lax.all_gather(qkv_weight, "fsdp", axis=0, tiled=True),
        lax.all_gather(qkv_bias, "fsdp", axis=0, tiled=True),
        lax.all_gather(out_weight, "fsdp", axis=0, tiled=True),
        lax.all_gather(out_bias, "fsdp", axis=0, tiled=True),
        lax.all_gather(ln2_gain, "fsdp", axis=0, tiled=True),
        lax.all_gather(ln2_shift, "fsdp", axis=0, tiled=True),
        lax.all_gather(down_bias, "fsdp", axis=0, tiled=True),
    )
    norm_one, norm_one_pull = jax.vjp(
        layer_norm, rows_in, gain_one.astype(jnp.float32), shift_one.astype(jnp.float32)
    )
    h_one = norm_one.astype(jnp.bfloat16)
    joined = project_rows(h_one, w_qkv)
    bias_full = b_qkv.astype(jnp.float32)
    query = (joined[:, :width] + bias_full[:width]).astype(jnp.bfloat16)
    keys = joined[:, width : 2 * width].astype(jnp.bfloat16)
    values = (joined[:, 2 * width :] + bias_full[width:]).astype(jnp.bfloat16)
    query3 = query.reshape(count, heads, head)
    keys3 = keys.reshape(count, heads, head)
    values3 = values.reshape(count, heads, head)
    doc_all = lax.all_gather(doc_rows, "ctx", axis=0, tiled=True)
    start_state = (
        jnp.full((heads, count), MASKED, jnp.float32),
        jnp.zeros((heads, count), jnp.float32),
        jnp.zeros((count, heads, head), jnp.float32),
    )
    key_piece = lax.all_gather(keys, "ctx", axis=0, tiled=True)
    value_piece = lax.all_gather(values, "ctx", axis=0, tiled=True)

    def visit(state, offset, size):
        top, total, accum = state
        key_part = lax.dynamic_slice_in_dim(key_piece, offset, size).reshape(size, heads, head)
        value_part = lax.dynamic_slice_in_dim(value_piece, offset, size).reshape(size, heads, head)
        key_pos = token_positions(offset + jnp.arange(size, dtype=jnp.int32), half_block, seq_len)
        key_doc = lax.dynamic_slice_in_dim(doc_all, offset, size)
        scores, allowed = score_block(
            query3, key_part, own_pos, doc_rows, key_pos, key_doc, alibi_slopes, scale
        )
        new_top = jnp.maximum(top, jnp.max(scores, axis=2))
        weights = jnp.where(allowed, jnp.exp(scores - new_top[:, :, None]), 0.0)
        factor = jnp.exp(top - new_top)
        total = total * factor + jnp.sum(weights, axis=2)
        accum = accum * jnp.transpose(factor)[:, :, None] + jnp.einsum(
            "hqk,khe->qhe",
            weights.astype(jnp.bfloat16),
            value_part,
            preferred_element_type=jnp.float32,
        )
        return (new_top, total, accum)

    top, total, accum = block_loop(key_piece.shape[0], 512, visit, start_state)
    log_total = top + jnp.log(total)
    attended = accum / jnp.transpose(total)[:, :, None]
    mixed = attended.reshape(count, width).astype(jnp.bfloat16)
    resid = rows_in + project_rows(mixed, w_out) + b_out.astype(jnp.float32)
    norm_two, norm_two_pull = jax.vjp(
        layer_norm, resid, gain_two.astype(jnp.float32), shift_two.astype(jnp.float32)
    )
    h_two = norm_two.astype(jnp.bfloat16)
    w_up, b_up, w_down = (
        lax.all_gather(up_weight, "fsdp", axis=0, tiled=True),
        lax.all_gather(up_bias, "fsdp", axis=0, tiled=True),
        lax.all_gather(down_weight, "fsdp", axis=0, tiled=True),
    )
    up = project_rows(h_two, w_up) + b_up.astype(jnp.float32)
    act, gelu_pull = jax.vjp(gelu_tanh, up)
    act_low = act.astype(jnp.bfloat16)
    branch = jnp.dot(act_low, w_down, preferred_element_type=jnp.float32)
    layer_out = resid + branch + b_down.astype(jnp.float32)
    dup = gelu_pull(project_rows(grad_low, w_down))[0].astype(jnp.bfloat16)
    stacked = lax.psum_scatter(
        jnp.concatenate([cross_rows(dup, h_two), cross_rows(act_low, grad_low)], axis=1).astype(
            jnp.bfloat16
        ),
        "fsdp",
        scatter_dimension=0,
        tiled=True,
    ).astype(jnp.float32)
    up_rows_grad = stacked[:, :width]
    down_rows_grad = stacked[:, width:]
    up_bias_term = jnp.sum(dup, axis=0, dtype=jnp.float32)
    dnorm_two = jnp.dot(dup, w_up, preferred_element_type=jnp.float32)
    dresid_norm, gain_two_grad, shift_two_grad = norm_two_pull(dnorm_two)
    dresid = grad_full + dresid_norm
    dbranch = dresid.astype(jnp.bfloat16)
    out_bias_grad = jnp.sum(dbranch, axis=0, dtype=jnp.float32)
    out_weight_grad = cross_rows(dbranch, mixed)
    dmixed = jnp.dot(dbranch, w_out, preferred_element_type=jnp.float32).astype(jnp.bfloat16)
    dmixed3 = dmixed.reshape(count, heads, head)
    delta = jnp.transpose(jnp.sum(dmixed3.astype(jnp.float32) * attended, axis=2))
    query_key_piece = lax.all_gather(keys, "ctx", axis=0, tiled=True)
    query_value_piece = lax.all_gather(values, "ctx", axis=0, tiled=True)

    def visit(accum_grad, offset, size):
        key_part = lax.dynamic_slice_in_dim(query_key_piece, offset, size).reshape(
            size, heads, head
        )
        value_part = lax.dynamic_slice_in_dim(query_value_piece, offset, size).reshape(
            size, heads, head
        )
        key_pos = token_positions(offset + jnp.arange(size, dtype=jnp.int32), half_block, seq_len)
        key_doc = lax.dynamic_slice_in_dim(doc_all, offset, size)
        scores, allowed = score_block(
            query3, key_part, own_pos, doc_rows, key_pos, key_doc, alibi_slopes, scale
        )
        probs = jnp.where(allowed, jnp.exp(scores - log_total[:, :, None]), 0.0)
        dprobs = jnp.einsum("qhe,khe->hqk", dmixed3, value_part, preferred_element_type=jnp.float32)
        dscores = (probs * (dprobs - delta[:, :, None])).astype(jnp.bfloat16)
        return accum_grad + jnp.einsum(
            "hqk,khe->qhe", dscores, key_part, preferred_element_type=jnp.float32
        )

    query_sum = block_loop(
        query_key_piece.shape[0], 512, visit, jnp.zeros((count, heads, head), jnp.float32)
    )
    dquery = (query_sum * scale).reshape(count, width).astype(jnp.bfloat16)
    total_all, delta_all = (
        lax.all_gather(
            jnp.transpose(log_total).astype(jnp.bfloat16), "ctx", axis=0, tiled=True
        ).astype(jnp.float32),
        lax.all_gather(jnp.transpose(delta).astype(jnp.bfloat16), "ctx", axis=0, tiled=True).astype(
            jnp.float32
        ),
    )
    empty = jnp.zeros((count, heads, head), jnp.float32)
    query_piece = lax.all_gather(query, "ctx", axis=0, tiled=True)
    grad_piece = lax.all_gather(dmixed, "ctx", axis=0, tiled=True)

    def visit(state, offset, size):
        dkeys, dvalues = state
        query_part = lax.dynamic_slice_in_dim(query_piece, offset, size).reshape(size, heads, head)
        grad_part = lax.dynamic_slice_in_dim(grad_piece, offset, size).reshape(size, heads, head)
        query_pos = token_positions(offset + jnp.arange(size, dtype=jnp.int32), half_block, seq_len)
        query_doc = lax.dynamic_slice_in_dim(doc_all, offset, size)
        total_part = jnp.transpose(lax.dynamic_slice_in_dim(total_all, offset, size))
        delta_part = jnp.transpose(lax.dynamic_slice_in_dim(delta_all, offset, size))
        scores, allowed = score_block(
            query_part, keys3, query_pos, query_doc, own_pos, doc_rows, alibi_slopes, scale
        )
        probs = jnp.where(allowed, jnp.exp(scores - total_part[:, :, None]), 0.0)
        dvalues = dvalues + jnp.einsum(
            "hqk,qhe->khe",
            probs.astype(jnp.bfloat16),
            grad_part,
            preferred_element_type=jnp.float32,
        )
        dprobs = jnp.einsum("qhe,khe->hqk", grad_part, values3, preferred_element_type=jnp.float32)
        dscores = (probs * (dprobs - delta_part[:, :, None])).astype(jnp.bfloat16)
        dkeys = dkeys + jnp.einsum(
            "hqk,qhe->khe", dscores, query_part, preferred_element_type=jnp.float32
        )
        return (dkeys, dvalues)

    dkeys, dvalues = block_loop(query_piece.shape[0], 512, visit, (empty, empty))
    dkeys_low = (dkeys * scale).reshape(count, width).astype(jnp.bfloat16)
    dvalues_low = dvalues.reshape(count, width).astype(jnp.bfloat16)
    dfused = jnp.concatenate([dquery, dkeys_low, dvalues_low], axis=1)
    qkv_weight_grad = cross_rows(dfused, h_one)
    qkv_bias_grad = jnp.concatenate(
        [
            jnp.sum(dquery, axis=0, dtype=jnp.float32),
            jnp.sum(dvalues_low, axis=0, dtype=jnp.float32),
        ]
    )
    dnorm_one = jnp.dot(dfused, w_qkv, preferred_element_type=jnp.float32)
    dinput_norm, gain_one_grad, shift_one_grad = norm_one_pull(dnorm_one)
    input_grad = (dresid + dinput_norm).astype(jnp.bfloat16).reshape(tokens.shape)
    down_bias_grad = jnp.sum(grad_full, axis=0)
    shares = (
        lax.psum_scatter(
            qkv_weight_grad.astype(jnp.bfloat16), "fsdp", scatter_dimension=0, tiled=True
        ).astype(jnp.float32),
        lax.psum_scatter(
            out_weight_grad.astype(jnp.bfloat16), "fsdp", scatter_dimension=0, tiled=True
        ).astype(jnp.float32),
        lax.psum_scatter(
            qkv_bias_grad.astype(jnp.bfloat16), "fsdp", scatter_dimension=0, tiled=True
        ).astype(jnp.float32),
        lax.psum_scatter(
            out_bias_grad.astype(jnp.bfloat16), "fsdp", scatter_dimension=0, tiled=True
        ).astype(jnp.float32),
        lax.psum_scatter(
            gain_one_grad.astype(jnp.bfloat16), "fsdp", scatter_dimension=0, tiled=True
        ).astype(jnp.float32),
        lax.psum_scatter(
            shift_one_grad.astype(jnp.bfloat16), "fsdp", scatter_dimension=0, tiled=True
        ).astype(jnp.float32),
        lax.psum_scatter(
            gain_two_grad.astype(jnp.bfloat16), "fsdp", scatter_dimension=0, tiled=True
        ).astype(jnp.float32),
        lax.psum_scatter(
            shift_two_grad.astype(jnp.bfloat16), "fsdp", scatter_dimension=0, tiled=True
        ).astype(jnp.float32),
        lax.psum_scatter(
            up_bias_term.astype(jnp.bfloat16), "fsdp", scatter_dimension=0, tiled=True
        ).astype(jnp.float32),
        lax.psum_scatter(
            down_bias_grad.astype(jnp.bfloat16), "fsdp", scatter_dimension=0, tiled=True
        ).astype(jnp.float32),
    )
    totals = (
        lax.psum(shares[0].astype(jnp.bfloat16), "ctx").astype(jnp.float32),
        lax.psum(shares[1].astype(jnp.bfloat16), "ctx").astype(jnp.float32),
        lax.psum(up_rows_grad.astype(jnp.bfloat16), "ctx").astype(jnp.float32),
        lax.psum(down_rows_grad.astype(jnp.bfloat16), "ctx").astype(jnp.float32),
        lax.psum(shares[2].astype(jnp.bfloat16), "ctx").astype(jnp.float32),
        lax.psum(shares[3].astype(jnp.bfloat16), "ctx").astype(jnp.float32),
        lax.psum(shares[4].astype(jnp.bfloat16), "ctx").astype(jnp.float32),
        lax.psum(shares[5].astype(jnp.bfloat16), "ctx").astype(jnp.float32),
        lax.psum(shares[6].astype(jnp.bfloat16), "ctx").astype(jnp.float32),
        lax.psum(shares[7].astype(jnp.bfloat16), "ctx").astype(jnp.float32),
        lax.psum(shares[8].astype(jnp.bfloat16), "ctx").astype(jnp.float32),
        lax.psum(shares[9].astype(jnp.bfloat16), "ctx").astype(jnp.float32),
    )
    return (
        layer_out.astype(jnp.bfloat16).reshape(tokens.shape),
        input_grad,
        totals[6],
        totals[7],
        totals[0],
        totals[4],
        totals[1],
        totals[5],
        totals[8],
        totals[9],
        totals[2],
        totals[10],
        totals[3],
        totals[11],
    )

F32 = jnp.float32
BF16 = jnp.bfloat16
LOG2E = 1.4426950408889634
LN2 = 0.6931471805599453
TILE = 256
DOC_LANES = 48
BACKWARD_ENDS = {j: (3, 7) if j < 3 else (7,) for j in range(8)}
GELU_A = 0.7978845608028654
GELU_B = 0.044715


def dot_nt(a, b):
    return lax.dot_general(a, b, (((1,), (1,)), ((), ())), preferred_element_type=F32)


def dot_nn(a, b):
    return lax.dot_general(a, b, (((1,), (0,)), ((), ())), preferred_element_type=F32)


def dot_tn(a, b):
    return lax.dot_general(a, b, (((0,), (0,)), ((), ())), preferred_element_type=F32)


def kernel_call(body, outs, ins, scratch=(), scalars=1, tied=(), spare=7, cost=0):
    groups = [x if isinstance(x, tuple) else (x,) for x in ins[scalars:]]
    flat = [x for group in groups for x in group]
    joined = [
        pltpu.VMEM((sum(x.shape[0] for x in group), *group[0].shape[1:]), group[0].dtype)
        for group in groups
        if len(group) > 1
    ]
    scratch = [*joined, *scratch]
    room = sum(int(np.prod(x.shape)) * jnp.dtype(x.dtype).itemsize for x in scratch)

    def run(*refs):
        numbers, refs = refs[:scalars], refs[scalars:]
        sources, refs = refs[: len(flat)], refs[len(flat) + len(tied) :]
        targets, refs = refs[: len(outs)], refs[len(outs) :]
        places, refs = list(refs[: len(joined)]), refs[len(joined) :]
        held, at = [], 0
        for group in groups:
            if len(group) == 1:
                held.append(sources[at])
            else:
                held.append(places.pop(0))
                row = 0
                for source in sources[at : at + len(group)]:
                    held[-1][row : row + source.shape[0], :] = source[...]
                    row += source.shape[0]
            at += len(group)
        body(*numbers, *held, *targets, *refs)

    vmem = pl.BlockSpec(memory_space=pltpu.VMEM)
    return pl.pallas_call(
        run,
        out_shape=list(outs),
        in_specs=[pl.BlockSpec(memory_space=pltpu.SMEM)] * scalars
        + [vmem] * len(flat)
        + [pl.BlockSpec(memory_space=pl.ANY)] * len(tied),
        out_specs=[vmem] * len(outs),
        scratch_shapes=scratch,
        compiler_params=pltpu.CompilerParams(vmem_limit_bytes=room + spare * 1024 * 1024),
        cost_estimate=pl.CostEstimate(
            flops=int(cost * 1e9), bytes_accessed=0, transcendentals=0
        ),
    )(*ins[:scalars], *flat, *tied)


def shaped(shape, dtype):
    return jax.ShapeDtypeStruct(shape, dtype)


def lanes_of(shape):
    return lax.broadcasted_iota(jnp.int32, shape, len(shape) - 1)


def three_pieces(v):
    high = v.astype(BF16).astype(F32)
    mid = (v - high).astype(BF16).astype(F32)
    return high, mid, v - high - mid


def normed(v):
    mean = jnp.mean(v, axis=-1, keepdims=True)
    centered = v - mean
    spread = jnp.mean(centered * centered, axis=-1, keepdims=True)
    root = lax.rsqrt(spread + EPS)
    return centered * root, root


def norm_back(dout, unit, root, gain):
    dn = dout * gain
    first = jnp.mean(dn, axis=-1, keepdims=True)
    second = jnp.mean(dn * unit, axis=-1, keepdims=True)
    return root * (dn - first - unit * second)


def block_rows(index, half_block):
    return pl.ds(pl.multiple_of(index * half_block, half_block), half_block)


def prepare_kernel(ids, *refs):
    own, w_ref, out_ref, up_ref, down_ref = refs[0:5]
    vectors, (chunk, pack, piece), places, sems = refs[5:14], refs[14:17], refs[17:31], refs[31]
    c = ids[0]

    def rows(ref, start, count):
        return ref.at[pl.ds(pl.multiple_of(start * count, count), count)]

    sources = [
        own,
        rows(w_ref, ids[5], 128),
        rows(out_ref, c, 32),
        rows(up_ref, c, 128),
        rows(down_ref, c, 128),
        *vectors,
    ]
    copies = [
        pltpu.make_async_copy(a, b, sems.at[i]) for i, (a, b) in enumerate(zip(sources, places))
    ]
    for copy in copies:
        copy.start()
    for copy in copies:
        copy.wait()
    doc, g1, s1, ob, g2, s2, db, qb, ub = places[5:]
    docs = doc[...].astype(F32)
    row = jnp.concatenate([docs[0:1], docs[1:2]], axis=1)
    chunk[256:272, :] = jnp.zeros((16, 1024), BF16)
    chunk[256:272, 0:256] = jnp.broadcast_to(row, (16, 256)).astype(BF16)

    def wide(ref):
        size = ref.shape[0]
        return jnp.broadcast_to(ref[...].astype(F32).reshape(1, size), (8, size))

    first = jnp.concatenate([wide(r) for r in (g1, s1, ob, g2)], axis=1)
    at = lax.broadcasted_iota(jnp.int32, (8, 1024), 0)
    first = jnp.where(at < 4, first, wide(ub))
    second = jnp.concatenate([wide(r) for r in (s2, db, qb)], axis=1)
    small = jnp.concatenate([first, second], axis=0).astype(BF16)
    chunk[0:256, :] = places[0][...]
    pack[0:128, :] = places[1][...]
    pack[128:144, :] = small
    pack[144:176, :] = places[2][...]
    piece[0:128, :] = places[3][...]
    piece[128:256, :] = places[4][...]


def project_kernel(ids, slopes, *refs):
    chunks, packs = refs[:8], refs[8:12]
    q_out, k_out, v_out, w_out, par_out, doc_out, h_out, out_rows, small = refs[12:]
    c, f = ids[0], ids[1]
    for k in range(4):
        plane = lax.rem(f + (4 - k), 4)
        small[plane] = packs[k][128:144, :].astype(F32)
        at = pl.multiple_of(plane * 32, 32)
        out_rows[pl.ds(at, 32), :] = packs[k][144:176, :]
        for kind in range(3):

            @pl.when(ids[2 + kind] == plane)
            def _():
                w_out[kind * 128 : (kind + 1) * 128, :] = packs[k][0:128, :]

    rows = [small[p] for p in range(4)]

    def whole(row, start, stop, planes=(0, 1, 2, 3)):
        return jnp.concatenate([rows[p][row * 8 : row * 8 + 1, start:stop] for p in planes], axis=1)

    par_out[0:1, :] = whole(0, 0, 256)
    par_out[1:2, :] = whole(0, 256, 512)
    par_out[2:3, :] = whole(0, 512, 768)
    par_out[3:4, :] = whole(0, 768, 1024)
    par_out[4:5, :] = whole(1, 0, 256)
    par_out[5:6, :] = whole(1, 256, 512)
    par_out[6:7, :] = whole(1, 512, 1024, (0, 1))
    par_out[7:8, :] = whole(1, 512, 1024, (2, 3))
    par_out[8:16, :] = small[f ^ 2][0:8, :]
    par_out[8:9, :] = small[f ^ 2][4:5, :]
    mine = pl.ds(pl.multiple_of(c * 128, 128), 128)
    bias_q = par_out[6:7, mine]
    bias_v = par_out[7:8, mine]
    gain, shift = par_out[0:1, :], par_out[1:2, :]
    weight = w_out[...]
    lane = lanes_of((256, 128))
    row = lax.broadcasted_iota(jnp.int32, (256, 128), 0)
    eye = (
        lax.broadcasted_iota(jnp.int32, (128, 128), 0) == lanes_of((128, 128))
    ).astype(BF16)
    sub = lax.broadcasted_iota(jnp.int32, (128, 256), 0).astype(F32) - 67.0
    is_doc = (lane >= 67) & (lane < 67 + DOC_LANES)
    low = lane < 64
    for d in range(8):
        cc = c ^ d
        h = (normed(chunks[d][0:256, :].astype(F32))[0] * gain + shift).astype(BF16)
        h_out[d % 2, d // 2] = h
        joined = dot_nt(h, weight)
        query = (joined[:, 0:128] + bias_q) * (LOG2E * 0.125)
        keys = joined[:, 128:256]
        values = joined[:, 256:384] + bias_v
        doc_row = chunks[d][256:272, 0:256].astype(F32)[0:1, :]
        doc_out[pl.ds(cc, 1), :] = doc_row[:, 0:128]
        doc_out[pl.ds(8 + cc, 1), :] = doc_row[:, 128:256]
        one_hot = dot_tn((sub == doc_row).astype(BF16), eye)
        pos = jnp.where(row < 128, cc * 128 + row, 2175 - cc * 128 - row).astype(F32)
        q_aug = jnp.where(lane < 67, 1.0, jnp.where(is_doc, one_hot, 0.0))
        k_tail = jnp.where(is_doc, (1.0 - one_hot) * MASKED, jnp.where(lane < 118, 1.0, 0.0))
        for hh in range(2):
            if hh == 1:
                query, keys, values = (pltpu.roll(t, 64, 1) for t in (query, keys, values))
            high, mid, rest = three_pieces(pos * (slopes[2 * c + hh] * LOG2E))
            k_aug = jnp.where(
                lane == 64, high, jnp.where(lane == 65, mid, jnp.where(lane == 66, rest, k_tail))
            )
            parts = (
                (q_out, jnp.where(low, query, q_aug).astype(BF16)),
                (k_out, jnp.where(low, keys, k_aug).astype(BF16)),
                (v_out, jnp.where(low, values, 1.0).astype(BF16)),
            )
            for ref, value in parts:
                ref[hh, block_rows(cc, 128), :] = value[0:128]
                ref[hh, block_rows(8 + cc, 128), :] = value[128:256]


def tile_start(i):
    return i * TILE if i < 4 else 1024 + (7 - i) * TILE


def tile_rows(i):
    start = jnp.where(i < 4, i * TILE, 1024 + (7 - i) * TILE)
    return pl.ds(pl.multiple_of(start, TILE), TILE)


def tile_docs(docs, i):
    at = tile_start(i) // 128
    return docs[at : at + 2, :]


def count_tiles(flags):
    total = jnp.sum(jnp.where(flags, 1.0, 0.0)).astype(jnp.int32)
    return lax.shift_right_logical(total, 8)


def span(first, last):
    out = []
    if first < 4 and first <= last:
        out.append(slice(first * TILE, (min(last, 3) + 1) * TILE))
    if last >= 4 and first <= last:
        out.append(slice(tile_start(last), tile_start(max(first, 4)) + TILE))
    return out


def attend_kernel(
    ids, docs_ref, q_ref, k_ref, v_ref, q_out, full_out, m0, m1, m2, m3, mixed_out, held
):
    docs = docs_ref[...]
    lane = lanes_of((TILE, 128))
    low = lane < 64
    step_right = lanes_of((TILE, TILE)) - lax.broadcasted_iota(jnp.int32, (TILE, TILE), 0)

    def widest(scores):
        return jnp.maximum(scores[:, 0:128], scores[:, 128:256])

    def one_tile(i, carry):
        own = tile_rows(i)
        at = jnp.where(i < 4, 2 * i, 8 + 2 * (7 - i))
        first = count_tiles(docs < jnp.min(docs_ref[pl.ds(at, 2), :]))
        allowed = jnp.where(i < 4, step_right, -step_right) <= 0
        queries = [q_ref[hh, own, :] for hh in range(2)]
        diagonal = [
            jnp.where(allowed, dot_nt(queries[hh], k_ref[hh, own, :]), MASKED) for hh in range(2)
        ]

        def look(j, tops):
            rows = tile_rows(j)
            out = []
            for hh in range(2):
                scores = dot_nt(queries[hh], k_ref[hh, rows, :])
                held[hh, j] = scores
                out.append(jnp.maximum(tops[hh], widest(scores)))
            return tuple(out)

        tops = lax.fori_loop(first, i, look, tuple(widest(s) for s in diagonal))
        tops = [jnp.max(t, axis=1, keepdims=True) for t in tops]

        def gather(j, sums):
            rows = tile_rows(j)
            out = []
            for hh in range(2):
                weights = jnp.exp2(held[hh, j] - tops[hh]).astype(BF16)
                out.append(sums[hh] + dot_nn(weights, v_ref[hh, rows, :]))
            return tuple(out)

        start = tuple(
            dot_nn(jnp.exp2(diagonal[hh] - tops[hh]).astype(BF16), v_ref[hh, own, :])
            for hh in range(2)
        )
        sums = lax.fori_loop(first, i, gather, start)
        outs = []
        for hh in range(2):
            total = sums[hh][:, 64:65]
            outs.append(sums[hh] / total)
            high, mid, rest = three_pieces(-(tops[hh] + jnp.log2(total)))
            tail = jnp.where(
                lane == 115,
                high,
                jnp.where(lane == 116, mid, jnp.where(lane == 117, rest, queries[hh].astype(F32))),
            )
            q_out[hh, own, :] = tail.astype(BF16)
        both = jnp.where(low, outs[0], pltpu.roll(outs[1], 64, 1))
        full_out[own, :] = both
        half = jnp.where(i < 4, 0, 128)
        chunk = jnp.where(i < 4, 2 * i, 2 * (7 - i))
        for piece in range(2):
            mixed_out[chunk + piece, pl.ds(pl.multiple_of(half, 128), 128), :] = both[
                piece * 128 : (piece + 1) * 128
            ].astype(BF16)
        return carry

    lax.fori_loop(0, 8, one_tile, 0)
    for e, ref in enumerate((m0, m1, m2, m3)):
        for parity in range(2):
            ref[parity * 256 : (parity + 1) * 256, :] = mixed_out[ids[0] ^ (2 * e + parity)]


def heads_far_kernel(g0, g1, g2, g3, out):
    for e, ref in enumerate((g0, g1, g2, g3)):
        out[e] = ref[256:512, :]


def attend_back_kernel(
    ids, docs_ref, q_ref, k_ref, v_ref, full_ref, g0, g1, g2, g3, g_far, keep, send, grads, dq, dk, dv, all_grads
):
    docs = docs_ref[...]
    lane = lanes_of((256, 128))
    low = lane < 64
    for e, ref in enumerate((g0, g1, g2, g3)):
        all_grads[ids[0] ^ (2 * e)] = ref[0:256, :]
        all_grads[ids[0] ^ (2 * e + 1)] = g_far[e]
    for at in range(8):
        piece = all_grads[at].astype(F32)
        other = jnp.concatenate(
            [
                full_ref[at * 128 : (at + 1) * 128, :],
                full_ref[1024 + at * 128 : 1024 + (at + 1) * 128, :],
            ],
            axis=0,
        )
        product = piece * other
        for hh in range(2):
            delta = jnp.sum(jnp.where(low == (hh == 0), product, 0.0), axis=1, keepdims=True)
            high, mid, rest = three_pieces(-delta)
            tail = jnp.where(
                lane == 64, high, jnp.where(lane == 65, mid, jnp.where(lane == 66, rest, 0.0))
            )
            moved = piece if hh == 0 else pltpu.roll(piece, 64, 1)
            value = jnp.where(low, moved, tail).astype(BF16)
            grads[hh, at * 128 : (at + 1) * 128, :] = value[0:128]
            grads[hh, 1024 + at * 128 : 1024 + (at + 1) * 128, :] = value[128:256]
    dq[...] = jnp.zeros_like(dq)
    down, right = lax.broadcasted_iota(jnp.int32, (TILE, TILE), 0), lanes_of((TILE, TILE))

    def run(j, last):
        own = slice(tile_start(j), tile_start(j) + TILE)
        allowed = (down <= right) if j < 4 else (down >= right)
        places = [own] + span(j + 1, last)

        def head(hh, carry):
            keys, values = k_ref[hh, own, :], v_ref[hh, own, :]
            dk_sum = dv_sum = 0.0
            for at, rows in enumerate(places):
                query, grad = q_ref[hh, rows, :], grads[hh, rows, :]
                probs = jnp.exp2(dot_nt(keys, query))
                if at == 0:
                    probs = jnp.where(allowed, probs, 0.0)
                dscores = (probs * dot_nt(values, grad)).astype(BF16)
                dq[hh, rows, :] += dot_tn(dscores, keys)
                dk_sum += dot_nn(dscores, query)
                dv_sum += dot_nn(probs.astype(BF16), grad)
            dk[hh, own, :] = dk_sum
            dv[hh, own, :] = dv_sum
            return carry

        lax.fori_loop(0, 2, head, 0)

    for j in range(8):
        ends = BACKWARD_ENDS[j]
        within = jnp.sum(jnp.where(docs <= jnp.max(tile_docs(docs, j)), 1.0, 0.0))
        last = lax.shift_right_logical(within.astype(jnp.int32) + (TILE - 1), 8) - 1
        for at, end in enumerate(ends):
            fits = last <= end
            if at:
                fits = fits & (last > ends[at - 1])
            if len(ends) == 1:
                run(j, end)
            else:
                pl.when(fits)(functools.partial(run, j, end))
    for j in range(4):
        for parity, ref in enumerate((keep, send)):
            cc = ids[0] ^ (2 * j + parity)
            for half in range(2):
                rows = block_rows(8 * half + cc, 128)
                at = slice(half * 128, (half + 1) * 128)
                for which, (held, scale) in enumerate(((dq, 0.125), (dk, LN2), (dv, 1.0))):
                    other = pltpu.roll(held[1, rows, :], 64, 1)
                    both = jnp.where(low[0:128], held[0, rows, :], other) * scale
                    ref[j, at, which * 128 : (which + 1) * 128] = both.astype(BF16)


def branch_kernel(ids, chunk, g0, g1, g2, g3, g_far, par, *refs):
    pieces, (w_out, mixed_out, resid_out, h_out) = refs[:8], refs[8:]
    for d in range(8):
        for plane in range(4):
            at = pl.multiple_of(plane * 256 + (ids[0] ^ d) * 32, 32)
            w_out[pl.ds(at, 32), :] = pieces[d][plane * 32 : (plane + 1) * 32, :]
    for e, ref in enumerate((g0, g1, g2, g3)):
        for parity, value in enumerate((ref[0:256, :], g_far[e])):
            at = pl.multiple_of((ids[0] ^ (2 * e + parity)) * 128, 128)
            mixed_out[:, pl.ds(at, 128)] = value
    resid = chunk[0:256, :].astype(F32) + dot_nt(mixed_out[...], w_out[...]) + par[2:3, :]
    resid_out[...] = resid
    h_out[...] = (normed(resid)[0] * par[3:4, :] + par[4:5, :]).astype(BF16)


def feed_step(h, cot, up_w, down_w, bias):
    u = dot_nt(h, up_w) + bias
    grad = dot_nt(cot, down_w)
    square = u * u
    th = jnp.tanh(GELU_A * u * (1.0 + GELU_B * square))
    half = 0.5 * (1.0 + th)
    act = (u * half).astype(BF16)
    slope = half + 0.5 * u * (1.0 - th * th) * (GELU_A * (1.0 + 3.0 * GELU_B * square))
    return act, (grad * slope).astype(BF16)


def feed_kernel(h_ref, cot_ref, up_ref, bias_ref, down_ref, act_out, dup_out, acc, dacc):
    acc[...] = jnp.zeros_like(acc)
    dacc[...] = jnp.zeros_like(dacc)

    def step(t, carry):
        at = pl.ds(pl.multiple_of(t * 256, 256), 256)
        up_w, down_w = up_ref[at, :], down_ref[at, :]
        act, dup = feed_step(h_ref[...], cot_ref[...], up_w, down_w, bias_ref[0:1, at])
        act_out[:, at] = act
        dup_out[:, at] = dup
        acc[...] += dot_nn(act, down_w)
        dacc[...] += dot_nn(dup, up_w)
        return carry

    lax.fori_loop(0, 4, step, 0)


def feed_other_kernel(ids, h_ref, cot_ref, par, acc_in, dacc_in, *refs):
    pieces, (act_out, dup_out, branch, dh, acc, dacc, ups, downs, bias) = refs[:8], refs[8:]
    for d in range(8):
        at = slice(d * 128, (d + 1) * 128)
        ups[at, :] = pieces[d][0:128, :]
        downs[at, :] = pieces[d][128:256, :]
        bias[0:1, at] = par[8:9, pl.ds(pl.multiple_of((ids[0] ^ d) * 128, 128), 128)]
    acc[...] = acc_in[...]
    dacc[...] = dacc_in[...]

    def step(t, carry):
        at = pl.ds(pl.multiple_of(t * 256, 256), 256)
        up_w, down_w = ups[at, :], downs[at, :]
        act, dup = feed_step(h_ref[...], cot_ref[...], up_w, down_w, bias[0:1, at])
        act_out[:, at] = act
        dup_out[:, at] = dup
        acc[...] += dot_nn(act, down_w)
        dacc[...] += dot_nn(dup, up_w)
        return carry

    lax.fori_loop(0, 4, step, 0)
    branch[...] = acc[...].astype(BF16)
    dh[...] = dacc[...].astype(BF16)


def middle_kernel(
    ids, d0, d1, resid_ref, cot_ref, par, w_ref, dresid_out, dbranch_out, m0, m1, m2, m3, sums, held
):
    dh = d0[...].astype(F32) + d1[...].astype(F32)
    unit, root = normed(resid_ref[...])
    cot = cot_ref[...].astype(F32)
    dresid = cot + norm_back(dh, unit, root, par[3:4, :])
    dresid_out[...] = dresid
    dbranch = dresid.astype(BF16)
    dbranch_out[...] = dbranch
    held[...] = dot_nn(dbranch, w_ref[...]).astype(BF16)
    for e, ref in enumerate((m0, m1, m2, m3)):
        for parity in range(2):
            at = pl.multiple_of((ids[0] ^ (2 * e + parity)) * 128, 128)
            ref[parity * 256 : (parity + 1) * 256, :] = held[:, pl.ds(at, 128)]
    sums[...] = jnp.zeros_like(sums)
    sums[0:1, :] = jnp.sum(dbranch.astype(F32), axis=0, keepdims=True)
    sums[1:2, :] = jnp.sum(dh * unit, axis=0, keepdims=True)
    sums[2:3, :] = jnp.sum(dh, axis=0, keepdims=True)
    sums[3:4, :] = jnp.sum(cot, axis=0, keepdims=True)


def feed_weights_kernel(ids, *refs):
    hs, cots, dups, acts, dups_far, acts_far = (refs[2 * i : 2 * i + 2] for i in range(6))
    keep, send, bias, all_rows = refs[12:]
    c = ids[0]

    def product(lefts, at, rights):
        return sum(dot_tn(a[:, at], b[...]) for a, b in zip(lefts, rights)).astype(BF16)

    for t in range(4):
        at = slice(t * 256, (t + 1) * 256)
        for which, (lefts, rights) in enumerate(((dups, hs), (acts, cots))):
            all_rows[which, at, :] = product(lefts, at, rights)
        for which, (lefts, rights) in enumerate(((dups_far, hs), (acts_far, cots))):
            both = product(lefts, at, rights)
            for parity, ref in enumerate((keep, send)):
                place = slice(256 + which * 128, 384 + which * 128)
                ref[t, place, :] = both[parity * 128 : (parity + 1) * 128]
    for e in range(4):
        for parity, ref in enumerate((keep, send)):
            rows = block_rows(c ^ (2 * e + parity), 128)
            ref[e, 0:128, :] = all_rows[0, rows, :]
            ref[e, 128:256, :] = all_rows[1, rows, :]

    def total(refs):
        return sum(jnp.sum(r[...].astype(F32), axis=0, keepdims=True) for r in refs)

    bias[0:1, :] = total(dups)
    far = total(dups_far)
    for d in range(8):
        at = pl.ds(pl.multiple_of((c ^ d) * 128, 128), 128)
        bias[8:9, at] = far[:, d * 128 : (d + 1) * 128]


def out_weights_kernel(ids, dbranch, mixed, keep, send, total):
    for t in range(4):
        at = slice(t * 256, (t + 1) * 256)
        total[at, :] = dot_tn(dbranch[:, at], mixed[...]).astype(BF16)
    for e in range(4):
        for parity, ref in enumerate((keep, send)):
            cc = ids[0] ^ (2 * e + parity)
            for plane in range(4):
                at = pl.multiple_of(plane * 256 + cc * 32, 32)
                ref[e, plane * 32 : (plane + 1) * 32, :] = total[pl.ds(at, 32), :]


def added(*values):
    return sum(v.astype(F32) for v in values).astype(BF16)


def pair_sum_kernel(keep, got, out_keep, out_got, x_out, y_out, own_out):
    def put(target, slot, e, part):
        rows = slice(256 * part, 256 * (part + 1))
        more = slice(64 * part, 64 * (part + 1))
        at = slot * 320
        target[at : at + 256, :] = added(keep[e, rows], got[e, rows])
        target[at + 256 : at + 320, :] = added(out_keep[e, more], out_got[e, more])

    put(x_out, 0, 1, 0)
    put(x_out, 1, 3, 0)
    put(y_out, 0, 2, 1)
    put(y_out, 1, 3, 1)
    put(own_out, 0, 0, 0)
    put(own_out, 1, 0, 1)
    put(own_out, 2, 2, 0)
    put(own_out, 3, 1, 1)


def relay_kernel(own, from_x, from_y, kept, x_out, y_out):
    half = own.shape[0] // 4
    kept[0:half, :] = added(own[0:half, :], from_x[0:half, :])
    y_out[...] = added(own[2 * half : 3 * half, :], from_x[half:, :])
    kept[half:, :] = added(own[half : 2 * half, :], from_y[0:half, :])
    x_out[...] = added(own[3 * half :, :], from_y[half:, :])


def owned_kernel(ids, kept, from_y, from_x, near, far, out_next, out_last, share):
    f = ids[1]
    near[0:256, :] = added(kept[0:256, :], from_y[0:256, :])
    far[0:256, :] = added(kept[320:576, :], from_x[0:256, :])
    share[0:64, :] = added(kept[256:320, :], from_y[256:320, :])
    share[64:128, :] = added(kept[576:640, :], from_x[256:320, :])
    for k, target in enumerate((near, out_next, far, out_last)):
        rows = pl.ds(pl.multiple_of(lax.rem(f + k, 4) * 32, 32), 32)
        if k % 2:
            target[...] = share[rows, :]
        else:
            target[256:288, :] = share[rows, :]


def feed_sum_kernel(near, far, out_next, out_last, out):
    out[0:256, :] = added(near[0:256, :], far[0:256, :])
    outs = (near[256:288, :], far[256:288, :], out_next[...], out_last[...])
    out[256:288, :] = added(*outs)


def slots_kernel(kept, got, near, far):
    near[...] = added(kept[0:144, :], got[0:144, :])
    far[...] = added(kept[144:288, :], got[144:288, :])


def sum_kernel(*refs):
    refs[-1][...] = added(*(r[...] for r in refs[:-1]))


def layer_out_kernel(resid, par, one, two, out):
    out[...] = (resid[...] + par[5:6, :] + one[...].astype(F32) + two[...].astype(F32)).astype(BF16)


def head_weights_kernel(keep, send, h_ref, total):
    for parity, ref in enumerate((keep, send)):
        for j in range(4):
            got = dot_tn(ref[j], h_ref[parity, j])
            if parity == 0 and j == 0:
                total[...] = got
            else:
                total[...] += got


def unproject_kernel(ids, *refs):
    chunks, (near, far, bias_far, w_near, w_far, par, sums, up_sums, wsum) = refs[:4], refs[4:13]
    x_out, y_out, own_out, slots_kept, slots_sent, slots, small = refs[13:]
    c, f = ids[0], ids[1]
    near_w, far_w = w_near[...], w_far[...]
    gain_grad = shift_grad = bias_grad = 0.0
    places = (
        (own_out, 0, own_out, 128),
        (x_out, 0, own_out, 384),
        (own_out, 256, y_out, 0),
        (x_out, 128, y_out, 128),
    )
    for e, chunk in enumerate(chunks):
        grads = near[e]
        unit = normed(chunk[0:256, :].astype(F32))[0]
        share = dot_nn(grads, near_w) + dot_nn(far[e], far_w)
        top, at, bottom, below = places[e]
        top[at : at + 128, :] = share[0:128].astype(BF16)
        bottom[below : below + 128, :] = share[128:256].astype(BF16)
        gain_grad += jnp.sum(share * unit, axis=0, keepdims=True)
        shift_grad += jnp.sum(share, axis=0, keepdims=True)
        bias_grad += jnp.sum(grads.astype(F32) + bias_far[e].astype(F32), axis=0, keepdims=True)
    small[...] = jnp.zeros_like(small)
    for p in range(4):
        at = slice(p * 256, (p + 1) * 256)
        small[p, 0:1, 0:256] = gain_grad[:, at]
        small[p, 0:1, 256:512] = shift_grad[:, at]
        small[p, 0:1, 512:768] = sums[0:1, at]
        small[p, 0:1, 768:1024] = sums[1:2, at]
        small[p, 1:2, 0:256] = sums[2:3, at]
        small[p, 1:2, 256:512] = sums[3:4, at]
        small[p, 1:2, 512:640] = bias_grad[:, 0:128] if p < 2 else bias_grad[:, 256:384]
        up_far = jnp.where(f == p ^ 2, up_sums[8:9, :], 0.0)
        small[p, 2:3, :] = jnp.where(f == p, up_sums[0:1, :], up_far)
        start = pl.multiple_of(ids[6 + p] * 128, 128)
        slots[p, 0:128, :] = wsum[pl.ds(start, 128), :].astype(BF16)
        slots[p, 128:144, :] = small[p].astype(BF16)
    for k in range(2):
        at = slice(k * 144, (k + 1) * 144)
        slots_kept[at, :] = slots[f ^ (2 * k)]
        slots_sent[at, :] = slots[f ^ (2 * k + 1)]


def input_kernel(kept, from_y, from_x, chunk, par, dresid, out):
    moved = jnp.concatenate([from_y[...], from_x[...]], axis=0)
    dh = kept[...].astype(F32) + moved.astype(F32)
    unit, root = normed(chunk[0:256, :].astype(F32))
    out[...] = (dresid[...] + norm_back(dh, unit, root, par[0:1, :])).astype(BF16)


def feed_grads_kernel(ids, *refs):
    pieces, (up_out, down_out, out_out, place, sems) = refs[:10], refs[10:]
    heads, tails = pieces[:6], (pieces[6:8], pieces[8:10])
    copies = []
    for d in range(8):
        cc = ids[0] ^ d
        if d < 6:
            place[d] = heads[d][...].astype(F32)
        else:
            place[d, 0:144] = tails[d - 6][0][...].astype(F32)
            place[d, 144:288] = tails[d - 6][1][...].astype(F32)
        moves = (
            (place.at[d, 0:128], up_out.at[block_rows(cc, 128)]),
            (place.at[d, 128:256], down_out.at[block_rows(cc, 128)]),
            (place.at[d, 256:288], out_out.at[pl.ds(pl.multiple_of(cc * 32, 32), 32)]),
        )
        for i, (a, b) in enumerate(moves):
            copies.append(pltpu.make_async_copy(a, b, sems.at[3 * d + i]))
            copies[-1].start()
    for copy in copies:
        copy.wait()


def last_grads_kernel(ids, *refs):
    pieces, (qkv_out, g1, s1, ob, g2, s2, db, ub, bias_out) = refs[:8], refs[8:]
    c, f = ids[0], ids[1]
    total = 0.0
    for d in range(8):
        cc = c ^ d
        place = lax.rem(cc + 24 - 6 * f, 8)

        @pl.when(place < 6)
        def _():
            qkv_out[block_rows(place, 128), :] = pieces[d][0:128, :].astype(F32)

        rows = pieces[d][128:144, :].astype(F32)
        total += rows

        @pl.when(lax.div(cc, 4) == lax.rem(f, 2))
        def _():
            at = pl.multiple_of(lax.rem(cc, 4) * 128, 128)
            bias_out[0:1, pl.ds(at, 128)] = rows[1:2, 512:640]

    for ref, row, start in ((g1, 0, 0), (s1, 0, 256), (ob, 0, 512), (g2, 0, 768), (s2, 1, 0), (db, 1, 256)):
        ref[...] = total[row : row + 1, start : start + 256]
    ub[...] = total[2:3, :]


def per_device(
    tokens,
    doc_ids,
    alibi_slopes,
    ln1_gain,
    ln1_shift,
    qkv_weight,
    qkv_bias,
    out_weight,
    out_bias,
    ln2_gain,
    ln2_shift,
    up_weight,
    up_bias,
    down_weight,
    down_bias,
    cotangent,
):
    c, f = lax.axis_index("ctx"), lax.axis_index("fsdp")
    width = 1024

    def swap(v, d):
        return lax.ppermute(v, "ctx", [(i, i ^ d) for i in range(8)])

    def shift(v, k):
        return lax.ppermute(v, "fsdp", [(i, (i + k) % 4) for i in range(4)])

    def pair(v):
        return lax.ppermute(v, "fsdp", [(i, i ^ 1) for i in range(4)])

    def after(value, *earlier):
        return lax.optimization_barrier((value, earlier))[0]

    def spread(v):
        near = [v] + [swap(v, d) for d in (2, 4, 6)]
        return [t for e in near for t in (e, swap(e, 1))]

    def spread_relayed(v, cut, *earlier):
        from_x, from_y = swap(v, 2), swap(v, 4)
        top, bottom = swap(from_x[:cut], 4), swap(from_y[cut:], 2)
        first = (v, from_x, from_y)
        pairs = [(p, swap(q, 1)) for p, q in zip(first, after(first, top, bottom))]
        later = (top, bottom)
        pairs += [(p, swap(q, 1)) for p, q in zip(later, after(later, *earlier))]
        last = [(pairs[3][side], pairs[4][side]) for side in range(2)]
        return [t for p in pairs[:3] for t in p] + last

    table = np.zeros((32, 16), np.int32)
    for ci in range(8):
        for fi in range(4):
            at = ci * 4 + fi
            table[at, 0:2] = ci, fi
            planes = [(8 * kind + ci) // 6 for kind in range(3)]
            table[at, 2:5] = planes
            for kind in range(3):
                if planes[kind] == fi:
                    table[at, 5] = (8 * kind + ci) % 6
            for k in range(4):
                if k in planes:
                    table[at, 6 + k] = planes.index(k)
    ids = lax.dynamic_index_in_dim(jnp.asarray(table), c * 4 + f, 0, keepdims=False)

    own = tokens.reshape(256, width)
    cot = cotangent.reshape(256, width)
    vectors_in = [ln1_gain, ln1_shift, out_bias, ln2_gain, ln2_shift, down_bias, qkv_bias, up_bias]
    vectors_in = [doc_ids.reshape(2, 128)] + vectors_in
    hbm = pl.BlockSpec(memory_space=pltpu.HBM)
    outs = [shaped((272, width), BF16), shaped((176, width), BF16), shaped((256, width), BF16)]
    sizes = [(size, width) for size in (256, 128, 32, 128, 128)]
    chunk, pack, piece = pl.pallas_call(
        prepare_kernel,
        out_shape=outs,
        in_specs=[pl.BlockSpec(memory_space=pltpu.SMEM)] + [hbm] * 14,
        out_specs=[pl.BlockSpec(memory_space=pltpu.VMEM)] * 3,
        scratch_shapes=[pltpu.VMEM(size, BF16) for size in sizes]
        + [pltpu.VMEM(x.shape, x.dtype) for x in vectors_in]
        + [pltpu.SemaphoreType.DMA((14,))],
        compiler_params=pltpu.CompilerParams(vmem_limit_bytes=58 * 1024 * 1024),
        cost_estimate=pl.CostEstimate(flops=0, bytes_accessed=0, transcendentals=0),
    )(ids, own, qkv_weight, out_weight, up_weight, down_weight, *vectors_in)
    packs = [pack] + [shift(pack, k) for k in (1, 2, 3)]
    chunks = spread_relayed(chunk, 128, *packs)

    heads = shaped((2, 2048, 128), BF16)
    q_one, keys, values, w_heads, par, docs, h_one, out_rows = kernel_call(
        project_kernel,
        [
            heads,
            heads,
            heads,
            shaped((384, width), BF16),
            shaped((16, width), F32),
            shaped((16, 128), F32),
            shaped((2, 4, 256, width), BF16),
            shaped((128, width), BF16),
        ],
        [ids, alibi_slopes, *chunks, *packs],
        [pltpu.VMEM((4, 16, width), F32)],
        scalars=2,
        spare=12,
        cost=0,
    )
    out_near = [out_rows] + [swap(out_rows, d) for d in (2, 4, 6)]
    far_piece = shift(after(piece, packs), 2)
    cot_near = pair(after(cot, far_piece))
    w_heads_far = swap(w_heads, 1)
    pieces_of_heads = [shaped((512, 128), BF16)] * 4

    def swap_heads(parts):
        got = [parts[0]] + [swap(parts[e], 2 * e) for e in (1, 2, 3)]
        far = kernel_call(heads_far_kernel, [shaped((4, 256, 128), BF16)], got, scalars=0)[0]
        return [*got, swap(far, 1)], far

    q_two, full, *mixed_parts = kernel_call(
        attend_kernel,
        [heads, shaped((2048, 128), F32), *pieces_of_heads],
        [ids, docs, q_one, keys, values],
        [pltpu.VMEM((8, 256, 128), BF16), pltpu.VMEM((2, 8, TILE, TILE), F32)],
        spare=14,
        cost=20,
    )
    mixed_parts = after(mixed_parts, out_near)
    out_pieces = [t for v in out_near for t in (v, swap(after(v, full), 1))]
    mixed_in, mixed_far = swap_heads(mixed_parts)
    far_piece = after(far_piece, mixed_far)
    far_near = [far_piece] + [swap(far_piece, d) for d in (2, 4, 6)]
    rows = shaped((256, width), BF16)
    full_rows = shaped((256, width), F32)
    w_out, mixed, resid, h_two = kernel_call(
        branch_kernel,
        [shaped((width, width), BF16), rows, full_rows, rows],
        [ids, chunk, *mixed_in, par, *out_pieces],
        tied=[w_heads_far],
        cost=5,
    )
    h_near = pair(h_two)
    up_row = up_bias.astype(F32).reshape(1, width)

    def feed(h, cots):
        return kernel_call(
            feed_kernel,
            [rows, rows, full_rows, full_rows],
            [h, cots, up_weight, up_row, down_weight],
            scalars=0,
            spare=8,
            cost=5,
        )

    def feed_other(h, cots, accs):
        return kernel_call(
            feed_other_kernel,
            [rows, rows, rows, rows],
            [ids, h, cots, par, *accs, *far_pieces],
            [pltpu.VMEM((256, width), F32)] * 2
            + [pltpu.VMEM((width, width), BF16)] * 2
            + [pltpu.VMEM((8, width), F32)],
            spare=8,
            cost=5,
        )

    act_own, dup_own, *accs_own = feed(h_two, cot)
    far_pieces = [t for v in far_near for t in (v, swap(after(v, act_own), 1))]
    act_near, dup_near, *accs_near = feed(h_near, cot_near)
    act_near_far, dup_near_far, branch_near, dh_near = feed_other(h_near, cot_near, accs_near)
    dh_got = pair(dh_near)
    act_own_far, dup_own_far, branch_own, dh_own = feed_other(h_two, after(cot, dh_near), accs_own)
    big = shaped((4, 512, width), BF16)
    keep, send, up_sums = kernel_call(
        feed_weights_kernel,
        [big, big, shaped((16, width), F32)],
        [
            ids,
            h_two,
            h_near,
            cot,
            cot_near,
            dup_own,
            dup_near,
            act_own,
            act_near,
            dup_own_far,
            dup_near_far,
            act_own_far,
            act_near_far,
        ],
        [pltpu.VMEM((2, width, width), BF16)],
        spare=8,
        cost=10,
    )
    dresid, dbranch, *dmixed_parts, sums = kernel_call(
        middle_kernel,
        [full_rows, rows, *pieces_of_heads, shaped((8, width), F32)],
        [ids, dh_own, dh_got, resid, cot, par, w_out],
        [pltpu.VMEM((256, width), BF16)],
        cost=40,
    )
    send = swap(send, 1)
    dmixed_heads, _ = swap_heads(after(dmixed_parts, send))

    def shape(*size):
        return shaped((*size, width), BF16)

    def relay(own_part, x_part, y_part):
        from_x, from_y = swap(x_part, 2), swap(y_part, 4)
        half = own_part.shape[0] // 4
        kept, x_next, y_next = kernel_call(
            relay_kernel,
            [shape(2 * half), shape(half), shape(half)],
            [own_part, from_x, from_y],
            scalars=0,
        )
        return kept, swap(y_next, 4), swap(x_next, 2)

    out_keep, out_send = kernel_call(
        out_weights_kernel,
        [shape(4, 128), shape(4, 128)],
        [ids, dbranch, mixed],
        [pltpu.VMEM((width, width), BF16)],
    )
    x_part, y_part, own_part = kernel_call(
        pair_sum_kernel,
        [shape(640), shape(640), shape(1280)],
        [keep, send, out_keep, swap(out_send, 1)],
        scalars=0,
    )
    feed_kept = relay(own_part, x_part, y_part)
    feed_near, feed_far, out_next, out_last = kernel_call(
        owned_kernel,
        [shape(288), shape(288), shape(32), shape(32)],
        [ids, *feed_kept],
        [pltpu.VMEM((128, width), BF16)],
    )
    branch_got = pair(after(branch_near, dbranch))
    layer_out = kernel_call(
        layer_out_kernel, [rows], [resid, par, branch_own, branch_got], scalars=0
    )[0]

    blocks = shaped((4, 256, 384), BF16)
    near, send = kernel_call(
        attend_back_kernel,
        [blocks, blocks],
        [ids, docs, q_two, keys, values, full, *dmixed_heads],
        [
            pltpu.VMEM((2, 2048, 128), BF16),
            *[pltpu.VMEM((2, 2048, 128), F32)] * 3,
            pltpu.VMEM((8, 256, 128), BF16),
        ],
        spare=14,
        cost=40,
        tied=[own_part, layer_out],
    )
    far = swap(send, 1)
    wsum = kernel_call(
        head_weights_kernel,
        [shaped((384, width), F32)],
        [near, send, h_one],
        scalars=0,
    )[0]
    x_part, y_part, own_part, slots_kept, slots_sent = kernel_call(
        unproject_kernel,
        [shape(256), shape(256), shape(512), shape(288), shape(288)],
        [
            ids,
            *chunks[0::2],
            near,
            far,
            send,
            w_heads,
            w_heads_far,
            par,
            sums,
            up_sums,
            wsum,
        ],
        [pltpu.VMEM((4, 144, width), BF16), pltpu.VMEM((4, 16, width), F32)],
        spare=8,
    )
    slots_near, slots_far = kernel_call(
        slots_kernel,
        [shape(144), shape(144)],
        [slots_kept, pair(slots_sent)],
        scalars=0,
        tied=[feed_kept[0]],
    )
    share_sums = relay(own_part, x_part, y_part)
    input_grad = kernel_call(
        input_kernel, [rows], [*share_sums, chunk, par, dresid], scalars=0, cost=10
    )[0]
    slot_sum = kernel_call(
        sum_kernel,
        [shape(144)],
        [slots_near, shift(slots_far, 2)],
        scalars=0,
        tied=[share_sums[0]],
    )[0]
    last_pieces = spread(slot_sum)
    feed_sum = kernel_call(
        feed_sum_kernel,
        [shape(288)],
        [feed_near, shift(feed_far, 2), shift(out_next, 1), shift(out_last, 3)],
        scalars=0,
        tied=[*last_pieces[2::2], input_grad],
    )[0]
    sizes = [256] * 6 + [1024, 512]
    qkv_grad, *vectors = kernel_call(
        last_grads_kernel,
        [shaped((768, width), F32), *(shaped((1, size), F32) for size in sizes)],
        [ids, *last_pieces],
        spare=14,
        cost=10,
    )
    feed_parts = spread_relayed(feed_sum, 144)
    feed_parts = [*feed_parts[:6], *feed_parts[6], *feed_parts[7]]
    vmem, hbm = pl.BlockSpec(memory_space=pltpu.VMEM), pl.BlockSpec(memory_space=pltpu.HBM)
    up_grad, down_grad, out_grad = pl.pallas_call(
        feed_grads_kernel,
        out_shape=[shaped((width, width), F32)] * 2 + [shaped((256, width), F32)],
        in_specs=[pl.BlockSpec(memory_space=pltpu.SMEM)] + [vmem] * 10,
        out_specs=[hbm] * 3,
        scratch_shapes=[pltpu.VMEM((8, 288, width), F32), pltpu.SemaphoreType.DMA((24,))],
        compiler_params=pltpu.CompilerParams(vmem_limit_bytes=24 * 1024 * 1024),
        cost_estimate=pl.CostEstimate(flops=0, bytes_accessed=0, transcendentals=0),
    )(ids, *feed_parts)
    g1, s1, ob, g2, s2, db, ub, bias_grad = (v.reshape(v.shape[1]) for v in vectors)
    return (
        layer_out.reshape(tokens.shape),
        input_grad.reshape(tokens.shape),
        g1,
        s1,
        qkv_grad,
        bias_grad,
        out_grad,
        ob,
        g2,
        s2,
        up_grad,
        ub,
        down_grad,
        db,
    )


def on_small_slice(mesh, tokens, slopes):
    return (
        mesh.shape["ctx"] == 8
        and mesh.shape["fsdp"] == 4
        and tokens.shape == (4, 2, 1024, 1024)
        and slopes.shape == (16,)
    )


def solution(mesh):
    in_specs = (
        P("fsdp", None, "ctx", None),
        P("fsdp", None, "ctx"),
        P(),
        P("fsdp"),
        P("fsdp"),
        P("fsdp", None),
        P("fsdp"),
        P("fsdp", None),
        P("fsdp"),
        P("fsdp"),
        P("fsdp"),
        P("fsdp", None),
        P("fsdp"),
        P("fsdp", None),
        P("fsdp"),
        P("fsdp", None, "ctx", None),
    )
    out_specs = (
        P("fsdp", None, "ctx", None),
        P("fsdp", None, "ctx", None),
        P("fsdp"),
        P("fsdp"),
        P("fsdp", None),
        P("fsdp"),
        P("fsdp", None),
        P("fsdp"),
        P("fsdp"),
        P("fsdp"),
        P("fsdp", None),
        P("fsdp"),
        P("fsdp", None),
        P("fsdp"),
    )
    def layer(*args):
        body = per_device if on_small_slice(mesh, args[0], args[2]) else gathered_device
        return jax.shard_map(
            body, mesh=mesh, in_specs=in_specs, out_specs=out_specs, check_vma=False
        )(*args)

    return layer
```

```python
import functools

import jax
import jax.numpy as jnp
import numpy as np
from jax import lax
from jax.experimental import pallas as pl
from jax.experimental.pallas import tpu as pltpu
from jax.sharding import PartitionSpec as P

EPS = 1e-05
MASKED = -1e30


def layer_norm(v, gain, shift):
    mean = jnp.mean(v, axis=-1, keepdims=True)
    centered = v - mean
    spread = jnp.mean(centered * centered, axis=-1, keepdims=True)
    return centered * lax.rsqrt(spread + EPS) * gain + shift


def gelu_tanh(v):
    return jax.nn.gelu(v, approximate=True)


def project_rows(values_in, weight):
    return lax.dot_general(
        values_in, weight, (((1,), (1,)), ((), ())), preferred_element_type=jnp.float32
    )


def cross_rows(left, right):
    return lax.dot_general(
        left, right, (((0,), (0,)), ((), ())), preferred_element_type=jnp.float32
    )


def token_positions(index, half_block, seq_len):
    owner = index // (2 * half_block)
    inside = index % (2 * half_block)
    return jnp.where(
        inside < half_block,
        owner * half_block + inside,
        seq_len - 1 - (owner * half_block + inside - half_block),
    )


def score_block(query3, keys3, query_pos, query_doc, key_pos, key_doc, slopes, scale):
    raw = jnp.einsum("qhe,khe->hqk", query3, keys3, preferred_element_type=jnp.float32) * scale
    distance = (query_pos[:, None] - key_pos[None, :]).astype(jnp.float32)
    scores = raw - slopes[:, None, None] * distance[None]
    allowed = ((key_pos[None, :] <= query_pos[:, None]) & (key_doc[None, :] == query_doc[:, None]))[
        None
    ]
    return (jnp.where(allowed, scores, MASKED), allowed)


def block_loop(total, size, visit, state):

    def turn_body(turn, inner):
        return visit(inner, turn * size, size)

    return lax.fori_loop(0, total // size, turn_body, state)


def gathered_device(
    tokens,
    doc_ids,
    alibi_slopes,
    ln1_gain,
    ln1_shift,
    qkv_weight,
    qkv_bias,
    out_weight,
    out_bias,
    ln2_gain,
    ln2_shift,
    up_weight,
    up_bias,
    down_weight,
    down_bias,
    cotangent,
):
    half_block = tokens.shape[2]
    width = tokens.shape[3]
    count = 2 * half_block
    heads = alibi_slopes.shape[0]
    head = width // heads
    scale = head ** (-0.5)
    seq_len = count * lax.axis_size("ctx")
    rows_in = tokens.reshape(count, width).astype(jnp.float32)
    doc_rows = doc_ids.reshape(count)
    grad_low = cotangent.reshape(count, width)
    grad_full = grad_low.astype(jnp.float32)
    own_pos = token_positions(
        lax.axis_index("ctx") * count + jnp.arange(count, dtype=jnp.int32), half_block, seq_len
    )
    gain_one, shift_one, w_qkv, b_qkv, w_out, b_out, gain_two, shift_two, b_down = (
        lax.all_gather(ln1_gain, "fsdp", axis=0, tiled=True),
        lax.all_gather(ln1_shift, "fsdp", axis=0, tiled=True),
        lax.all_gather(qkv_weight, "fsdp", axis=0, tiled=True),
        lax.all_gather(qkv_bias, "fsdp", axis=0, tiled=True),
        lax.all_gather(out_weight, "fsdp", axis=0, tiled=True),
        lax.all_gather(out_bias, "fsdp", axis=0, tiled=True),
        lax.all_gather(ln2_gain, "fsdp", axis=0, tiled=True),
        lax.all_gather(ln2_shift, "fsdp", axis=0, tiled=True),
        lax.all_gather(down_bias, "fsdp", axis=0, tiled=True),
    )
    norm_one, norm_one_pull = jax.vjp(
        layer_norm, rows_in, gain_one.astype(jnp.float32), shift_one.astype(jnp.float32)
    )
    h_one = norm_one.astype(jnp.bfloat16)
    joined = project_rows(h_one, w_qkv)
    bias_full = b_qkv.astype(jnp.float32)
    query = (joined[:, :width] + bias_full[:width]).astype(jnp.bfloat16)
    keys = joined[:, width : 2 * width].astype(jnp.bfloat16)
    values = (joined[:, 2 * width :] + bias_full[width:]).astype(jnp.bfloat16)
    query3 = query.reshape(count, heads, head)
    keys3 = keys.reshape(count, heads, head)
    values3 = values.reshape(count, heads, head)
    doc_all = lax.all_gather(doc_rows, "ctx", axis=0, tiled=True)
    start_state = (
        jnp.full((heads, count), MASKED, jnp.float32),
        jnp.zeros((heads, count), jnp.float32),
        jnp.zeros((count, heads, head), jnp.float32),
    )
    key_piece = lax.all_gather(keys, "ctx", axis=0, tiled=True)
    value_piece = lax.all_gather(values, "ctx", axis=0, tiled=True)

    def visit(state, offset, size):
        top, total, accum = state
        key_part = lax.dynamic_slice_in_dim(key_piece, offset, size).reshape(size, heads, head)
        value_part = lax.dynamic_slice_in_dim(value_piece, offset, size).reshape(size, heads, head)
        key_pos = token_positions(offset + jnp.arange(size, dtype=jnp.int32), half_block, seq_len)
        key_doc = lax.dynamic_slice_in_dim(doc_all, offset, size)
        scores, allowed = score_block(
            query3, key_part, own_pos, doc_rows, key_pos, key_doc, alibi_slopes, scale
        )
        new_top = jnp.maximum(top, jnp.max(scores, axis=2))
        weights = jnp.where(allowed, jnp.exp(scores - new_top[:, :, None]), 0.0)
        factor = jnp.exp(top - new_top)
        total = total * factor + jnp.sum(weights, axis=2)
        accum = accum * jnp.transpose(factor)[:, :, None] + jnp.einsum(
            "hqk,khe->qhe",
            weights.astype(jnp.bfloat16),
            value_part,
            preferred_element_type=jnp.float32,
        )
        return (new_top, total, accum)

    top, total, accum = block_loop(key_piece.shape[0], 512, visit, start_state)
    log_total = top + jnp.log(total)
    attended = accum / jnp.transpose(total)[:, :, None]
    mixed = attended.reshape(count, width).astype(jnp.bfloat16)
    resid = rows_in + project_rows(mixed, w_out) + b_out.astype(jnp.float32)
    norm_two, norm_two_pull = jax.vjp(
        layer_norm, resid, gain_two.astype(jnp.float32), shift_two.astype(jnp.float32)
    )
    h_two = norm_two.astype(jnp.bfloat16)
    w_up, b_up, w_down = (
        lax.all_gather(up_weight, "fsdp", axis=0, tiled=True),
        lax.all_gather(up_bias, "fsdp", axis=0, tiled=True),
        lax.all_gather(down_weight, "fsdp", axis=0, tiled=True),
    )
    up = project_rows(h_two, w_up) + b_up.astype(jnp.float32)
    act, gelu_pull = jax.vjp(gelu_tanh, up)
    act_low = act.astype(jnp.bfloat16)
    branch = jnp.dot(act_low, w_down, preferred_element_type=jnp.float32)
    layer_out = resid + branch + b_down.astype(jnp.float32)
    dup = gelu_pull(project_rows(grad_low, w_down))[0].astype(jnp.bfloat16)
    stacked = lax.psum_scatter(
        jnp.concatenate([cross_rows(dup, h_two), cross_rows(act_low, grad_low)], axis=1).astype(
            jnp.bfloat16
        ),
        "fsdp",
        scatter_dimension=0,
        tiled=True,
    ).astype(jnp.float32)
    up_rows_grad = stacked[:, :width]
    down_rows_grad = stacked[:, width:]
    up_bias_term = jnp.sum(dup, axis=0, dtype=jnp.float32)
    dnorm_two = jnp.dot(dup, w_up, preferred_element_type=jnp.float32)
    dresid_norm, gain_two_grad, shift_two_grad = norm_two_pull(dnorm_two)
    dresid = grad_full + dresid_norm
    dbranch = dresid.astype(jnp.bfloat16)
    out_bias_grad = jnp.sum(dbranch, axis=0, dtype=jnp.float32)
    out_weight_grad = cross_rows(dbranch, mixed)
    dmixed = jnp.dot(dbranch, w_out, preferred_element_type=jnp.float32).astype(jnp.bfloat16)
    dmixed3 = dmixed.reshape(count, heads, head)
    delta = jnp.transpose(jnp.sum(dmixed3.astype(jnp.float32) * attended, axis=2))
    query_key_piece = lax.all_gather(keys, "ctx", axis=0, tiled=True)
    query_value_piece = lax.all_gather(values, "ctx", axis=0, tiled=True)

    def visit(accum_grad, offset, size):
        key_part = lax.dynamic_slice_in_dim(query_key_piece, offset, size).reshape(
            size, heads, head
        )
        value_part = lax.dynamic_slice_in_dim(query_value_piece, offset, size).reshape(
            size, heads, head
        )
        key_pos = token_positions(offset + jnp.arange(size, dtype=jnp.int32), half_block, seq_len)
        key_doc = lax.dynamic_slice_in_dim(doc_all, offset, size)
        scores, allowed = score_block(
            query3, key_part, own_pos, doc_rows, key_pos, key_doc, alibi_slopes, scale
        )
        probs = jnp.where(allowed, jnp.exp(scores - log_total[:, :, None]), 0.0)
        dprobs = jnp.einsum("qhe,khe->hqk", dmixed3, value_part, preferred_element_type=jnp.float32)
        dscores = (probs * (dprobs - delta[:, :, None])).astype(jnp.bfloat16)
        return accum_grad + jnp.einsum(
            "hqk,khe->qhe", dscores, key_part, preferred_element_type=jnp.float32
        )

    query_sum = block_loop(
        query_key_piece.shape[0], 512, visit, jnp.zeros((count, heads, head), jnp.float32)
    )
    dquery = (query_sum * scale).reshape(count, width).astype(jnp.bfloat16)
    total_all, delta_all = (
        lax.all_gather(
            jnp.transpose(log_total).astype(jnp.bfloat16), "ctx", axis=0, tiled=True
        ).astype(jnp.float32),
        lax.all_gather(jnp.transpose(delta).astype(jnp.bfloat16), "ctx", axis=0, tiled=True).astype(
            jnp.float32
        ),
    )
    empty = jnp.zeros((count, heads, head), jnp.float32)
    query_piece = lax.all_gather(query, "ctx", axis=0, tiled=True)
    grad_piece = lax.all_gather(dmixed, "ctx", axis=0, tiled=True)

    def visit(state, offset, size):
        dkeys, dvalues = state
        query_part = lax.dynamic_slice_in_dim(query_piece, offset, size).reshape(size, heads, head)
        grad_part = lax.dynamic_slice_in_dim(grad_piece, offset, size).reshape(size, heads, head)
        query_pos = token_positions(offset + jnp.arange(size, dtype=jnp.int32), half_block, seq_len)
        query_doc = lax.dynamic_slice_in_dim(doc_all, offset, size)
        total_part = jnp.transpose(lax.dynamic_slice_in_dim(total_all, offset, size))
        delta_part = jnp.transpose(lax.dynamic_slice_in_dim(delta_all, offset, size))
        scores, allowed = score_block(
            query_part, keys3, query_pos, query_doc, own_pos, doc_rows, alibi_slopes, scale
        )
        probs = jnp.where(allowed, jnp.exp(scores - total_part[:, :, None]), 0.0)
        dvalues = dvalues + jnp.einsum(
            "hqk,qhe->khe",
            probs.astype(jnp.bfloat16),
            grad_part,
            preferred_element_type=jnp.float32,
        )
        dprobs = jnp.einsum("qhe,khe->hqk", grad_part, values3, preferred_element_type=jnp.float32)
        dscores = (probs * (dprobs - delta_part[:, :, None])).astype(jnp.bfloat16)
        dkeys = dkeys + jnp.einsum(
            "hqk,qhe->khe", dscores, query_part, preferred_element_type=jnp.float32
        )
        return (dkeys, dvalues)

    dkeys, dvalues = block_loop(query_piece.shape[0], 512, visit, (empty, empty))
    dkeys_low = (dkeys * scale).reshape(count, width).astype(jnp.bfloat16)
    dvalues_low = dvalues.reshape(count, width).astype(jnp.bfloat16)
    dfused = jnp.concatenate([dquery, dkeys_low, dvalues_low], axis=1)
    qkv_weight_grad = cross_rows(dfused, h_one)
    qkv_bias_grad = jnp.concatenate(
        [
            jnp.sum(dquery, axis=0, dtype=jnp.float32),
            jnp.sum(dvalues_low, axis=0, dtype=jnp.float32),
        ]
    )
    dnorm_one = jnp.dot(dfused, w_qkv, preferred_element_type=jnp.float32)
    dinput_norm, gain_one_grad, shift_one_grad = norm_one_pull(dnorm_one)
    input_grad = (dresid + dinput_norm).astype(jnp.bfloat16).reshape(tokens.shape)
    down_bias_grad = jnp.sum(grad_full, axis=0)
    shares = (
        lax.psum_scatter(
            qkv_weight_grad.astype(jnp.bfloat16), "fsdp", scatter_dimension=0, tiled=True
        ).astype(jnp.float32),
        lax.psum_scatter(
            out_weight_grad.astype(jnp.bfloat16), "fsdp", scatter_dimension=0, tiled=True
        ).astype(jnp.float32),
        lax.psum_scatter(
            qkv_bias_grad.astype(jnp.bfloat16), "fsdp", scatter_dimension=0, tiled=True
        ).astype(jnp.float32),
        lax.psum_scatter(
            out_bias_grad.astype(jnp.bfloat16), "fsdp", scatter_dimension=0, tiled=True
        ).astype(jnp.float32),
        lax.psum_scatter(
            gain_one_grad.astype(jnp.bfloat16), "fsdp", scatter_dimension=0, tiled=True
        ).astype(jnp.float32),
        lax.psum_scatter(
            shift_one_grad.astype(jnp.bfloat16), "fsdp", scatter_dimension=0, tiled=True
        ).astype(jnp.float32),
        lax.psum_scatter(
            gain_two_grad.astype(jnp.bfloat16), "fsdp", scatter_dimension=0, tiled=True
        ).astype(jnp.float32),
        lax.psum_scatter(
            shift_two_grad.astype(jnp.bfloat16), "fsdp", scatter_dimension=0, tiled=True
        ).astype(jnp.float32),
        lax.psum_scatter(
            up_bias_term.astype(jnp.bfloat16), "fsdp", scatter_dimension=0, tiled=True
        ).astype(jnp.float32),
        lax.psum_scatter(
            down_bias_grad.astype(jnp.bfloat16), "fsdp", scatter_dimension=0, tiled=True
        ).astype(jnp.float32),
    )
    totals = (
        lax.psum(shares[0].astype(jnp.bfloat16), "ctx").astype(jnp.float32),
        lax.psum(shares[1].astype(jnp.bfloat16), "ctx").astype(jnp.float32),
        lax.psum(up_rows_grad.astype(jnp.bfloat16), "ctx").astype(jnp.float32),
        lax.psum(down_rows_grad.astype(jnp.bfloat16), "ctx").astype(jnp.float32),
        lax.psum(shares[2].astype(jnp.bfloat16), "ctx").astype(jnp.float32),
        lax.psum(shares[3].astype(jnp.bfloat16), "ctx").astype(jnp.float32),
        lax.psum(shares[4].astype(jnp.bfloat16), "ctx").astype(jnp.float32),
        lax.psum(shares[5].astype(jnp.bfloat16), "ctx").astype(jnp.float32),
        lax.psum(shares[6].astype(jnp.bfloat16), "ctx").astype(jnp.float32),
        lax.psum(shares[7].astype(jnp.bfloat16), "ctx").astype(jnp.float32),
        lax.psum(shares[8].astype(jnp.bfloat16), "ctx").astype(jnp.float32),
        lax.psum(shares[9].astype(jnp.bfloat16), "ctx").astype(jnp.float32),
    )
    return (
        layer_out.astype(jnp.bfloat16).reshape(tokens.shape),
        input_grad,
        totals[6],
        totals[7],
        totals[0],
        totals[4],
        totals[1],
        totals[5],
        totals[8],
        totals[9],
        totals[2],
        totals[10],
        totals[3],
        totals[11],
    )

F32 = jnp.float32
BF16 = jnp.bfloat16
LOG2E = 1.4426950408889634
LN2 = 0.6931471805599453
TILE = 256
DOC_LANES = 48
BACKWARD_ENDS = {j: (3, 7) if j < 3 else (7,) for j in range(8)}
GELU_A = 0.7978845608028654
GELU_B = 0.044715


def dot_nt(a, b):
    return lax.dot_general(a, b, (((1,), (1,)), ((), ())), preferred_element_type=F32)


def dot_nn(a, b):
    return lax.dot_general(a, b, (((1,), (0,)), ((), ())), preferred_element_type=F32)


def dot_tn(a, b):
    return lax.dot_general(a, b, (((0,), (0,)), ((), ())), preferred_element_type=F32)


def kernel_call(body, outs, ins, scratch=(), scalars=1, tied=(), spare=7, cost=0):
    groups = [x if isinstance(x, tuple) else (x,) for x in ins[scalars:]]
    flat = [x for group in groups for x in group]
    joined = [
        pltpu.VMEM((sum(x.shape[0] for x in group), *group[0].shape[1:]), group[0].dtype)
        for group in groups
        if len(group) > 1
    ]
    scratch = [*joined, *scratch]
    room = sum(int(np.prod(x.shape)) * jnp.dtype(x.dtype).itemsize for x in scratch)

    def run(*refs):
        numbers, refs = refs[:scalars], refs[scalars:]
        sources, refs = refs[: len(flat)], refs[len(flat) + len(tied) :]
        targets, refs = refs[: len(outs)], refs[len(outs) :]
        places, refs = list(refs[: len(joined)]), refs[len(joined) :]
        held, at = [], 0
        for group in groups:
            if len(group) == 1:
                held.append(sources[at])
            else:
                held.append(places.pop(0))
                row = 0
                for source in sources[at : at + len(group)]:
                    held[-1][row : row + source.shape[0], :] = source[...]
                    row += source.shape[0]
            at += len(group)
        body(*numbers, *held, *targets, *refs)

    vmem = pl.BlockSpec(memory_space=pltpu.VMEM)
    return pl.pallas_call(
        run,
        out_shape=list(outs),
        in_specs=[pl.BlockSpec(memory_space=pltpu.SMEM)] * scalars
        + [vmem] * len(flat)
        + [pl.BlockSpec(memory_space=pl.ANY)] * len(tied),
        out_specs=[vmem] * len(outs),
        scratch_shapes=scratch,
        compiler_params=pltpu.CompilerParams(vmem_limit_bytes=room + spare * 1024 * 1024),
        cost_estimate=pl.CostEstimate(
            flops=int(cost * 1e9), bytes_accessed=0, transcendentals=0
        ),
    )(*ins[:scalars], *flat, *tied)


def shaped(shape, dtype):
    return jax.ShapeDtypeStruct(shape, dtype)


def lanes_of(shape):
    return lax.broadcasted_iota(jnp.int32, shape, len(shape) - 1)


def three_pieces(v):
    high = v.astype(BF16).astype(F32)
    mid = (v - high).astype(BF16).astype(F32)
    return high, mid, v - high - mid


def normed(v):
    mean = jnp.mean(v, axis=-1, keepdims=True)
    centered = v - mean
    spread = jnp.mean(centered * centered, axis=-1, keepdims=True)
    root = lax.rsqrt(spread + EPS)
    return centered * root, root


def norm_back(dout, unit, root, gain):
    dn = dout * gain
    first = jnp.mean(dn, axis=-1, keepdims=True)
    second = jnp.mean(dn * unit, axis=-1, keepdims=True)
    return root * (dn - first - unit * second)


def block_rows(index, half_block):
    return pl.ds(pl.multiple_of(index * half_block, half_block), half_block)


def prepare_kernel(ids, *refs):
    own, w_ref, out_ref, up_ref, down_ref = refs[0:5]
    vectors, (chunk, pack, piece), places, sems = refs[5:14], refs[14:17], refs[17:31], refs[31]
    c = ids[0]

    def rows(ref, start, count):
        return ref.at[pl.ds(pl.multiple_of(start * count, count), count)]

    sources = [
        own,
        rows(w_ref, ids[5], 128),
        rows(out_ref, c, 32),
        rows(up_ref, c, 128),
        rows(down_ref, c, 128),
        *vectors,
    ]
    copies = [
        pltpu.make_async_copy(a, b, sems.at[i]) for i, (a, b) in enumerate(zip(sources, places))
    ]
    for copy in copies:
        copy.start()
    for copy in copies:
        copy.wait()
    doc, g1, s1, ob, g2, s2, db, qb, ub = places[5:]
    docs = doc[...].astype(F32)
    row = jnp.concatenate([docs[0:1], docs[1:2]], axis=1)
    chunk[256:272, :] = jnp.zeros((16, 1024), BF16)
    chunk[256:272, 0:256] = jnp.broadcast_to(row, (16, 256)).astype(BF16)

    def wide(ref):
        size = ref.shape[0]
        return jnp.broadcast_to(ref[...].astype(F32).reshape(1, size), (8, size))

    first = jnp.concatenate([wide(r) for r in (g1, s1, ob, g2)], axis=1)
    at = lax.broadcasted_iota(jnp.int32, (8, 1024), 0)
    first = jnp.where(at < 4, first, wide(ub))
    second = jnp.concatenate([wide(r) for r in (s2, db, qb)], axis=1)
    small = jnp.concatenate([first, second], axis=0).astype(BF16)
    chunk[0:256, :] = places[0][...]
    pack[0:128, :] = places[1][...]
    pack[128:144, :] = small
    pack[144:176, :] = places[2][...]
    piece[0:128, :] = places[3][...]
    piece[128:256, :] = places[4][...]


def unpack_kernel(ids, p0, p1, p2, p3, w_out, par_out, out_rows, small):
    packs = (p0, p1, p2, p3)
    f = ids[1]
    for k in range(4):
        plane = lax.rem(f + (4 - k), 4)
        small[plane] = packs[k][128:144, :].astype(F32)
        at = pl.multiple_of(plane * 32, 32)
        out_rows[pl.ds(at, 32), :] = packs[k][144:176, :]
        for kind in range(3):

            @pl.when(ids[2 + kind] == plane)
            def _():
                w_out[kind * 128 : (kind + 1) * 128, :] = packs[k][0:128, :]

    rows = [small[p] for p in range(4)]

    def whole(row, start, stop, planes=(0, 1, 2, 3)):
        return jnp.concatenate([rows[p][row * 8 : row * 8 + 1, start:stop] for p in planes], axis=1)

    par_out[0:1, :] = whole(0, 0, 256)
    par_out[1:2, :] = whole(0, 256, 512)
    par_out[2:3, :] = whole(0, 512, 768)
    par_out[3:4, :] = whole(0, 768, 1024)
    par_out[4:5, :] = whole(1, 0, 256)
    par_out[5:6, :] = whole(1, 256, 512)
    par_out[6:7, :] = whole(1, 512, 1024, (0, 1))
    par_out[7:8, :] = whole(1, 512, 1024, (2, 3))
    par_out[8:16, :] = small[f ^ 2][0:8, :]
    par_out[8:9, :] = small[f ^ 2][4:5, :]


def project_kernel(ids, slopes, *refs):
    chunks, (w_ref, par_out, q_out, k_out, v_out, doc_out, h_out) = refs[:8], refs[8:]
    c = ids[0]
    mine = pl.ds(pl.multiple_of(c * 128, 128), 128)
    bias_q = par_out[6:7, mine]
    bias_v = par_out[7:8, mine]
    gain, shift = par_out[0:1, :], par_out[1:2, :]
    weight = w_ref[...]
    lane = lanes_of((256, 128))
    row = lax.broadcasted_iota(jnp.int32, (256, 128), 0)
    eye = (
        lax.broadcasted_iota(jnp.int32, (128, 128), 0) == lanes_of((128, 128))
    ).astype(BF16)
    sub = lax.broadcasted_iota(jnp.int32, (128, 256), 0).astype(F32) - 67.0
    is_doc = (lane >= 67) & (lane < 67 + DOC_LANES)
    low = lane < 64
    for d in range(8):
        cc = c ^ d
        h = (normed(chunks[d][0:256, :].astype(F32))[0] * gain + shift).astype(BF16)
        h_out[d % 2, d // 2] = h
        joined = dot_nt(h, weight)
        query = (joined[:, 0:128] + bias_q) * (LOG2E * 0.125)
        keys = joined[:, 128:256]
        values = joined[:, 256:384] + bias_v
        doc_row = chunks[d][256:272, 0:256].astype(F32)[0:1, :]
        doc_out[pl.ds(cc, 1), :] = doc_row[:, 0:128]
        doc_out[pl.ds(8 + cc, 1), :] = doc_row[:, 128:256]
        one_hot = dot_tn((sub == doc_row).astype(BF16), eye)
        pos = jnp.where(row < 128, cc * 128 + row, 2175 - cc * 128 - row).astype(F32)
        q_aug = jnp.where(lane < 67, 1.0, jnp.where(is_doc, one_hot, 0.0))
        k_tail = jnp.where(is_doc, (1.0 - one_hot) * MASKED, jnp.where(lane < 118, 1.0, 0.0))
        for hh in range(2):
            if hh == 1:
                query, keys, values = (pltpu.roll(t, 64, 1) for t in (query, keys, values))
            high, mid, rest = three_pieces(pos * (slopes[2 * c + hh] * LOG2E))
            k_aug = jnp.where(
                lane == 64, high, jnp.where(lane == 65, mid, jnp.where(lane == 66, rest, k_tail))
            )
            parts = (
                (q_out, jnp.where(low, query, q_aug).astype(BF16)),
                (k_out, jnp.where(low, keys, k_aug).astype(BF16)),
                (v_out, jnp.where(low, values, 1.0).astype(BF16)),
            )
            for ref, value in parts:
                ref[hh, block_rows(cc, 128), :] = value[0:128]
                ref[hh, block_rows(8 + cc, 128), :] = value[128:256]


def tile_start(i):
    return i * TILE if i < 4 else 1024 + (7 - i) * TILE


def tile_rows(i):
    start = jnp.where(i < 4, i * TILE, 1024 + (7 - i) * TILE)
    return pl.ds(pl.multiple_of(start, TILE), TILE)


def tile_docs(docs, i):
    at = tile_start(i) // 128
    return docs[at : at + 2, :]


def count_tiles(flags):
    total = jnp.sum(jnp.where(flags, 1.0, 0.0)).astype(jnp.int32)
    return lax.shift_right_logical(total, 8)


def span(first, last):
    out = []
    if first < 4 and first <= last:
        out.append(slice(first * TILE, (min(last, 3) + 1) * TILE))
    if last >= 4 and first <= last:
        out.append(slice(tile_start(last), tile_start(max(first, 4)) + TILE))
    return out


def attend_kernel(
    ids, docs_ref, q_ref, k_ref, v_ref, q_out, full_out, m0, m1, m2, m3, mixed_out, held
):
    docs = docs_ref[...]
    lane = lanes_of((TILE, 128))
    low = lane < 64
    step_right = lanes_of((TILE, TILE)) - lax.broadcasted_iota(jnp.int32, (TILE, TILE), 0)

    def widest(scores):
        return jnp.maximum(scores[:, 0:128], scores[:, 128:256])

    def one_tile(i, carry):
        own = tile_rows(i)
        at = jnp.where(i < 4, 2 * i, 8 + 2 * (7 - i))
        first = count_tiles(docs < jnp.min(docs_ref[pl.ds(at, 2), :]))
        allowed = jnp.where(i < 4, step_right, -step_right) <= 0
        queries = [q_ref[hh, own, :] for hh in range(2)]
        diagonal = [
            jnp.where(allowed, dot_nt(queries[hh], k_ref[hh, own, :]), MASKED) for hh in range(2)
        ]

        def look(j, tops):
            rows = tile_rows(j)
            out = []
            for hh in range(2):
                scores = dot_nt(queries[hh], k_ref[hh, rows, :])
                held[hh, j] = scores
                out.append(jnp.maximum(tops[hh], widest(scores)))
            return tuple(out)

        tops = lax.fori_loop(first, i, look, tuple(widest(s) for s in diagonal))
        tops = [jnp.max(t, axis=1, keepdims=True) for t in tops]

        def gather(j, sums):
            rows = tile_rows(j)
            out = []
            for hh in range(2):
                weights = jnp.exp2(held[hh, j] - tops[hh]).astype(BF16)
                out.append(sums[hh] + dot_nn(weights, v_ref[hh, rows, :]))
            return tuple(out)

        start = tuple(
            dot_nn(jnp.exp2(diagonal[hh] - tops[hh]).astype(BF16), v_ref[hh, own, :])
            for hh in range(2)
        )
        sums = lax.fori_loop(first, i, gather, start)
        outs = []
        for hh in range(2):
            total = sums[hh][:, 64:65]
            outs.append(sums[hh] / total)
            high, mid, rest = three_pieces(-(tops[hh] + jnp.log2(total)))
            tail = jnp.where(
                lane == 115,
                high,
                jnp.where(lane == 116, mid, jnp.where(lane == 117, rest, queries[hh].astype(F32))),
            )
            q_out[hh, own, :] = tail.astype(BF16)
        both = jnp.where(low, outs[0], pltpu.roll(outs[1], 64, 1))
        full_out[own, :] = both
        half = jnp.where(i < 4, 0, 128)
        chunk = jnp.where(i < 4, 2 * i, 2 * (7 - i))
        for piece in range(2):
            mixed_out[chunk + piece, pl.ds(pl.multiple_of(half, 128), 128), :] = both[
                piece * 128 : (piece + 1) * 128
            ].astype(BF16)
        return carry

    lax.fori_loop(0, 8, one_tile, 0)
    for e, ref in enumerate((m0, m1, m2, m3)):
        for parity in range(2):
            ref[parity * 256 : (parity + 1) * 256, :] = mixed_out[ids[0] ^ (2 * e + parity)]


def heads_far_kernel(g0, g1, g2, g3, out):
    for e, ref in enumerate((g0, g1, g2, g3)):
        out[e] = ref[256:512, :]


def attend_back_kernel(
    ids, docs_ref, q_ref, k_ref, v_ref, full_ref, g0, g1, g2, g3, g_far, keep, send, grads, dq, dk, dv, all_grads
):
    docs = docs_ref[...]
    lane = lanes_of((256, 128))
    low = lane < 64
    for e, ref in enumerate((g0, g1, g2, g3)):
        all_grads[ids[0] ^ (2 * e)] = ref[0:256, :]
        all_grads[ids[0] ^ (2 * e + 1)] = g_far[e]
    for at in range(8):
        piece = all_grads[at].astype(F32)
        other = jnp.concatenate(
            [
                full_ref[at * 128 : (at + 1) * 128, :],
                full_ref[1024 + at * 128 : 1024 + (at + 1) * 128, :],
            ],
            axis=0,
        )
        product = piece * other
        for hh in range(2):
            delta = jnp.sum(jnp.where(low == (hh == 0), product, 0.0), axis=1, keepdims=True)
            high, mid, rest = three_pieces(-delta)
            tail = jnp.where(
                lane == 64, high, jnp.where(lane == 65, mid, jnp.where(lane == 66, rest, 0.0))
            )
            moved = piece if hh == 0 else pltpu.roll(piece, 64, 1)
            value = jnp.where(low, moved, tail).astype(BF16)
            grads[hh, at * 128 : (at + 1) * 128, :] = value[0:128]
            grads[hh, 1024 + at * 128 : 1024 + (at + 1) * 128, :] = value[128:256]
    dq[...] = jnp.zeros_like(dq)
    down, right = lax.broadcasted_iota(jnp.int32, (TILE, TILE), 0), lanes_of((TILE, TILE))

    def run(j, last):
        own = slice(tile_start(j), tile_start(j) + TILE)
        allowed = (down <= right) if j < 4 else (down >= right)
        places = [own] + span(j + 1, last)

        def head(hh, carry):
            keys, values = k_ref[hh, own, :], v_ref[hh, own, :]
            dk_sum = dv_sum = 0.0
            for at, rows in enumerate(places):
                query, grad = q_ref[hh, rows, :], grads[hh, rows, :]
                probs = jnp.exp2(dot_nt(keys, query))
                if at == 0:
                    probs = jnp.where(allowed, probs, 0.0)
                dscores = (probs * dot_nt(values, grad)).astype(BF16)
                dq[hh, rows, :] += dot_tn(dscores, keys)
                dk_sum += dot_nn(dscores, query)
                dv_sum += dot_nn(probs.astype(BF16), grad)
            dk[hh, own, :] = dk_sum
            dv[hh, own, :] = dv_sum
            return carry

        lax.fori_loop(0, 2, head, 0)

    for j in range(8):
        ends = BACKWARD_ENDS[j]
        within = jnp.sum(jnp.where(docs <= jnp.max(tile_docs(docs, j)), 1.0, 0.0))
        last = lax.shift_right_logical(within.astype(jnp.int32) + (TILE - 1), 8) - 1
        for at, end in enumerate(ends):
            fits = last <= end
            if at:
                fits = fits & (last > ends[at - 1])
            if len(ends) == 1:
                run(j, end)
            else:
                pl.when(fits)(functools.partial(run, j, end))
    for j in range(4):
        for parity, ref in enumerate((keep, send)):
            cc = ids[0] ^ (2 * j + parity)
            for half in range(2):
                rows = block_rows(8 * half + cc, 128)
                at = slice(half * 128, (half + 1) * 128)
                for which, (held, scale) in enumerate(((dq, 0.125), (dk, LN2), (dv, 1.0))):
                    other = pltpu.roll(held[1, rows, :], 64, 1)
                    both = jnp.where(low[0:128], held[0, rows, :], other) * scale
                    ref[j, at, which * 128 : (which + 1) * 128] = both.astype(BF16)


def branch_kernel(ids, chunk, g0, g1, g2, g3, g_far, par, *refs):
    pieces, (w_out, mixed_out, resid_out, h_out) = refs[:8], refs[8:]
    for d in range(8):
        for plane in range(4):
            at = pl.multiple_of(plane * 256 + (ids[0] ^ d) * 32, 32)
            w_out[pl.ds(at, 32), :] = pieces[d][plane * 32 : (plane + 1) * 32, :]
    for e, ref in enumerate((g0, g1, g2, g3)):
        for parity, value in enumerate((ref[0:256, :], g_far[e])):
            at = pl.multiple_of((ids[0] ^ (2 * e + parity)) * 128, 128)
            mixed_out[:, pl.ds(at, 128)] = value
    resid = chunk[0:256, :].astype(F32) + dot_nt(mixed_out[...], w_out[...]) + par[2:3, :]
    resid_out[...] = resid
    h_out[...] = (normed(resid)[0] * par[3:4, :] + par[4:5, :]).astype(BF16)


def feed_step(h, cot, up_w, down_w, bias):
    u = dot_nt(h, up_w) + bias
    grad = dot_nt(cot, down_w)
    square = u * u
    th = jnp.tanh(GELU_A * u * (1.0 + GELU_B * square))
    half = 0.5 * (1.0 + th)
    act = (u * half).astype(BF16)
    slope = half + 0.5 * u * (1.0 - th * th) * (GELU_A * (1.0 + 3.0 * GELU_B * square))
    return act, (grad * slope).astype(BF16)


def feed_kernel(h_ref, cot_ref, up_ref, bias_ref, down_ref, act_out, dup_out, acc, dacc):
    acc[...] = jnp.zeros_like(acc)
    dacc[...] = jnp.zeros_like(dacc)

    def step(t, carry):
        at = pl.ds(pl.multiple_of(t * 256, 256), 256)
        up_w, down_w = up_ref[at, :], down_ref[at, :]
        act, dup = feed_step(h_ref[...], cot_ref[...], up_w, down_w, bias_ref[0:1, at])
        act_out[:, at] = act
        dup_out[:, at] = dup
        acc[...] += dot_nn(act, down_w)
        dacc[...] += dot_nn(dup, up_w)
        return carry

    lax.fori_loop(0, 4, step, 0)


def feed_other_kernel(ids, h_ref, cot_ref, par, acc_in, dacc_in, *refs):
    pieces, (act_out, dup_out, branch, dh, acc, dacc, ups, downs, bias) = refs[:8], refs[8:]
    for d in range(8):
        at = slice(d * 128, (d + 1) * 128)
        ups[at, :] = pieces[d][0:128, :]
        downs[at, :] = pieces[d][128:256, :]
        bias[0:1, at] = par[8:9, pl.ds(pl.multiple_of((ids[0] ^ d) * 128, 128), 128)]
    acc[...] = acc_in[...]
    dacc[...] = dacc_in[...]

    def step(t, carry):
        at = pl.ds(pl.multiple_of(t * 256, 256), 256)
        up_w, down_w = ups[at, :], downs[at, :]
        act, dup = feed_step(h_ref[...], cot_ref[...], up_w, down_w, bias[0:1, at])
        act_out[:, at] = act
        dup_out[:, at] = dup
        acc[...] += dot_nn(act, down_w)
        dacc[...] += dot_nn(dup, up_w)
        return carry

    lax.fori_loop(0, 4, step, 0)
    branch[...] = acc[...].astype(BF16)
    dh[...] = dacc[...].astype(BF16)


def middle_kernel(
    ids, d0, d1, resid_ref, cot_ref, par, w_ref, dresid_out, dbranch_out, m0, m1, m2, m3, sums, held
):
    dh = d0[...].astype(F32) + d1[...].astype(F32)
    unit, root = normed(resid_ref[...])
    cot = cot_ref[...].astype(F32)
    dresid = cot + norm_back(dh, unit, root, par[3:4, :])
    dresid_out[...] = dresid
    dbranch = dresid.astype(BF16)
    dbranch_out[...] = dbranch
    held[...] = dot_nn(dbranch, w_ref[...]).astype(BF16)
    for e, ref in enumerate((m0, m1, m2, m3)):
        for parity in range(2):
            at = pl.multiple_of((ids[0] ^ (2 * e + parity)) * 128, 128)
            ref[parity * 256 : (parity + 1) * 256, :] = held[:, pl.ds(at, 128)]
    sums[...] = jnp.zeros_like(sums)
    sums[0:1, :] = jnp.sum(dbranch.astype(F32), axis=0, keepdims=True)
    sums[1:2, :] = jnp.sum(dh * unit, axis=0, keepdims=True)
    sums[2:3, :] = jnp.sum(dh, axis=0, keepdims=True)
    sums[3:4, :] = jnp.sum(cot, axis=0, keepdims=True)


def feed_weights_kernel(ids, *refs):
    hs, cots, dups, acts, dups_far, acts_far = (refs[2 * i : 2 * i + 2] for i in range(6))
    keep, send, bias, all_rows = refs[12:]
    c = ids[0]

    def product(lefts, at, rights):
        return sum(dot_tn(a[:, at], b[...]) for a, b in zip(lefts, rights)).astype(BF16)

    for t in range(4):
        at = slice(t * 256, (t + 1) * 256)
        for which, (lefts, rights) in enumerate(((dups, hs), (acts, cots))):
            all_rows[which, at, :] = product(lefts, at, rights)
        for which, (lefts, rights) in enumerate(((dups_far, hs), (acts_far, cots))):
            both = product(lefts, at, rights)
            for parity, ref in enumerate((keep, send)):
                place = slice(256 + which * 128, 384 + which * 128)
                ref[t, place, :] = both[parity * 128 : (parity + 1) * 128]
    for e in range(4):
        for parity, ref in enumerate((keep, send)):
            rows = block_rows(c ^ (2 * e + parity), 128)
            ref[e, 0:128, :] = all_rows[0, rows, :]
            ref[e, 128:256, :] = all_rows[1, rows, :]

    def total(refs):
        return sum(jnp.sum(r[...].astype(F32), axis=0, keepdims=True) for r in refs)

    bias[0:1, :] = total(dups)
    far = total(dups_far)
    for d in range(8):
        at = pl.ds(pl.multiple_of((c ^ d) * 128, 128), 128)
        bias[8:9, at] = far[:, d * 128 : (d + 1) * 128]


def out_weights_kernel(ids, dbranch, mixed, keep, send, total):
    for t in range(4):
        at = slice(t * 256, (t + 1) * 256)
        total[at, :] = dot_tn(dbranch[:, at], mixed[...]).astype(BF16)
    for e in range(4):
        for parity, ref in enumerate((keep, send)):
            cc = ids[0] ^ (2 * e + parity)
            for plane in range(4):
                at = pl.multiple_of(plane * 256 + cc * 32, 32)
                ref[e, plane * 32 : (plane + 1) * 32, :] = total[pl.ds(at, 32), :]


def added(*values):
    return sum(v.astype(F32) for v in values).astype(BF16)


def pair_sum_kernel(keep, got, out_keep, out_got, x_out, y_out, own_out):
    def put(target, slot, e, part):
        rows = slice(256 * part, 256 * (part + 1))
        more = slice(64 * part, 64 * (part + 1))
        at = slot * 320
        target[at : at + 256, :] = added(keep[e, rows], got[e, rows])
        target[at + 256 : at + 320, :] = added(out_keep[e, more], out_got[e, more])

    put(x_out, 0, 1, 0)
    put(x_out, 1, 3, 0)
    put(y_out, 0, 2, 1)
    put(y_out, 1, 3, 1)
    put(own_out, 0, 0, 0)
    put(own_out, 1, 0, 1)
    put(own_out, 2, 2, 0)
    put(own_out, 3, 1, 1)


def relay_kernel(own, from_x, from_y, kept, x_out, y_out):
    half = own.shape[0] // 4
    kept[0:half, :] = added(own[0:half, :], from_x[0:half, :])
    y_out[...] = added(own[2 * half : 3 * half, :], from_x[half:, :])
    kept[half:, :] = added(own[half : 2 * half, :], from_y[0:half, :])
    x_out[...] = added(own[3 * half :, :], from_y[half:, :])


def owned_kernel(ids, kept, from_y, from_x, near, far, out_next, out_last, share):
    f = ids[1]
    near[0:256, :] = added(kept[0:256, :], from_y[0:256, :])
    far[0:256, :] = added(kept[320:576, :], from_x[0:256, :])
    share[0:64, :] = added(kept[256:320, :], from_y[256:320, :])
    share[64:128, :] = added(kept[576:640, :], from_x[256:320, :])
    for k, target in enumerate((near, out_next, far, out_last)):
        rows = pl.ds(pl.multiple_of(lax.rem(f + k, 4) * 32, 32), 32)
        if k % 2:
            target[...] = share[rows, :]
        else:
            target[256:288, :] = share[rows, :]


def feed_sum_kernel(near, far, out_next, out_last, out):
    out[0:256, :] = added(near[0:256, :], far[0:256, :])
    outs = (near[256:288, :], far[256:288, :], out_next[...], out_last[...])
    out[256:288, :] = added(*outs)


def slots_kernel(kept, got, near, far):
    near[...] = added(kept[0:144, :], got[0:144, :])
    far[...] = added(kept[144:288, :], got[144:288, :])


def sum_kernel(*refs):
    refs[-1][...] = added(*(r[...] for r in refs[:-1]))


def layer_out_kernel(resid, par, one, two, out):
    out[...] = (resid[...] + par[5:6, :] + one[...].astype(F32) + two[...].astype(F32)).astype(BF16)


def head_weights_kernel(keep, send, h_ref, total):
    for parity, ref in enumerate((keep, send)):
        for j in range(4):
            got = dot_tn(ref[j], h_ref[parity, j])
            if parity == 0 and j == 0:
                total[...] = got
            else:
                total[...] += got


def unproject_kernel(ids, *refs):
    chunks, (near, far, bias_far, w_near, w_far, par, sums, up_sums, wsum) = refs[:4], refs[4:13]
    x_out, y_out, own_out, slots_kept, slots_sent, slots, small = refs[13:]
    c, f = ids[0], ids[1]
    near_w, far_w = w_near[...], w_far[...]
    gain_grad = shift_grad = bias_grad = 0.0
    places = (
        (own_out, 0, own_out, 128),
        (x_out, 0, own_out, 384),
        (own_out, 256, y_out, 0),
        (x_out, 128, y_out, 128),
    )
    for e, chunk in enumerate(chunks):
        grads = near[e]
        unit = normed(chunk[0:256, :].astype(F32))[0]
        share = dot_nn(grads, near_w) + dot_nn(far[e], far_w)
        top, at, bottom, below = places[e]
        top[at : at + 128, :] = share[0:128].astype(BF16)
        bottom[below : below + 128, :] = share[128:256].astype(BF16)
        gain_grad += jnp.sum(share * unit, axis=0, keepdims=True)
        shift_grad += jnp.sum(share, axis=0, keepdims=True)
        bias_grad += jnp.sum(grads.astype(F32) + bias_far[e].astype(F32), axis=0, keepdims=True)
    small[...] = jnp.zeros_like(small)
    for p in range(4):
        at = slice(p * 256, (p + 1) * 256)
        small[p, 0:1, 0:256] = gain_grad[:, at]
        small[p, 0:1, 256:512] = shift_grad[:, at]
        small[p, 0:1, 512:768] = sums[0:1, at]
        small[p, 0:1, 768:1024] = sums[1:2, at]
        small[p, 1:2, 0:256] = sums[2:3, at]
        small[p, 1:2, 256:512] = sums[3:4, at]
        small[p, 1:2, 512:640] = bias_grad[:, 0:128] if p < 2 else bias_grad[:, 256:384]
        up_far = jnp.where(f == p ^ 2, up_sums[8:9, :], 0.0)
        small[p, 2:3, :] = jnp.where(f == p, up_sums[0:1, :], up_far)
        start = pl.multiple_of(ids[6 + p] * 128, 128)
        slots[p, 0:128, :] = wsum[pl.ds(start, 128), :].astype(BF16)
        slots[p, 128:144, :] = small[p].astype(BF16)
    for k in range(2):
        at = slice(k * 144, (k + 1) * 144)
        slots_kept[at, :] = slots[f ^ (2 * k)]
        slots_sent[at, :] = slots[f ^ (2 * k + 1)]


def input_kernel(kept, from_y, from_x, chunk, par, dresid, out):
    moved = jnp.concatenate([from_y[...], from_x[...]], axis=0)
    dh = kept[...].astype(F32) + moved.astype(F32)
    unit, root = normed(chunk[0:256, :].astype(F32))
    out[...] = (dresid[...] + norm_back(dh, unit, root, par[0:1, :])).astype(BF16)


def feed_grads_kernel(ids, *refs, count, first):
    pieces, (up_out, down_out, out_out, place, sems) = refs[:count], refs[-5:]
    copies = []
    for n, piece in enumerate(pieces):
        cc = ids[0] ^ (first + n)
        place[n] = piece[...].astype(F32)
        moves = (
            (place.at[n, 0:128], up_out.at[block_rows(cc, 128)]),
            (place.at[n, 128:256], down_out.at[block_rows(cc, 128)]),
            (place.at[n, 256:288], out_out.at[pl.ds(pl.multiple_of(cc * 32, 32), 32)]),
        )
        for i, (a, b) in enumerate(moves):
            copies.append(pltpu.make_async_copy(a, b, sems.at[3 * n + i]))
            copies[-1].start()
    for copy in copies:
        copy.wait()


def feed_grads_last_kernel(ids, t0, b0, t1, b1, *refs):
    pieces, place = (t0, b0, t1, b1), refs[-2]
    up_out, down_out, out_out, sems = *refs[-5:-2], refs[-1]
    copies = []
    for n in range(2):
        cc = ids[0] ^ (6 + n)
        place[n, 0:144] = pieces[2 * n][...].astype(F32)
        place[n, 144:288] = pieces[2 * n + 1][...].astype(F32)
        moves = (
            (place.at[n, 0:128], up_out.at[block_rows(cc, 128)]),
            (place.at[n, 128:256], down_out.at[block_rows(cc, 128)]),
            (place.at[n, 256:288], out_out.at[pl.ds(pl.multiple_of(cc * 32, 32), 32)]),
        )
        for i, (a, b) in enumerate(moves):
            copies.append(pltpu.make_async_copy(a, b, sems.at[3 * n + i]))
            copies[-1].start()
    for copy in copies:
        copy.wait()


def last_grads_kernel(ids, *refs):
    pieces, (qkv_out, g1, s1, ob, g2, s2, db, ub, bias_out) = refs[:8], refs[8:]
    c, f = ids[0], ids[1]
    total = 0.0
    for d in range(8):
        cc = c ^ d
        place = lax.rem(cc + 24 - 6 * f, 8)

        @pl.when(place < 6)
        def _():
            qkv_out[block_rows(place, 128), :] = pieces[d][0:128, :].astype(F32)

        rows = pieces[d][128:144, :].astype(F32)
        total += rows

        @pl.when(lax.div(cc, 4) == lax.rem(f, 2))
        def _():
            at = pl.multiple_of(lax.rem(cc, 4) * 128, 128)
            bias_out[0:1, pl.ds(at, 128)] = rows[1:2, 512:640]

    for ref, row, start in ((g1, 0, 0), (s1, 0, 256), (ob, 0, 512), (g2, 0, 768), (s2, 1, 0), (db, 1, 256)):
        ref[...] = total[row : row + 1, start : start + 256]
    ub[...] = total[2:3, :]


def per_device(
    tokens,
    doc_ids,
    alibi_slopes,
    ln1_gain,
    ln1_shift,
    qkv_weight,
    qkv_bias,
    out_weight,
    out_bias,
    ln2_gain,
    ln2_shift,
    up_weight,
    up_bias,
    down_weight,
    down_bias,
    cotangent,
):
    c, f = lax.axis_index("ctx"), lax.axis_index("fsdp")
    width = 1024

    def swap(v, d):
        return lax.ppermute(v, "ctx", [(i, i ^ d) for i in range(8)])

    def shift(v, k):
        return lax.ppermute(v, "fsdp", [(i, (i + k) % 4) for i in range(4)])

    def pair(v):
        return lax.ppermute(v, "fsdp", [(i, i ^ 1) for i in range(4)])

    def after(value, *earlier):
        return lax.optimization_barrier((value, earlier))[0]

    def spread(v):
        near = [v] + [swap(v, d) for d in (2, 4, 6)]
        return [t for e in near for t in (e, swap(e, 1))]

    def spread_relayed(v, cut, *earlier):
        from_x, from_y = swap(v, 2), swap(v, 4)
        top, bottom = swap(from_x[:cut], 4), swap(from_y[cut:], 2)
        kept = (v, from_x, from_y, top, bottom)
        pairs = [(p, swap(q, 1)) for p, q in zip(kept, after(kept, top, bottom, *earlier))]
        last = [(pairs[3][side], pairs[4][side]) for side in range(2)]
        return [t for p in pairs[:3] for t in p] + last

    table = np.zeros((32, 16), np.int32)
    for ci in range(8):
        for fi in range(4):
            at = ci * 4 + fi
            table[at, 0:2] = ci, fi
            planes = [(8 * kind + ci) // 6 for kind in range(3)]
            table[at, 2:5] = planes
            for kind in range(3):
                if planes[kind] == fi:
                    table[at, 5] = (8 * kind + ci) % 6
            for k in range(4):
                if k in planes:
                    table[at, 6 + k] = planes.index(k)
    ids = lax.dynamic_index_in_dim(jnp.asarray(table), c * 4 + f, 0, keepdims=False)

    own = tokens.reshape(256, width)
    cot = cotangent.reshape(256, width)
    vectors_in = [ln1_gain, ln1_shift, out_bias, ln2_gain, ln2_shift, down_bias, qkv_bias, up_bias]
    vectors_in = [doc_ids.reshape(2, 128)] + vectors_in
    hbm = pl.BlockSpec(memory_space=pltpu.HBM)
    outs = [shaped((272, width), BF16), shaped((176, width), BF16), shaped((256, width), BF16)]
    sizes = [(size, width) for size in (256, 128, 32, 128, 128)]
    chunk, pack, piece = pl.pallas_call(
        prepare_kernel,
        out_shape=outs,
        in_specs=[pl.BlockSpec(memory_space=pltpu.SMEM)] + [hbm] * 14,
        out_specs=[pl.BlockSpec(memory_space=pltpu.VMEM)] * 3,
        scratch_shapes=[pltpu.VMEM(size, BF16) for size in sizes]
        + [pltpu.VMEM(x.shape, x.dtype) for x in vectors_in]
        + [pltpu.SemaphoreType.DMA((14,))],
        compiler_params=pltpu.CompilerParams(vmem_limit_bytes=58 * 1024 * 1024),
        cost_estimate=pl.CostEstimate(flops=0, bytes_accessed=0, transcendentals=0),
    )(ids, own, qkv_weight, out_weight, up_weight, down_weight, *vectors_in)
    packs = [pack] + [shift(pack, k) for k in (1, 2, 3)]
    w_heads, par, out_rows = kernel_call(
        unpack_kernel,
        [shaped((384, width), BF16), shaped((16, width), F32), shaped((128, width), BF16)],
        [ids, *packs],
        [pltpu.VMEM((4, 16, width), F32)],
        cost=3,
    )
    chunks = spread_relayed(chunk, 128, par)

    heads = shaped((2, 2048, 128), BF16)
    q_one, keys, values, docs, h_one = kernel_call(
        project_kernel,
        [heads, heads, heads, shaped((16, 128), F32), shaped((2, 4, 256, width), BF16)],
        [ids, alibi_slopes, *chunks, w_heads, par],
        scalars=2,
        spare=12,
        cost=0,
    )
    out_near = [out_rows] + [swap(out_rows, d) for d in (2, 4, 6)]
    far_piece = shift(after(piece, packs), 2)
    w_heads_far = swap(w_heads, 1)
    pieces_of_heads = [shaped((512, 128), BF16)] * 4

    def swap_heads(parts):
        got = [parts[0]] + [swap(parts[e], 2 * e) for e in (1, 2, 3)]
        far = kernel_call(heads_far_kernel, [shaped((4, 256, 128), BF16)], got, scalars=0)[0]
        return [*got, swap(far, 1)], far

    q_two, full, *mixed_parts = kernel_call(
        attend_kernel,
        [heads, shaped((2048, 128), F32), *pieces_of_heads],
        [ids, docs, q_one, keys, values],
        [pltpu.VMEM((8, 256, 128), BF16), pltpu.VMEM((2, 8, TILE, TILE), F32)],
        spare=14,
        cost=20,
    )
    cot_near = pair(after(cot, full))
    mixed_parts = after(mixed_parts, out_near)
    out_pieces = [t for v in out_near for t in (v, swap(after(v, full), 1))]
    mixed_in, mixed_far = swap_heads(mixed_parts)
    far_piece = after(far_piece, mixed_far)
    rows = shaped((256, width), BF16)
    full_rows = shaped((256, width), F32)
    w_out, mixed, resid, h_two = kernel_call(
        branch_kernel,
        [shaped((width, width), BF16), rows, full_rows, rows],
        [ids, chunk, *mixed_in, par, *out_pieces],
        tied=[w_heads_far, cot_near],
        cost=5,
    )
    h_near = pair(h_two)
    up_row = up_bias.astype(F32).reshape(1, width)

    def feed(h, cots):
        return kernel_call(
            feed_kernel,
            [rows, rows, full_rows, full_rows],
            [h, cots, up_weight, up_row, down_weight],
            scalars=0,
            spare=8,
            cost=5,
        )

    def feed_other(h, cots, accs):
        return kernel_call(
            feed_other_kernel,
            [rows, rows, rows, rows],
            [ids, h, cots, par, *accs, *far_pieces],
            [pltpu.VMEM((256, width), F32)] * 2
            + [pltpu.VMEM((width, width), BF16)] * 2
            + [pltpu.VMEM((8, width), F32)],
            spare=8,
            cost=5,
        )

    act_own, dup_own, *accs_own = feed(h_two, cot)
    far_pieces = spread_relayed(far_piece, 128, act_own)
    act_near, dup_near, *accs_near = feed(h_near, cot_near)
    act_near_far, dup_near_far, branch_near, dh_near = feed_other(h_near, cot_near, accs_near)
    dh_got = pair(dh_near)
    act_own_far, dup_own_far, branch_own, dh_own = feed_other(h_two, after(cot, dh_near), accs_own)
    big = shaped((4, 512, width), BF16)
    keep, send, up_sums = kernel_call(
        feed_weights_kernel,
        [big, big, shaped((16, width), F32)],
        [
            ids,
            h_two,
            h_near,
            cot,
            cot_near,
            dup_own,
            dup_near,
            act_own,
            act_near,
            dup_own_far,
            dup_near_far,
            act_own_far,
            act_near_far,
        ],
        [pltpu.VMEM((2, width, width), BF16)],
        spare=8,
        cost=10,
    )
    dresid, dbranch, *dmixed_parts, sums = kernel_call(
        middle_kernel,
        [full_rows, rows, *pieces_of_heads, shaped((8, width), F32)],
        [ids, dh_own, dh_got, resid, cot, par, w_out],
        [pltpu.VMEM((256, width), BF16)],
        cost=40,
    )
    send = swap(send, 1)
    dmixed_heads, _ = swap_heads(after(dmixed_parts, send))

    def shape(*size):
        return shaped((*size, width), BF16)

    def relay(own_part, x_part, y_part):
        from_x, from_y = swap(x_part, 2), swap(y_part, 4)
        half = own_part.shape[0] // 4
        kept, x_next, y_next = kernel_call(
            relay_kernel,
            [shape(2 * half), shape(half), shape(half)],
            [own_part, from_x, from_y],
            scalars=0,
        )
        return kept, swap(y_next, 4), swap(x_next, 2)

    out_keep, out_send = kernel_call(
        out_weights_kernel,
        [shape(4, 128), shape(4, 128)],
        [ids, dbranch, mixed],
        [pltpu.VMEM((width, width), BF16)],
    )
    x_part, y_part, own_part = kernel_call(
        pair_sum_kernel,
        [shape(640), shape(640), shape(1280)],
        [keep, send, out_keep, swap(out_send, 1)],
        scalars=0,
    )
    feed_kept = relay(own_part, x_part, y_part)
    feed_near, feed_far, out_next, out_last = kernel_call(
        owned_kernel,
        [shape(288), shape(288), shape(32), shape(32)],
        [ids, *feed_kept],
        [pltpu.VMEM((128, width), BF16)],
    )
    branch_got = pair(after(branch_near, dh_got))
    layer_out = kernel_call(
        layer_out_kernel, [rows], [resid, par, branch_own, branch_got], scalars=0
    )[0]

    blocks = shaped((4, 256, 384), BF16)
    near, send = kernel_call(
        attend_back_kernel,
        [blocks, blocks],
        [ids, docs, q_two, keys, values, full, *dmixed_heads],
        [
            pltpu.VMEM((2, 2048, 128), BF16),
            *[pltpu.VMEM((2, 2048, 128), F32)] * 3,
            pltpu.VMEM((8, 256, 128), BF16),
        ],
        spare=14,
        cost=40,
        tied=[own_part, branch_got],
    )
    far = swap(send, 1)
    wsum = kernel_call(
        head_weights_kernel,
        [shaped((384, width), F32)],
        [near, send, h_one],
        scalars=0,
    )[0]
    x_part, y_part, own_part, slots_kept, slots_sent = kernel_call(
        unproject_kernel,
        [shape(256), shape(256), shape(512), shape(288), shape(288)],
        [
            ids,
            *chunks[0::2],
            near,
            far,
            send,
            w_heads,
            w_heads_far,
            par,
            sums,
            up_sums,
            wsum,
        ],
        [pltpu.VMEM((4, 144, width), BF16), pltpu.VMEM((4, 16, width), F32)],
        spare=8,
    )
    slots_near, slots_far = kernel_call(
        slots_kernel,
        [shape(144), shape(144)],
        [slots_kept, pair(slots_sent)],
        scalars=0,
        tied=[feed_kept[0]],
    )
    share_sums = relay(own_part, x_part, y_part)
    input_grad = kernel_call(
        input_kernel, [rows], [*share_sums, chunk, par, dresid], scalars=0, cost=10
    )[0]
    slot_sum = kernel_call(
        sum_kernel,
        [shape(144)],
        [slots_near, shift(slots_far, 2)],
        scalars=0,
        tied=[share_sums[0]],
    )[0]
    last_pieces = spread(slot_sum)
    feed_sum = kernel_call(
        feed_sum_kernel,
        [shape(288)],
        [feed_near, shift(feed_far, 2), shift(out_next, 1), shift(out_last, 3)],
        scalars=0,
        tied=[*last_pieces[2::2], input_grad],
    )[0]
    sizes = [256] * 6 + [1024, 512]
    qkv_grad, *vectors = kernel_call(
        last_grads_kernel,
        [shaped((768, width), F32), *(shaped((1, size), F32) for size in sizes)],
        [ids, *last_pieces],
        spare=14,
        cost=10,
    )
    feed_parts = spread_relayed(feed_sum, 144)
    vmem, hbm = pl.BlockSpec(memory_space=pltpu.VMEM), pl.BlockSpec(memory_space=pltpu.HBM)

    def write(body, parts, count, before, cost):
        return pl.pallas_call(
            body,
            out_shape=[shaped((width, width), F32)] * 2 + [shaped((256, width), F32)],
            in_specs=[pl.BlockSpec(memory_space=pltpu.SMEM)]
            + [vmem] * len(parts)
            + [hbm] * len(before),
            out_specs=[hbm] * 3,
            input_output_aliases={1 + len(parts) + i: i for i in range(len(before))},
            scratch_shapes=[
                pltpu.VMEM((count, 288, width), F32),
                pltpu.SemaphoreType.DMA((3 * count,)),
            ],
            compiler_params=pltpu.CompilerParams(vmem_limit_bytes=16 * 1024 * 1024),
            cost_estimate=pl.CostEstimate(
                flops=int(cost * 1e9), bytes_accessed=0, transcendentals=0
            ),
        )(ids, *parts, *before)

    body = functools.partial(feed_grads_kernel, count=6, first=0)
    grads = write(body, feed_parts[:6], 6, [], 10)
    tails = [*feed_parts[6], *feed_parts[7]]
    up_grad, down_grad, out_grad = write(feed_grads_last_kernel, tails, 2, grads, 0)
    g1, s1, ob, g2, s2, db, ub, bias_grad = (v.reshape(v.shape[1]) for v in vectors)
    return (
        layer_out.reshape(tokens.shape),
        input_grad.reshape(tokens.shape),
        g1,
        s1,
        qkv_grad,
        bias_grad,
        out_grad,
        ob,
        g2,
        s2,
        up_grad,
        ub,
        down_grad,
        db,
    )


def on_small_slice(mesh, tokens, slopes):
    return (
        mesh.shape["ctx"] == 8
        and mesh.shape["fsdp"] == 4
        and tokens.shape == (4, 2, 1024, 1024)
        and slopes.shape == (16,)
    )


def solution(mesh):
    in_specs = (
        P("fsdp", None, "ctx", None),
        P("fsdp", None, "ctx"),
        P(),
        P("fsdp"),
        P("fsdp"),
        P("fsdp", None),
        P("fsdp"),
        P("fsdp", None),
        P("fsdp"),
        P("fsdp"),
        P("fsdp"),
        P("fsdp", None),
        P("fsdp"),
        P("fsdp", None),
        P("fsdp"),
        P("fsdp", None, "ctx", None),
    )
    out_specs = (
        P("fsdp", None, "ctx", None),
        P("fsdp", None, "ctx", None),
        P("fsdp"),
        P("fsdp"),
        P("fsdp", None),
        P("fsdp"),
        P("fsdp", None),
        P("fsdp"),
        P("fsdp"),
        P("fsdp"),
        P("fsdp", None),
        P("fsdp"),
        P("fsdp", None),
        P("fsdp"),
    )
    def layer(*args):
        body = per_device if on_small_slice(mesh, args[0], args[2]) else gathered_device
        return jax.shard_map(
            body, mesh=mesh, in_specs=in_specs, out_specs=out_specs, check_vma=False
        )(*args)

    return layer
```

```python
import functools

import jax
import jax.numpy as jnp
import numpy as np
from jax import lax
from jax.experimental import pallas as pl
from jax.experimental.pallas import tpu as pltpu
from jax.sharding import PartitionSpec as P

EPS = 1e-05
MASKED = -1e30


def layer_norm(v, gain, shift):
    mean = jnp.mean(v, axis=-1, keepdims=True)
    centered = v - mean
    spread = jnp.mean(centered * centered, axis=-1, keepdims=True)
    return centered * lax.rsqrt(spread + EPS) * gain + shift


def gelu_tanh(v):
    return jax.nn.gelu(v, approximate=True)


def project_rows(values_in, weight):
    return lax.dot_general(
        values_in, weight, (((1,), (1,)), ((), ())), preferred_element_type=jnp.float32
    )


def cross_rows(left, right):
    return lax.dot_general(
        left, right, (((0,), (0,)), ((), ())), preferred_element_type=jnp.float32
    )


def token_positions(index, half_block, seq_len):
    owner = index // (2 * half_block)
    inside = index % (2 * half_block)
    return jnp.where(
        inside < half_block,
        owner * half_block + inside,
        seq_len - 1 - (owner * half_block + inside - half_block),
    )


def score_block(query3, keys3, query_pos, query_doc, key_pos, key_doc, slopes, scale):
    raw = jnp.einsum("qhe,khe->hqk", query3, keys3, preferred_element_type=jnp.float32) * scale
    distance = (query_pos[:, None] - key_pos[None, :]).astype(jnp.float32)
    scores = raw - slopes[:, None, None] * distance[None]
    allowed = ((key_pos[None, :] <= query_pos[:, None]) & (key_doc[None, :] == query_doc[:, None]))[
        None
    ]
    return (jnp.where(allowed, scores, MASKED), allowed)


def block_loop(total, size, visit, state):

    def turn_body(turn, inner):
        return visit(inner, turn * size, size)

    return lax.fori_loop(0, total // size, turn_body, state)


def gathered_device(
    tokens,
    doc_ids,
    alibi_slopes,
    ln1_gain,
    ln1_shift,
    qkv_weight,
    qkv_bias,
    out_weight,
    out_bias,
    ln2_gain,
    ln2_shift,
    up_weight,
    up_bias,
    down_weight,
    down_bias,
    cotangent,
):
    half_block = tokens.shape[2]
    width = tokens.shape[3]
    count = 2 * half_block
    heads = alibi_slopes.shape[0]
    head = width // heads
    scale = head ** (-0.5)
    seq_len = count * lax.axis_size("ctx")
    rows_in = tokens.reshape(count, width).astype(jnp.float32)
    doc_rows = doc_ids.reshape(count)
    grad_low = cotangent.reshape(count, width)
    grad_full = grad_low.astype(jnp.float32)
    own_pos = token_positions(
        lax.axis_index("ctx") * count + jnp.arange(count, dtype=jnp.int32), half_block, seq_len
    )
    gain_one, shift_one, w_qkv, b_qkv, w_out, b_out, gain_two, shift_two, b_down = (
        lax.all_gather(ln1_gain, "fsdp", axis=0, tiled=True),
        lax.all_gather(ln1_shift, "fsdp", axis=0, tiled=True),
        lax.all_gather(qkv_weight, "fsdp", axis=0, tiled=True),
        lax.all_gather(qkv_bias, "fsdp", axis=0, tiled=True),
        lax.all_gather(out_weight, "fsdp", axis=0, tiled=True),
        lax.all_gather(out_bias, "fsdp", axis=0, tiled=True),
        lax.all_gather(ln2_gain, "fsdp", axis=0, tiled=True),
        lax.all_gather(ln2_shift, "fsdp", axis=0, tiled=True),
        lax.all_gather(down_bias, "fsdp", axis=0, tiled=True),
    )
    norm_one, norm_one_pull = jax.vjp(
        layer_norm, rows_in, gain_one.astype(jnp.float32), shift_one.astype(jnp.float32)
    )
    h_one = norm_one.astype(jnp.bfloat16)
    joined = project_rows(h_one, w_qkv)
    bias_full = b_qkv.astype(jnp.float32)
    query = (joined[:, :width] + bias_full[:width]).astype(jnp.bfloat16)
    keys = joined[:, width : 2 * width].astype(jnp.bfloat16)
    values = (joined[:, 2 * width :] + bias_full[width:]).astype(jnp.bfloat16)
    query3 = query.reshape(count, heads, head)
    keys3 = keys.reshape(count, heads, head)
    values3 = values.reshape(count, heads, head)
    doc_all = lax.all_gather(doc_rows, "ctx", axis=0, tiled=True)
    start_state = (
        jnp.full((heads, count), MASKED, jnp.float32),
        jnp.zeros((heads, count), jnp.float32),
        jnp.zeros((count, heads, head), jnp.float32),
    )
    key_piece = lax.all_gather(keys, "ctx", axis=0, tiled=True)
    value_piece = lax.all_gather(values, "ctx", axis=0, tiled=True)

    def visit(state, offset, size):
        top, total, accum = state
        key_part = lax.dynamic_slice_in_dim(key_piece, offset, size).reshape(size, heads, head)
        value_part = lax.dynamic_slice_in_dim(value_piece, offset, size).reshape(size, heads, head)
        key_pos = token_positions(offset + jnp.arange(size, dtype=jnp.int32), half_block, seq_len)
        key_doc = lax.dynamic_slice_in_dim(doc_all, offset, size)
        scores, allowed = score_block(
            query3, key_part, own_pos, doc_rows, key_pos, key_doc, alibi_slopes, scale
        )
        new_top = jnp.maximum(top, jnp.max(scores, axis=2))
        weights = jnp.where(allowed, jnp.exp(scores - new_top[:, :, None]), 0.0)
        factor = jnp.exp(top - new_top)
        total = total * factor + jnp.sum(weights, axis=2)
        accum = accum * jnp.transpose(factor)[:, :, None] + jnp.einsum(
            "hqk,khe->qhe",
            weights.astype(jnp.bfloat16),
            value_part,
            preferred_element_type=jnp.float32,
        )
        return (new_top, total, accum)

    top, total, accum = block_loop(key_piece.shape[0], 512, visit, start_state)
    log_total = top + jnp.log(total)
    attended = accum / jnp.transpose(total)[:, :, None]
    mixed = attended.reshape(count, width).astype(jnp.bfloat16)
    resid = rows_in + project_rows(mixed, w_out) + b_out.astype(jnp.float32)
    norm_two, norm_two_pull = jax.vjp(
        layer_norm, resid, gain_two.astype(jnp.float32), shift_two.astype(jnp.float32)
    )
    h_two = norm_two.astype(jnp.bfloat16)
    w_up, b_up, w_down = (
        lax.all_gather(up_weight, "fsdp", axis=0, tiled=True),
        lax.all_gather(up_bias, "fsdp", axis=0, tiled=True),
        lax.all_gather(down_weight, "fsdp", axis=0, tiled=True),
    )
    up = project_rows(h_two, w_up) + b_up.astype(jnp.float32)
    act, gelu_pull = jax.vjp(gelu_tanh, up)
    act_low = act.astype(jnp.bfloat16)
    branch = jnp.dot(act_low, w_down, preferred_element_type=jnp.float32)
    layer_out = resid + branch + b_down.astype(jnp.float32)
    dup = gelu_pull(project_rows(grad_low, w_down))[0].astype(jnp.bfloat16)
    stacked = lax.psum_scatter(
        jnp.concatenate([cross_rows(dup, h_two), cross_rows(act_low, grad_low)], axis=1).astype(
            jnp.bfloat16
        ),
        "fsdp",
        scatter_dimension=0,
        tiled=True,
    ).astype(jnp.float32)
    up_rows_grad = stacked[:, :width]
    down_rows_grad = stacked[:, width:]
    up_bias_term = jnp.sum(dup, axis=0, dtype=jnp.float32)
    dnorm_two = jnp.dot(dup, w_up, preferred_element_type=jnp.float32)
    dresid_norm, gain_two_grad, shift_two_grad = norm_two_pull(dnorm_two)
    dresid = grad_full + dresid_norm
    dbranch = dresid.astype(jnp.bfloat16)
    out_bias_grad = jnp.sum(dbranch, axis=0, dtype=jnp.float32)
    out_weight_grad = cross_rows(dbranch, mixed)
    dmixed = jnp.dot(dbranch, w_out, preferred_element_type=jnp.float32).astype(jnp.bfloat16)
    dmixed3 = dmixed.reshape(count, heads, head)
    delta = jnp.transpose(jnp.sum(dmixed3.astype(jnp.float32) * attended, axis=2))
    query_key_piece = lax.all_gather(keys, "ctx", axis=0, tiled=True)
    query_value_piece = lax.all_gather(values, "ctx", axis=0, tiled=True)

    def visit(accum_grad, offset, size):
        key_part = lax.dynamic_slice_in_dim(query_key_piece, offset, size).reshape(
            size, heads, head
        )
        value_part = lax.dynamic_slice_in_dim(query_value_piece, offset, size).reshape(
            size, heads, head
        )
        key_pos = token_positions(offset + jnp.arange(size, dtype=jnp.int32), half_block, seq_len)
        key_doc = lax.dynamic_slice_in_dim(doc_all, offset, size)
        scores, allowed = score_block(
            query3, key_part, own_pos, doc_rows, key_pos, key_doc, alibi_slopes, scale
        )
        probs = jnp.where(allowed, jnp.exp(scores - log_total[:, :, None]), 0.0)
        dprobs = jnp.einsum("qhe,khe->hqk", dmixed3, value_part, preferred_element_type=jnp.float32)
        dscores = (probs * (dprobs - delta[:, :, None])).astype(jnp.bfloat16)
        return accum_grad + jnp.einsum(
            "hqk,khe->qhe", dscores, key_part, preferred_element_type=jnp.float32
        )

    query_sum = block_loop(
        query_key_piece.shape[0], 512, visit, jnp.zeros((count, heads, head), jnp.float32)
    )
    dquery = (query_sum * scale).reshape(count, width).astype(jnp.bfloat16)
    total_all, delta_all = (
        lax.all_gather(
            jnp.transpose(log_total).astype(jnp.bfloat16), "ctx", axis=0, tiled=True
        ).astype(jnp.float32),
        lax.all_gather(jnp.transpose(delta).astype(jnp.bfloat16), "ctx", axis=0, tiled=True).astype(
            jnp.float32
        ),
    )
    empty = jnp.zeros((count, heads, head), jnp.float32)
    query_piece = lax.all_gather(query, "ctx", axis=0, tiled=True)
    grad_piece = lax.all_gather(dmixed, "ctx", axis=0, tiled=True)

    def visit(state, offset, size):
        dkeys, dvalues = state
        query_part = lax.dynamic_slice_in_dim(query_piece, offset, size).reshape(size, heads, head)
        grad_part = lax.dynamic_slice_in_dim(grad_piece, offset, size).reshape(size, heads, head)
        query_pos = token_positions(offset + jnp.arange(size, dtype=jnp.int32), half_block, seq_len)
        query_doc = lax.dynamic_slice_in_dim(doc_all, offset, size)
        total_part = jnp.transpose(lax.dynamic_slice_in_dim(total_all, offset, size))
        delta_part = jnp.transpose(lax.dynamic_slice_in_dim(delta_all, offset, size))
        scores, allowed = score_block(
            query_part, keys3, query_pos, query_doc, own_pos, doc_rows, alibi_slopes, scale
        )
        probs = jnp.where(allowed, jnp.exp(scores - total_part[:, :, None]), 0.0)
        dvalues = dvalues + jnp.einsum(
            "hqk,qhe->khe",
            probs.astype(jnp.bfloat16),
            grad_part,
            preferred_element_type=jnp.float32,
        )
        dprobs = jnp.einsum("qhe,khe->hqk", grad_part, values3, preferred_element_type=jnp.float32)
        dscores = (probs * (dprobs - delta_part[:, :, None])).astype(jnp.bfloat16)
        dkeys = dkeys + jnp.einsum(
            "hqk,qhe->khe", dscores, query_part, preferred_element_type=jnp.float32
        )
        return (dkeys, dvalues)

    dkeys, dvalues = block_loop(query_piece.shape[0], 512, visit, (empty, empty))
    dkeys_low = (dkeys * scale).reshape(count, width).astype(jnp.bfloat16)
    dvalues_low = dvalues.reshape(count, width).astype(jnp.bfloat16)
    dfused = jnp.concatenate([dquery, dkeys_low, dvalues_low], axis=1)
    qkv_weight_grad = cross_rows(dfused, h_one)
    qkv_bias_grad = jnp.concatenate(
        [
            jnp.sum(dquery, axis=0, dtype=jnp.float32),
            jnp.sum(dvalues_low, axis=0, dtype=jnp.float32),
        ]
    )
    dnorm_one = jnp.dot(dfused, w_qkv, preferred_element_type=jnp.float32)
    dinput_norm, gain_one_grad, shift_one_grad = norm_one_pull(dnorm_one)
    input_grad = (dresid + dinput_norm).astype(jnp.bfloat16).reshape(tokens.shape)
    down_bias_grad = jnp.sum(grad_full, axis=0)
    shares = (
        lax.psum_scatter(
            qkv_weight_grad.astype(jnp.bfloat16), "fsdp", scatter_dimension=0, tiled=True
        ).astype(jnp.float32),
        lax.psum_scatter(
            out_weight_grad.astype(jnp.bfloat16), "fsdp", scatter_dimension=0, tiled=True
        ).astype(jnp.float32),
        lax.psum_scatter(
            qkv_bias_grad.astype(jnp.bfloat16), "fsdp", scatter_dimension=0, tiled=True
        ).astype(jnp.float32),
        lax.psum_scatter(
            out_bias_grad.astype(jnp.bfloat16), "fsdp", scatter_dimension=0, tiled=True
        ).astype(jnp.float32),
        lax.psum_scatter(
            gain_one_grad.astype(jnp.bfloat16), "fsdp", scatter_dimension=0, tiled=True
        ).astype(jnp.float32),
        lax.psum_scatter(
            shift_one_grad.astype(jnp.bfloat16), "fsdp", scatter_dimension=0, tiled=True
        ).astype(jnp.float32),
        lax.psum_scatter(
            gain_two_grad.astype(jnp.bfloat16), "fsdp", scatter_dimension=0, tiled=True
        ).astype(jnp.float32),
        lax.psum_scatter(
            shift_two_grad.astype(jnp.bfloat16), "fsdp", scatter_dimension=0, tiled=True
        ).astype(jnp.float32),
        lax.psum_scatter(
            up_bias_term.astype(jnp.bfloat16), "fsdp", scatter_dimension=0, tiled=True
        ).astype(jnp.float32),
        lax.psum_scatter(
            down_bias_grad.astype(jnp.bfloat16), "fsdp", scatter_dimension=0, tiled=True
        ).astype(jnp.float32),
    )
    totals = (
        lax.psum(shares[0].astype(jnp.bfloat16), "ctx").astype(jnp.float32),
        lax.psum(shares[1].astype(jnp.bfloat16), "ctx").astype(jnp.float32),
        lax.psum(up_rows_grad.astype(jnp.bfloat16), "ctx").astype(jnp.float32),
        lax.psum(down_rows_grad.astype(jnp.bfloat16), "ctx").astype(jnp.float32),
        lax.psum(shares[2].astype(jnp.bfloat16), "ctx").astype(jnp.float32),
        lax.psum(shares[3].astype(jnp.bfloat16), "ctx").astype(jnp.float32),
        lax.psum(shares[4].astype(jnp.bfloat16), "ctx").astype(jnp.float32),
        lax.psum(shares[5].astype(jnp.bfloat16), "ctx").astype(jnp.float32),
        lax.psum(shares[6].astype(jnp.bfloat16), "ctx").astype(jnp.float32),
        lax.psum(shares[7].astype(jnp.bfloat16), "ctx").astype(jnp.float32),
        lax.psum(shares[8].astype(jnp.bfloat16), "ctx").astype(jnp.float32),
        lax.psum(shares[9].astype(jnp.bfloat16), "ctx").astype(jnp.float32),
    )
    return (
        layer_out.astype(jnp.bfloat16).reshape(tokens.shape),
        input_grad,
        totals[6],
        totals[7],
        totals[0],
        totals[4],
        totals[1],
        totals[5],
        totals[8],
        totals[9],
        totals[2],
        totals[10],
        totals[3],
        totals[11],
    )

F32 = jnp.float32
BF16 = jnp.bfloat16
LOG2E = 1.4426950408889634
LN2 = 0.6931471805599453
TILE = 256
DOC_LANES = 48
BACKWARD_ENDS = {j: (3, 7) if j < 3 else (7,) for j in range(8)}
GELU_A = 0.7978845608028654
GELU_B = 0.044715


def dot_nt(a, b):
    return lax.dot_general(a, b, (((1,), (1,)), ((), ())), preferred_element_type=F32)


def dot_nn(a, b):
    return lax.dot_general(a, b, (((1,), (0,)), ((), ())), preferred_element_type=F32)


def dot_tn(a, b):
    return lax.dot_general(a, b, (((0,), (0,)), ((), ())), preferred_element_type=F32)


def kernel_call(body, outs, ins, scratch=(), scalars=1, tied=(), spare=7, cost=0):
    groups = [x if isinstance(x, tuple) else (x,) for x in ins[scalars:]]
    flat = [x for group in groups for x in group]
    joined = [
        pltpu.VMEM((sum(x.shape[0] for x in group), *group[0].shape[1:]), group[0].dtype)
        for group in groups
        if len(group) > 1
    ]
    scratch = [*joined, *scratch]
    room = sum(int(np.prod(x.shape)) * jnp.dtype(x.dtype).itemsize for x in scratch)

    def run(*refs):
        numbers, refs = refs[:scalars], refs[scalars:]
        sources, refs = refs[: len(flat)], refs[len(flat) + len(tied) :]
        targets, refs = refs[: len(outs)], refs[len(outs) :]
        places, refs = list(refs[: len(joined)]), refs[len(joined) :]
        held, at = [], 0
        for group in groups:
            if len(group) == 1:
                held.append(sources[at])
            else:
                held.append(places.pop(0))
                row = 0
                for source in sources[at : at + len(group)]:
                    held[-1][row : row + source.shape[0], :] = source[...]
                    row += source.shape[0]
            at += len(group)
        body(*numbers, *held, *targets, *refs)

    vmem = pl.BlockSpec(memory_space=pltpu.VMEM)
    return pl.pallas_call(
        run,
        out_shape=list(outs),
        in_specs=[pl.BlockSpec(memory_space=pltpu.SMEM)] * scalars
        + [vmem] * len(flat)
        + [pl.BlockSpec(memory_space=pl.ANY)] * len(tied),
        out_specs=[vmem] * len(outs),
        scratch_shapes=scratch,
        compiler_params=pltpu.CompilerParams(vmem_limit_bytes=room + spare * 1024 * 1024),
        cost_estimate=pl.CostEstimate(
            flops=int(cost * 1e9), bytes_accessed=0, transcendentals=0
        ),
    )(*ins[:scalars], *flat, *tied)


def shaped(shape, dtype):
    return jax.ShapeDtypeStruct(shape, dtype)


def lanes_of(shape):
    return lax.broadcasted_iota(jnp.int32, shape, len(shape) - 1)


def three_pieces(v):
    high = v.astype(BF16).astype(F32)
    mid = (v - high).astype(BF16).astype(F32)
    return high, mid, v - high - mid


def normed(v):
    mean = jnp.mean(v, axis=-1, keepdims=True)
    centered = v - mean
    spread = jnp.mean(centered * centered, axis=-1, keepdims=True)
    root = lax.rsqrt(spread + EPS)
    return centered * root, root


def norm_back(dout, unit, root, gain):
    dn = dout * gain
    first = jnp.mean(dn, axis=-1, keepdims=True)
    second = jnp.mean(dn * unit, axis=-1, keepdims=True)
    return root * (dn - first - unit * second)


def block_rows(index, half_block):
    return pl.ds(pl.multiple_of(index * half_block, half_block), half_block)


def prepare_kernel(ids, *refs):
    own, w_ref, out_ref, up_ref, down_ref = refs[0:5]
    vectors, (chunk, pack, piece), places, sems = refs[5:14], refs[14:17], refs[17:31], refs[31]
    c = ids[0]

    def rows(ref, start, count):
        return ref.at[pl.ds(pl.multiple_of(start * count, count), count)]

    sources = [
        own,
        rows(w_ref, ids[5], 128),
        rows(out_ref, c, 32),
        rows(up_ref, c, 128),
        rows(down_ref, c, 128),
        *vectors,
    ]
    copies = [
        pltpu.make_async_copy(a, b, sems.at[i]) for i, (a, b) in enumerate(zip(sources, places))
    ]
    for copy in copies:
        copy.start()
    for copy in copies:
        copy.wait()
    doc, g1, s1, ob, g2, s2, db, qb, ub = places[5:]
    docs = doc[...].astype(F32)
    row = jnp.concatenate([docs[0:1], docs[1:2]], axis=1)
    chunk[256:272, :] = jnp.zeros((16, 1024), BF16)
    chunk[256:272, 0:256] = jnp.broadcast_to(row, (16, 256)).astype(BF16)

    def wide(ref):
        size = ref.shape[0]
        return jnp.broadcast_to(ref[...].astype(F32).reshape(1, size), (8, size))

    first = jnp.concatenate([wide(r) for r in (g1, s1, ob, g2)], axis=1)
    at = lax.broadcasted_iota(jnp.int32, (8, 1024), 0)
    first = jnp.where(at < 4, first, wide(ub))
    second = jnp.concatenate([wide(r) for r in (s2, db, qb)], axis=1)
    small = jnp.concatenate([first, second], axis=0).astype(BF16)
    chunk[0:256, :] = places[0][...]
    pack[0:128, :] = places[1][...]
    pack[128:144, :] = small
    pack[144:176, :] = places[2][...]
    piece[0:128, :] = places[3][...]
    piece[128:256, :] = places[4][...]


def unpack_kernel(ids, p0, p1, p2, p3, w_out, par_out, out_rows, small):
    packs = (p0, p1, p2, p3)
    f = ids[1]
    for k in range(4):
        plane = lax.rem(f + (4 - k), 4)
        small[plane] = packs[k][128:144, :].astype(F32)
        at = pl.multiple_of(plane * 32, 32)
        out_rows[pl.ds(at, 32), :] = packs[k][144:176, :]
        for kind in range(3):

            @pl.when(ids[2 + kind] == plane)
            def _():
                w_out[kind * 128 : (kind + 1) * 128, :] = packs[k][0:128, :]

    rows = [small[p] for p in range(4)]

    def whole(row, start, stop, planes=(0, 1, 2, 3)):
        return jnp.concatenate([rows[p][row * 8 : row * 8 + 1, start:stop] for p in planes], axis=1)

    par_out[0:1, :] = whole(0, 0, 256)
    par_out[1:2, :] = whole(0, 256, 512)
    par_out[2:3, :] = whole(0, 512, 768)
    par_out[3:4, :] = whole(0, 768, 1024)
    par_out[4:5, :] = whole(1, 0, 256)
    par_out[5:6, :] = whole(1, 256, 512)
    par_out[6:7, :] = whole(1, 512, 1024, (0, 1))
    par_out[7:8, :] = whole(1, 512, 1024, (2, 3))
    par_out[8:16, :] = small[f ^ 2][0:8, :]
    par_out[8:9, :] = small[f ^ 2][4:5, :]


def project_kernel(ids, slopes, *refs):
    chunks, (w_ref, par_out, q_out, k_out, v_out, doc_out, h_out) = refs[:8], refs[8:]
    c = ids[0]
    mine = pl.ds(pl.multiple_of(c * 128, 128), 128)
    bias_q = par_out[6:7, mine]
    bias_v = par_out[7:8, mine]
    gain, shift = par_out[0:1, :], par_out[1:2, :]
    weight = w_ref[...]
    lane = lanes_of((256, 128))
    row = lax.broadcasted_iota(jnp.int32, (256, 128), 0)
    eye = (
        lax.broadcasted_iota(jnp.int32, (128, 128), 0) == lanes_of((128, 128))
    ).astype(BF16)
    sub = lax.broadcasted_iota(jnp.int32, (128, 256), 0).astype(F32) - 67.0
    is_doc = (lane >= 67) & (lane < 67 + DOC_LANES)
    low = lane < 64
    for d in range(8):
        cc = c ^ d
        h = (normed(chunks[d][0:256, :].astype(F32))[0] * gain + shift).astype(BF16)
        h_out[d % 2, d // 2] = h
        joined = dot_nt(h, weight)
        query = (joined[:, 0:128] + bias_q) * (LOG2E * 0.125)
        keys = joined[:, 128:256]
        values = joined[:, 256:384] + bias_v
        doc_row = chunks[d][256:272, 0:256].astype(F32)[0:1, :]
        doc_out[pl.ds(cc, 1), :] = doc_row[:, 0:128]
        doc_out[pl.ds(8 + cc, 1), :] = doc_row[:, 128:256]
        one_hot = dot_tn((sub == doc_row).astype(BF16), eye)
        pos = jnp.where(row < 128, cc * 128 + row, 2175 - cc * 128 - row).astype(F32)
        q_aug = jnp.where(lane < 67, 1.0, jnp.where(is_doc, one_hot, 0.0))
        k_tail = jnp.where(is_doc, (1.0 - one_hot) * MASKED, jnp.where(lane < 118, 1.0, 0.0))
        for hh in range(2):
            if hh == 1:
                query, keys, values = (pltpu.roll(t, 64, 1) for t in (query, keys, values))
            high, mid, rest = three_pieces(pos * (slopes[2 * c + hh] * LOG2E))
            k_aug = jnp.where(
                lane == 64, high, jnp.where(lane == 65, mid, jnp.where(lane == 66, rest, k_tail))
            )
            parts = (
                (q_out, jnp.where(low, query, q_aug).astype(BF16)),
                (k_out, jnp.where(low, keys, k_aug).astype(BF16)),
                (v_out, jnp.where(low, values, 1.0).astype(BF16)),
            )
            for ref, value in parts:
                ref[hh, block_rows(cc, 128), :] = value[0:128]
                ref[hh, block_rows(8 + cc, 128), :] = value[128:256]


def tile_start(i):
    return i * TILE if i < 4 else 1024 + (7 - i) * TILE


def tile_rows(i):
    start = jnp.where(i < 4, i * TILE, 1024 + (7 - i) * TILE)
    return pl.ds(pl.multiple_of(start, TILE), TILE)


def tile_docs(docs, i):
    at = tile_start(i) // 128
    return docs[at : at + 2, :]


def count_tiles(flags):
    total = jnp.sum(jnp.where(flags, 1.0, 0.0)).astype(jnp.int32)
    return lax.shift_right_logical(total, 8)


def span(first, last):
    out = []
    if first < 4 and first <= last:
        out.append(slice(first * TILE, (min(last, 3) + 1) * TILE))
    if last >= 4 and first <= last:
        out.append(slice(tile_start(last), tile_start(max(first, 4)) + TILE))
    return out


def attend_kernel(
    ids, docs_ref, q_ref, k_ref, v_ref, q_out, full_out, m0, m1, m2, m3, mixed_out, held
):
    docs = docs_ref[...]
    size = 2 * TILE
    lane = lanes_of((size, 128))
    low = lane < 64
    step_right = lanes_of((size, size)) - lax.broadcasted_iota(jnp.int32, (size, size), 0)

    def widest(scores):
        parts = [scores[:, at : at + 128] for at in range(0, size, 128)]
        return functools.reduce(jnp.maximum, parts)

    def rows_of(i):
        start = jnp.where(i < 2, i * size, 1024 + (3 - i) * size)
        return pl.ds(pl.multiple_of(start, size), size)

    def one_tile(i, carry):
        own = rows_of(i)
        at = jnp.where(i < 2, 4 * i, 8 + 4 * (3 - i))
        first = count_tiles(docs < jnp.min(docs_ref[pl.ds(at, 4), :]))
        first = lax.shift_right_logical(first, 1)
        allowed = jnp.where(i < 2, step_right, -step_right) <= 0
        queries = [q_ref[hh, own, :] for hh in range(2)]
        diagonal = [
            jnp.where(allowed, dot_nt(queries[hh], k_ref[hh, own, :]), MASKED) for hh in range(2)
        ]

        def look(j, tops):
            rows = rows_of(j)
            out = []
            for hh in range(2):
                scores = dot_nt(queries[hh], k_ref[hh, rows, :])
                held[hh, j] = scores
                out.append(jnp.maximum(tops[hh], widest(scores)))
            return tuple(out)

        tops = lax.fori_loop(first, i, look, tuple(widest(s) for s in diagonal))
        tops = [jnp.max(t, axis=1, keepdims=True) for t in tops]

        def gather(j, sums):
            rows = rows_of(j)
            out = []
            for hh in range(2):
                weights = jnp.exp2(held[hh, j] - tops[hh]).astype(BF16)
                out.append(sums[hh] + dot_nn(weights, v_ref[hh, rows, :]))
            return tuple(out)

        start = tuple(
            dot_nn(jnp.exp2(diagonal[hh] - tops[hh]).astype(BF16), v_ref[hh, own, :])
            for hh in range(2)
        )
        sums = lax.fori_loop(first, i, gather, start)
        outs = []
        for hh in range(2):
            total = sums[hh][:, 64:65]
            outs.append(sums[hh] / total)
            high, mid, rest = three_pieces(-(tops[hh] + jnp.log2(total)))
            tail = jnp.where(
                lane == 115,
                high,
                jnp.where(lane == 116, mid, jnp.where(lane == 117, rest, queries[hh].astype(F32))),
            )
            q_out[hh, own, :] = tail.astype(BF16)
        both = jnp.where(low, outs[0], pltpu.roll(outs[1], 64, 1))
        full_out[own, :] = both
        half = jnp.where(i < 2, 0, 128)
        chunk = jnp.where(i < 2, 4 * i, 4 * (3 - i))
        for piece in range(4):
            mixed_out[chunk + piece, pl.ds(pl.multiple_of(half, 128), 128), :] = both[
                piece * 128 : (piece + 1) * 128
            ].astype(BF16)
        return carry

    lax.fori_loop(0, 4, one_tile, 0)
    for e, ref in enumerate((m0, m1, m2, m3)):
        for parity in range(2):
            ref[parity * 256 : (parity + 1) * 256, :] = mixed_out[ids[0] ^ (2 * e + parity)]


def heads_far_kernel(g0, g1, g2, g3, out):
    for e, ref in enumerate((g0, g1, g2, g3)):
        out[e] = ref[256:512, :]


def attend_back_kernel(
    ids, docs_ref, q_ref, k_ref, v_ref, full_ref, g0, g1, g2, g3, g_far, keep, send, grads, dq, dk, dv, all_grads
):
    docs = docs_ref[...]
    lane = lanes_of((256, 128))
    low = lane < 64
    for e, ref in enumerate((g0, g1, g2, g3)):
        all_grads[ids[0] ^ (2 * e)] = ref[0:256, :]
        all_grads[ids[0] ^ (2 * e + 1)] = g_far[e]
    for at in range(8):
        piece = all_grads[at].astype(F32)
        other = jnp.concatenate(
            [
                full_ref[at * 128 : (at + 1) * 128, :],
                full_ref[1024 + at * 128 : 1024 + (at + 1) * 128, :],
            ],
            axis=0,
        )
        product = piece * other
        for hh in range(2):
            delta = jnp.sum(jnp.where(low == (hh == 0), product, 0.0), axis=1, keepdims=True)
            high, mid, rest = three_pieces(-delta)
            tail = jnp.where(
                lane == 64, high, jnp.where(lane == 65, mid, jnp.where(lane == 66, rest, 0.0))
            )
            moved = piece if hh == 0 else pltpu.roll(piece, 64, 1)
            value = jnp.where(low, moved, tail).astype(BF16)
            grads[hh, at * 128 : (at + 1) * 128, :] = value[0:128]
            grads[hh, 1024 + at * 128 : 1024 + (at + 1) * 128, :] = value[128:256]
    dq[...] = jnp.zeros_like(dq)
    down, right = lax.broadcasted_iota(jnp.int32, (TILE, TILE), 0), lanes_of((TILE, TILE))

    def run(j, last):
        own = slice(tile_start(j), tile_start(j) + TILE)
        allowed = (down <= right) if j < 4 else (down >= right)
        places = [own] + span(j + 1, last)

        def head(hh, carry):
            keys, values = k_ref[hh, own, :], v_ref[hh, own, :]
            dk_sum = dv_sum = 0.0
            for at, rows in enumerate(places):
                query, grad = q_ref[hh, rows, :], grads[hh, rows, :]
                probs = jnp.exp2(dot_nt(keys, query))
                if at == 0:
                    probs = jnp.where(allowed, probs, 0.0)
                dscores = (probs * dot_nt(values, grad)).astype(BF16)
                dq[hh, rows, :] += dot_tn(dscores, keys)
                dk_sum += dot_nn(dscores, query)
                dv_sum += dot_nn(probs.astype(BF16), grad)
            dk[hh, own, :] = dk_sum
            dv[hh, own, :] = dv_sum
            return carry

        lax.fori_loop(0, 2, head, 0)

    for j in range(8):
        ends = BACKWARD_ENDS[j]
        within = jnp.sum(jnp.where(docs <= jnp.max(tile_docs(docs, j)), 1.0, 0.0))
        last = lax.shift_right_logical(within.astype(jnp.int32) + (TILE - 1), 8) - 1
        for at, end in enumerate(ends):
            fits = last <= end
            if at:
                fits = fits & (last > ends[at - 1])
            if len(ends) == 1:
                run(j, end)
            else:
                pl.when(fits)(functools.partial(run, j, end))
    for j in range(4):
        for parity, ref in enumerate((keep, send)):
            cc = ids[0] ^ (2 * j + parity)
            for half in range(2):
                rows = block_rows(8 * half + cc, 128)
                at = slice(half * 128, (half + 1) * 128)
                for which, (held, scale) in enumerate(((dq, 0.125), (dk, LN2), (dv, 1.0))):
                    other = pltpu.roll(held[1, rows, :], 64, 1)
                    both = jnp.where(low[0:128], held[0, rows, :], other) * scale
                    ref[j, at, which * 128 : (which + 1) * 128] = both.astype(BF16)


def branch_kernel(ids, chunk, g0, g1, g2, g3, g_far, par, *refs):
    pieces, (w_out, mixed_out, resid_out, h_out) = refs[:8], refs[8:]
    for d in range(8):
        for plane in range(4):
            at = pl.multiple_of(plane * 256 + (ids[0] ^ d) * 32, 32)
            w_out[pl.ds(at, 32), :] = pieces[d][plane * 32 : (plane + 1) * 32, :]
    for e, ref in enumerate((g0, g1, g2, g3)):
        for parity, value in enumerate((ref[0:256, :], g_far[e])):
            at = pl.multiple_of((ids[0] ^ (2 * e + parity)) * 128, 128)
            mixed_out[:, pl.ds(at, 128)] = value
    resid = chunk[0:256, :].astype(F32) + dot_nt(mixed_out[...], w_out[...]) + par[2:3, :]
    resid_out[...] = resid
    h_out[...] = (normed(resid)[0] * par[3:4, :] + par[4:5, :]).astype(BF16)


def feed_step(h, cot, up_w, down_w, bias):
    u = dot_nt(h, up_w) + bias
    grad = dot_nt(cot, down_w)
    square = u * u
    th = jnp.tanh(GELU_A * u * (1.0 + GELU_B * square))
    half = 0.5 * (1.0 + th)
    act = (u * half).astype(BF16)
    slope = half + 0.5 * u * (1.0 - th * th) * (GELU_A * (1.0 + 3.0 * GELU_B * square))
    return act, (grad * slope).astype(BF16)


def feed_kernel(h_ref, cot_ref, up_ref, bias_ref, down_ref, act_out, dup_out, acc, dacc):
    acc[...] = jnp.zeros_like(acc)
    dacc[...] = jnp.zeros_like(dacc)

    def step(t, carry):
        at = pl.ds(pl.multiple_of(t * 256, 256), 256)
        up_w, down_w = up_ref[at, :], down_ref[at, :]
        act, dup = feed_step(h_ref[...], cot_ref[...], up_w, down_w, bias_ref[0:1, at])
        act_out[:, at] = act
        dup_out[:, at] = dup
        acc[...] += dot_nn(act, down_w)
        dacc[...] += dot_nn(dup, up_w)
        return carry

    lax.fori_loop(0, 4, step, 0)


def feed_other_kernel(ids, h_ref, cot_ref, par, acc_in, dacc_in, *refs):
    pieces, (act_out, dup_out, branch, dh, acc, dacc, ups, downs, bias) = refs[:8], refs[8:]
    for d in range(8):
        at = slice(d * 128, (d + 1) * 128)
        ups[at, :] = pieces[d][0:128, :]
        downs[at, :] = pieces[d][128:256, :]
        bias[0:1, at] = par[8:9, pl.ds(pl.multiple_of((ids[0] ^ d) * 128, 128), 128)]
    acc[...] = acc_in[...]
    dacc[...] = dacc_in[...]

    def step(t, carry):
        at = pl.ds(pl.multiple_of(t * 256, 256), 256)
        up_w, down_w = ups[at, :], downs[at, :]
        act, dup = feed_step(h_ref[...], cot_ref[...], up_w, down_w, bias[0:1, at])
        act_out[:, at] = act
        dup_out[:, at] = dup
        acc[...] += dot_nn(act, down_w)
        dacc[...] += dot_nn(dup, up_w)
        return carry

    lax.fori_loop(0, 4, step, 0)
    branch[...] = acc[...].astype(BF16)
    dh[...] = dacc[...].astype(BF16)


def middle_kernel(
    ids, d0, d1, resid_ref, cot_ref, par, w_ref, dresid_out, dbranch_out, m0, m1, m2, m3, sums, held
):
    dh = d0[...].astype(F32) + d1[...].astype(F32)
    unit, root = normed(resid_ref[...])
    cot = cot_ref[...].astype(F32)
    dresid = cot + norm_back(dh, unit, root, par[3:4, :])
    dresid_out[...] = dresid
    dbranch = dresid.astype(BF16)
    dbranch_out[...] = dbranch
    held[...] = dot_nn(dbranch, w_ref[...]).astype(BF16)
    for e, ref in enumerate((m0, m1, m2, m3)):
        for parity in range(2):
            at = pl.multiple_of((ids[0] ^ (2 * e + parity)) * 128, 128)
            ref[parity * 256 : (parity + 1) * 256, :] = held[:, pl.ds(at, 128)]
    sums[...] = jnp.zeros_like(sums)
    sums[0:1, :] = jnp.sum(dbranch.astype(F32), axis=0, keepdims=True)
    sums[1:2, :] = jnp.sum(dh * unit, axis=0, keepdims=True)
    sums[2:3, :] = jnp.sum(dh, axis=0, keepdims=True)
    sums[3:4, :] = jnp.sum(cot, axis=0, keepdims=True)


def feed_weights_kernel(ids, *refs):
    hs, cots, dups, acts, dups_far, acts_far = (refs[2 * i : 2 * i + 2] for i in range(6))
    keep, send, bias, all_rows = refs[12:]
    c = ids[0]

    def product(lefts, at, rights):
        return sum(dot_tn(a[:, at], b[...]) for a, b in zip(lefts, rights)).astype(BF16)

    for t in range(4):
        at = slice(t * 256, (t + 1) * 256)
        for which, (lefts, rights) in enumerate(((dups, hs), (acts, cots))):
            all_rows[which, at, :] = product(lefts, at, rights)
        for which, (lefts, rights) in enumerate(((dups_far, hs), (acts_far, cots))):
            both = product(lefts, at, rights)
            for parity, ref in enumerate((keep, send)):
                place = slice(256 + which * 128, 384 + which * 128)
                ref[t, place, :] = both[parity * 128 : (parity + 1) * 128]
    for e in range(4):
        for parity, ref in enumerate((keep, send)):
            rows = block_rows(c ^ (2 * e + parity), 128)
            ref[e, 0:128, :] = all_rows[0, rows, :]
            ref[e, 128:256, :] = all_rows[1, rows, :]

    def total(refs):
        return sum(jnp.sum(r[...].astype(F32), axis=0, keepdims=True) for r in refs)

    bias[0:1, :] = total(dups)
    far = total(dups_far)
    for d in range(8):
        at = pl.ds(pl.multiple_of((c ^ d) * 128, 128), 128)
        bias[8:9, at] = far[:, d * 128 : (d + 1) * 128]


def out_weights_kernel(ids, dbranch, mixed, keep, send, total):
    for t in range(4):
        at = slice(t * 256, (t + 1) * 256)
        total[at, :] = dot_tn(dbranch[:, at], mixed[...]).astype(BF16)
    for e in range(4):
        for parity, ref in enumerate((keep, send)):
            cc = ids[0] ^ (2 * e + parity)
            for plane in range(4):
                at = pl.multiple_of(plane * 256 + cc * 32, 32)
                ref[e, plane * 32 : (plane + 1) * 32, :] = total[pl.ds(at, 32), :]


def added(*values):
    return sum(v.astype(F32) for v in values).astype(BF16)


def pair_sum_kernel(keep, got, out_keep, out_got, x_out, y_out, own_out):
    def put(target, slot, e, part):
        rows = slice(256 * part, 256 * (part + 1))
        more = slice(64 * part, 64 * (part + 1))
        at = slot * 320
        target[at : at + 256, :] = added(keep[e, rows], got[e, rows])
        target[at + 256 : at + 320, :] = added(out_keep[e, more], out_got[e, more])

    put(x_out, 0, 1, 0)
    put(x_out, 1, 3, 0)
    put(y_out, 0, 2, 1)
    put(y_out, 1, 3, 1)
    put(own_out, 0, 0, 0)
    put(own_out, 1, 0, 1)
    put(own_out, 2, 2, 0)
    put(own_out, 3, 1, 1)


def relay_kernel(own, from_x, from_y, kept, x_out, y_out):
    half = own.shape[0] // 4
    kept[0:half, :] = added(own[0:half, :], from_x[0:half, :])
    y_out[...] = added(own[2 * half : 3 * half, :], from_x[half:, :])
    kept[half:, :] = added(own[half : 2 * half, :], from_y[0:half, :])
    x_out[...] = added(own[3 * half :, :], from_y[half:, :])


def owned_kernel(ids, kept, from_y, from_x, near, far, out_next, out_last, share):
    f = ids[1]
    near[0:256, :] = added(kept[0:256, :], from_y[0:256, :])
    far[0:256, :] = added(kept[320:576, :], from_x[0:256, :])
    share[0:64, :] = added(kept[256:320, :], from_y[256:320, :])
    share[64:128, :] = added(kept[576:640, :], from_x[256:320, :])
    for k, target in enumerate((near, out_next, far, out_last)):
        rows = pl.ds(pl.multiple_of(lax.rem(f + k, 4) * 32, 32), 32)
        if k % 2:
            target[...] = share[rows, :]
        else:
            target[256:288, :] = share[rows, :]


def feed_sum_kernel(near, far, out_next, out_last, out):
    out[0:256, :] = added(near[0:256, :], far[0:256, :])
    outs = (near[256:288, :], far[256:288, :], out_next[...], out_last[...])
    out[256:288, :] = added(*outs)


def slots_kernel(kept, got, near, far):
    near[...] = added(kept[0:144, :], got[0:144, :])
    far[...] = added(kept[144:288, :], got[144:288, :])


def sum_kernel(*refs):
    refs[-1][...] = added(*(r[...] for r in refs[:-1]))


def layer_out_kernel(resid, par, one, two, out):
    out[...] = (resid[...] + par[5:6, :] + one[...].astype(F32) + two[...].astype(F32)).astype(BF16)


def head_weights_kernel(keep, send, h_ref, total):
    for parity, ref in enumerate((keep, send)):
        for j in range(4):
            got = dot_tn(ref[j], h_ref[parity, j])
            if parity == 0 and j == 0:
                total[...] = got
            else:
                total[...] += got


def unproject_kernel(ids, *refs):
    chunks, (near, far, bias_far, w_near, w_far, par, sums, up_sums, wsum) = refs[:4], refs[4:13]
    x_out, y_out, own_out, slots_kept, slots_sent, slots, small = refs[13:]
    c, f = ids[0], ids[1]
    near_w, far_w = w_near[...], w_far[...]
    gain_grad = shift_grad = bias_grad = 0.0
    places = (
        (own_out, 0, own_out, 128),
        (x_out, 0, own_out, 384),
        (own_out, 256, y_out, 0),
        (x_out, 128, y_out, 128),
    )
    for e, chunk in enumerate(chunks):
        grads = near[e]
        unit = normed(chunk[0:256, :].astype(F32))[0]
        share = dot_nn(grads, near_w) + dot_nn(far[e], far_w)
        top, at, bottom, below = places[e]
        top[at : at + 128, :] = share[0:128].astype(BF16)
        bottom[below : below + 128, :] = share[128:256].astype(BF16)
        gain_grad += jnp.sum(share * unit, axis=0, keepdims=True)
        shift_grad += jnp.sum(share, axis=0, keepdims=True)
        bias_grad += jnp.sum(grads.astype(F32) + bias_far[e].astype(F32), axis=0, keepdims=True)
    small[...] = jnp.zeros_like(small)
    for p in range(4):
        at = slice(p * 256, (p + 1) * 256)
        small[p, 0:1, 0:256] = gain_grad[:, at]
        small[p, 0:1, 256:512] = shift_grad[:, at]
        small[p, 0:1, 512:768] = sums[0:1, at]
        small[p, 0:1, 768:1024] = sums[1:2, at]
        small[p, 1:2, 0:256] = sums[2:3, at]
        small[p, 1:2, 256:512] = sums[3:4, at]
        small[p, 1:2, 512:640] = bias_grad[:, 0:128] if p < 2 else bias_grad[:, 256:384]
        up_far = jnp.where(f == p ^ 2, up_sums[8:9, :], 0.0)
        small[p, 2:3, :] = jnp.where(f == p, up_sums[0:1, :], up_far)
        start = pl.multiple_of(ids[6 + p] * 128, 128)
        slots[p, 0:128, :] = wsum[pl.ds(start, 128), :].astype(BF16)
        slots[p, 128:144, :] = small[p].astype(BF16)
    for k in range(2):
        at = slice(k * 144, (k + 1) * 144)
        slots_kept[at, :] = slots[f ^ (2 * k)]
        slots_sent[at, :] = slots[f ^ (2 * k + 1)]


def input_kernel(kept, from_y, from_x, chunk, par, dresid, out):
    moved = jnp.concatenate([from_y[...], from_x[...]], axis=0)
    dh = kept[...].astype(F32) + moved.astype(F32)
    unit, root = normed(chunk[0:256, :].astype(F32))
    out[...] = (dresid[...] + norm_back(dh, unit, root, par[0:1, :])).astype(BF16)


def feed_grads_kernel(ids, *refs, count, first):
    pieces, (up_out, down_out, out_out, place, sems) = refs[:count], refs[-5:]
    copies = []
    for n, piece in enumerate(pieces):
        cc = ids[0] ^ (first + n)
        place[n] = piece[...].astype(F32)
        moves = (
            (place.at[n, 0:128], up_out.at[block_rows(cc, 128)]),
            (place.at[n, 128:256], down_out.at[block_rows(cc, 128)]),
            (place.at[n, 256:288], out_out.at[pl.ds(pl.multiple_of(cc * 32, 32), 32)]),
        )
        for i, (a, b) in enumerate(moves):
            copies.append(pltpu.make_async_copy(a, b, sems.at[3 * n + i]))
            copies[-1].start()
    for copy in copies:
        copy.wait()


def feed_grads_last_kernel(ids, t0, b0, t1, b1, *refs):
    pieces, place = (t0, b0, t1, b1), refs[-2]
    up_out, down_out, out_out, sems = *refs[-5:-2], refs[-1]
    copies = []
    for n in range(2):
        cc = ids[0] ^ (6 + n)
        place[n, 0:144] = pieces[2 * n][...].astype(F32)
        place[n, 144:288] = pieces[2 * n + 1][...].astype(F32)
        moves = (
            (place.at[n, 0:128], up_out.at[block_rows(cc, 128)]),
            (place.at[n, 128:256], down_out.at[block_rows(cc, 128)]),
            (place.at[n, 256:288], out_out.at[pl.ds(pl.multiple_of(cc * 32, 32), 32)]),
        )
        for i, (a, b) in enumerate(moves):
            copies.append(pltpu.make_async_copy(a, b, sems.at[3 * n + i]))
            copies[-1].start()
    for copy in copies:
        copy.wait()


def last_grads_kernel(ids, *refs):
    pieces, (qkv_out, g1, s1, ob, g2, s2, db, ub, bias_out) = refs[:8], refs[8:]
    c, f = ids[0], ids[1]
    total = 0.0
    for d in range(8):
        cc = c ^ d
        place = lax.rem(cc + 24 - 6 * f, 8)

        @pl.when(place < 6)
        def _():
            qkv_out[block_rows(place, 128), :] = pieces[d][0:128, :].astype(F32)

        rows = pieces[d][128:144, :].astype(F32)
        total += rows

        @pl.when(lax.div(cc, 4) == lax.rem(f, 2))
        def _():
            at = pl.multiple_of(lax.rem(cc, 4) * 128, 128)
            bias_out[0:1, pl.ds(at, 128)] = rows[1:2, 512:640]

    for ref, row, start in ((g1, 0, 0), (s1, 0, 256), (ob, 0, 512), (g2, 0, 768), (s2, 1, 0), (db, 1, 256)):
        ref[...] = total[row : row + 1, start : start + 256]
    ub[...] = total[2:3, :]


def per_device(
    tokens,
    doc_ids,
    alibi_slopes,
    ln1_gain,
    ln1_shift,
    qkv_weight,
    qkv_bias,
    out_weight,
    out_bias,
    ln2_gain,
    ln2_shift,
    up_weight,
    up_bias,
    down_weight,
    down_bias,
    cotangent,
):
    c, f = lax.axis_index("ctx"), lax.axis_index("fsdp")
    width = 1024

    def swap(v, d):
        return lax.ppermute(v, "ctx", [(i, i ^ d) for i in range(8)])

    def shift(v, k):
        return lax.ppermute(v, "fsdp", [(i, (i + k) % 4) for i in range(4)])

    def pair(v):
        return lax.ppermute(v, "fsdp", [(i, i ^ 1) for i in range(4)])

    def after(value, *earlier):
        return lax.optimization_barrier((value, earlier))[0]

    def spread(v):
        near = [v] + [swap(v, d) for d in (2, 4, 6)]
        return [t for e in near for t in (e, swap(e, 1))]

    def spread_relayed(v, cut, *earlier):
        from_x, from_y = swap(v, 2), swap(v, 4)
        top, bottom = swap(from_x[:cut], 4), swap(from_y[cut:], 2)
        kept = (v, from_x, from_y, top, bottom)
        pairs = [(p, swap(q, 1)) for p, q in zip(kept, after(kept, top, bottom, *earlier))]
        last = [(pairs[3][side], pairs[4][side]) for side in range(2)]
        return [t for p in pairs[:3] for t in p] + last

    table = np.zeros((32, 16), np.int32)
    for ci in range(8):
        for fi in range(4):
            at = ci * 4 + fi
            table[at, 0:2] = ci, fi
            planes = [(8 * kind + ci) // 6 for kind in range(3)]
            table[at, 2:5] = planes
            for kind in range(3):
                if planes[kind] == fi:
                    table[at, 5] = (8 * kind + ci) % 6
            for k in range(4):
                if k in planes:
                    table[at, 6 + k] = planes.index(k)
    ids = lax.dynamic_index_in_dim(jnp.asarray(table), c * 4 + f, 0, keepdims=False)

    own = tokens.reshape(256, width)
    cot = cotangent.reshape(256, width)
    vectors_in = [ln1_gain, ln1_shift, out_bias, ln2_gain, ln2_shift, down_bias, qkv_bias, up_bias]
    vectors_in = [doc_ids.reshape(2, 128)] + vectors_in
    hbm = pl.BlockSpec(memory_space=pltpu.HBM)
    outs = [shaped((272, width), BF16), shaped((176, width), BF16), shaped((256, width), BF16)]
    sizes = [(size, width) for size in (256, 128, 32, 128, 128)]
    chunk, pack, piece = pl.pallas_call(
        prepare_kernel,
        out_shape=outs,
        in_specs=[pl.BlockSpec(memory_space=pltpu.SMEM)] + [hbm] * 14,
        out_specs=[pl.BlockSpec(memory_space=pltpu.VMEM)] * 3,
        scratch_shapes=[pltpu.VMEM(size, BF16) for size in sizes]
        + [pltpu.VMEM(x.shape, x.dtype) for x in vectors_in]
        + [pltpu.SemaphoreType.DMA((14,))],
        compiler_params=pltpu.CompilerParams(vmem_limit_bytes=58 * 1024 * 1024),
        cost_estimate=pl.CostEstimate(flops=0, bytes_accessed=0, transcendentals=0),
    )(ids, own, qkv_weight, out_weight, up_weight, down_weight, *vectors_in)
    packs = [pack] + [shift(pack, k) for k in (1, 2, 3)]
    w_heads, par, out_rows = kernel_call(
        unpack_kernel,
        [shaped((384, width), BF16), shaped((16, width), F32), shaped((128, width), BF16)],
        [ids, *packs],
        [pltpu.VMEM((4, 16, width), F32)],
        cost=3,
    )
    chunks = spread_relayed(chunk, 128, par)

    heads = shaped((2, 2048, 128), BF16)
    q_one, keys, values, docs, h_one = kernel_call(
        project_kernel,
        [heads, heads, heads, shaped((16, 128), F32), shaped((2, 4, 256, width), BF16)],
        [ids, alibi_slopes, *chunks, w_heads, par],
        scalars=2,
        spare=12,
        cost=0,
    )
    out_near = [out_rows] + [swap(out_rows, d) for d in (2, 4, 6)]
    far_piece = shift(after(piece, packs), 2)
    w_heads_far = swap(w_heads, 1)
    pieces_of_heads = [shaped((512, 128), BF16)] * 4

    def swap_heads(parts):
        got = [parts[0]] + [swap(parts[e], 2 * e) for e in (1, 2, 3)]
        far = kernel_call(heads_far_kernel, [shaped((4, 256, 128), BF16)], got, scalars=0)[0]
        return [*got, swap(far, 1)], far

    q_two, full, *mixed_parts = kernel_call(
        attend_kernel,
        [heads, shaped((2048, 128), F32), *pieces_of_heads],
        [ids, docs, q_one, keys, values],
        [pltpu.VMEM((8, 256, 128), BF16), pltpu.VMEM((2, 4, 2 * TILE, 2 * TILE), F32)],
        spare=14,
        cost=20,
    )
    cot_near = pair(after(cot, full))
    mixed_parts = after(mixed_parts, out_near)
    out_pieces = [t for v in out_near for t in (v, swap(after(v, full), 1))]
    mixed_in, mixed_far = swap_heads(mixed_parts)
    far_piece = after(far_piece, mixed_far)
    rows = shaped((256, width), BF16)
    full_rows = shaped((256, width), F32)
    w_out, mixed, resid, h_two = kernel_call(
        branch_kernel,
        [shaped((width, width), BF16), rows, full_rows, rows],
        [ids, chunk, *mixed_in, par, *out_pieces],
        tied=[w_heads_far, cot_near],
        cost=5,
    )
    h_near = pair(h_two)
    up_row = up_bias.astype(F32).reshape(1, width)

    def feed(h, cots):
        return kernel_call(
            feed_kernel,
            [rows, rows, full_rows, full_rows],
            [h, cots, up_weight, up_row, down_weight],
            scalars=0,
            spare=8,
            cost=5,
        )

    def feed_other(h, cots, accs):
        return kernel_call(
            feed_other_kernel,
            [rows, rows, rows, rows],
            [ids, h, cots, par, *accs, *far_pieces],
            [pltpu.VMEM((256, width), F32)] * 2
            + [pltpu.VMEM((width, width), BF16)] * 2
            + [pltpu.VMEM((8, width), F32)],
            spare=8,
            cost=5,
        )

    act_own, dup_own, *accs_own = feed(h_two, cot)
    far_pieces = spread_relayed(far_piece, 128, act_own)
    act_near, dup_near, *accs_near = feed(h_near, cot_near)
    act_near_far, dup_near_far, branch_near, dh_near = feed_other(h_near, cot_near, accs_near)
    dh_got = pair(dh_near)
    act_own_far, dup_own_far, branch_own, dh_own = feed_other(h_two, after(cot, dh_near), accs_own)
    big = shaped((4, 512, width), BF16)
    keep, send, up_sums = kernel_call(
        feed_weights_kernel,
        [big, big, shaped((16, width), F32)],
        [
            ids,
            h_two,
            h_near,
            cot,
            cot_near,
            dup_own,
            dup_near,
            act_own,
            act_near,
            dup_own_far,
            dup_near_far,
            act_own_far,
            act_near_far,
        ],
        [pltpu.VMEM((2, width, width), BF16)],
        spare=8,
        cost=10,
    )
    dresid, dbranch, *dmixed_parts, sums = kernel_call(
        middle_kernel,
        [full_rows, rows, *pieces_of_heads, shaped((8, width), F32)],
        [ids, dh_own, dh_got, resid, cot, par, w_out],
        [pltpu.VMEM((256, width), BF16)],
        cost=40,
    )
    send = swap(send, 1)
    dmixed_heads, _ = swap_heads(after(dmixed_parts, send))

    def shape(*size):
        return shaped((*size, width), BF16)

    def relay(own_part, x_part, y_part):
        from_x, from_y = swap(x_part, 2), swap(y_part, 4)
        half = own_part.shape[0] // 4
        kept, x_next, y_next = kernel_call(
            relay_kernel,
            [shape(2 * half), shape(half), shape(half)],
            [own_part, from_x, from_y],
            scalars=0,
        )
        return kept, swap(y_next, 4), swap(x_next, 2)

    out_keep, out_send = kernel_call(
        out_weights_kernel,
        [shape(4, 128), shape(4, 128)],
        [ids, dbranch, mixed],
        [pltpu.VMEM((width, width), BF16)],
    )
    x_part, y_part, own_part = kernel_call(
        pair_sum_kernel,
        [shape(640), shape(640), shape(1280)],
        [keep, send, out_keep, swap(out_send, 1)],
        scalars=0,
    )
    feed_kept = relay(own_part, x_part, y_part)
    feed_near, feed_far, out_next, out_last = kernel_call(
        owned_kernel,
        [shape(288), shape(288), shape(32), shape(32)],
        [ids, *feed_kept],
        [pltpu.VMEM((128, width), BF16)],
    )
    branch_got = pair(after(branch_near, dh_got))
    layer_out = kernel_call(
        layer_out_kernel, [rows], [resid, par, branch_own, branch_got], scalars=0
    )[0]

    blocks = shaped((4, 256, 384), BF16)
    near, send = kernel_call(
        attend_back_kernel,
        [blocks, blocks],
        [ids, docs, q_two, keys, values, full, *dmixed_heads],
        [
            pltpu.VMEM((2, 2048, 128), BF16),
            *[pltpu.VMEM((2, 2048, 128), F32)] * 3,
            pltpu.VMEM((8, 256, 128), BF16),
        ],
        spare=14,
        cost=40,
        tied=[own_part, branch_got],
    )
    far = swap(send, 1)
    wsum = kernel_call(
        head_weights_kernel,
        [shaped((384, width), F32)],
        [near, send, h_one],
        scalars=0,
    )[0]
    x_part, y_part, own_part, slots_kept, slots_sent = kernel_call(
        unproject_kernel,
        [shape(256), shape(256), shape(512), shape(288), shape(288)],
        [
            ids,
            *chunks[0::2],
            near,
            far,
            send,
            w_heads,
            w_heads_far,
            par,
            sums,
            up_sums,
            wsum,
        ],
        [pltpu.VMEM((4, 144, width), BF16), pltpu.VMEM((4, 16, width), F32)],
        spare=8,
    )
    slots_near, slots_far = kernel_call(
        slots_kernel,
        [shape(144), shape(144)],
        [slots_kept, pair(slots_sent)],
        scalars=0,
        tied=[feed_kept[0]],
    )
    share_sums = relay(own_part, x_part, y_part)
    input_grad = kernel_call(
        input_kernel, [rows], [*share_sums, chunk, par, dresid], scalars=0, cost=10
    )[0]
    slot_sum = kernel_call(
        sum_kernel,
        [shape(144)],
        [slots_near, shift(slots_far, 2)],
        scalars=0,
        tied=[share_sums[0]],
    )[0]
    last_pieces = spread(slot_sum)
    feed_sum = kernel_call(
        feed_sum_kernel,
        [shape(288)],
        [feed_near, shift(feed_far, 2), shift(out_next, 1), shift(out_last, 3)],
        scalars=0,
        tied=[*last_pieces[2::2], input_grad],
    )[0]
    sizes = [256] * 6 + [1024, 512]
    qkv_grad, *vectors = kernel_call(
        last_grads_kernel,
        [shaped((768, width), F32), *(shaped((1, size), F32) for size in sizes)],
        [ids, *last_pieces],
        spare=14,
        cost=10,
    )
    feed_parts = spread_relayed(feed_sum, 144)
    vmem, hbm = pl.BlockSpec(memory_space=pltpu.VMEM), pl.BlockSpec(memory_space=pltpu.HBM)

    def write(body, parts, count, before, cost):
        return pl.pallas_call(
            body,
            out_shape=[shaped((width, width), F32)] * 2 + [shaped((256, width), F32)],
            in_specs=[pl.BlockSpec(memory_space=pltpu.SMEM)]
            + [vmem] * len(parts)
            + [hbm] * len(before),
            out_specs=[hbm] * 3,
            input_output_aliases={1 + len(parts) + i: i for i in range(len(before))},
            scratch_shapes=[
                pltpu.VMEM((count, 288, width), F32),
                pltpu.SemaphoreType.DMA((3 * count,)),
            ],
            compiler_params=pltpu.CompilerParams(vmem_limit_bytes=16 * 1024 * 1024),
            cost_estimate=pl.CostEstimate(
                flops=int(cost * 1e9), bytes_accessed=0, transcendentals=0
            ),
        )(ids, *parts, *before)

    body = functools.partial(feed_grads_kernel, count=6, first=0)
    grads = write(body, feed_parts[:6], 6, [], 10)
    tails = [*feed_parts[6], *feed_parts[7]]
    up_grad, down_grad, out_grad = write(feed_grads_last_kernel, tails, 2, grads, 0)
    g1, s1, ob, g2, s2, db, ub, bias_grad = (v.reshape(v.shape[1]) for v in vectors)
    return (
        layer_out.reshape(tokens.shape),
        input_grad.reshape(tokens.shape),
        g1,
        s1,
        qkv_grad,
        bias_grad,
        out_grad,
        ob,
        g2,
        s2,
        up_grad,
        ub,
        down_grad,
        db,
    )


def on_small_slice(mesh, tokens, slopes):
    return (
        mesh.shape["ctx"] == 8
        and mesh.shape["fsdp"] == 4
        and tokens.shape == (4, 2, 1024, 1024)
        and slopes.shape == (16,)
    )


def solution(mesh):
    in_specs = (
        P("fsdp", None, "ctx", None),
        P("fsdp", None, "ctx"),
        P(),
        P("fsdp"),
        P("fsdp"),
        P("fsdp", None),
        P("fsdp"),
        P("fsdp", None),
        P("fsdp"),
        P("fsdp"),
        P("fsdp"),
        P("fsdp", None),
        P("fsdp"),
        P("fsdp", None),
        P("fsdp"),
        P("fsdp", None, "ctx", None),
    )
    out_specs = (
        P("fsdp", None, "ctx", None),
        P("fsdp", None, "ctx", None),
        P("fsdp"),
        P("fsdp"),
        P("fsdp", None),
        P("fsdp"),
        P("fsdp", None),
        P("fsdp"),
        P("fsdp"),
        P("fsdp"),
        P("fsdp", None),
        P("fsdp"),
        P("fsdp", None),
        P("fsdp"),
    )
    def layer(*args):
        body = per_device if on_small_slice(mesh, args[0], args[2]) else gathered_device
        return jax.shard_map(
            body, mesh=mesh, in_specs=in_specs, out_specs=out_specs, check_vma=False
        )(*args)

    return layer
```

```python
import functools

import jax
import jax.numpy as jnp
import numpy as np
from jax import lax
from jax.experimental import pallas as pl
from jax.experimental.pallas import tpu as pltpu
from jax.sharding import PartitionSpec as P

EPS = 1e-05
MASKED = -1e30


def layer_norm(v, gain, shift):
    mean = jnp.mean(v, axis=-1, keepdims=True)
    centered = v - mean
    spread = jnp.mean(centered * centered, axis=-1, keepdims=True)
    return centered * lax.rsqrt(spread + EPS) * gain + shift


def gelu_tanh(v):
    return jax.nn.gelu(v, approximate=True)


def project_rows(values_in, weight):
    return lax.dot_general(
        values_in, weight, (((1,), (1,)), ((), ())), preferred_element_type=jnp.float32
    )


def cross_rows(left, right):
    return lax.dot_general(
        left, right, (((0,), (0,)), ((), ())), preferred_element_type=jnp.float32
    )


def token_positions(index, half_block, seq_len):
    owner = index // (2 * half_block)
    inside = index % (2 * half_block)
    return jnp.where(
        inside < half_block,
        owner * half_block + inside,
        seq_len - 1 - (owner * half_block + inside - half_block),
    )


def score_block(query3, keys3, query_pos, query_doc, key_pos, key_doc, slopes, scale):
    raw = jnp.einsum("qhe,khe->hqk", query3, keys3, preferred_element_type=jnp.float32) * scale
    distance = (query_pos[:, None] - key_pos[None, :]).astype(jnp.float32)
    scores = raw - slopes[:, None, None] * distance[None]
    allowed = ((key_pos[None, :] <= query_pos[:, None]) & (key_doc[None, :] == query_doc[:, None]))[
        None
    ]
    return (jnp.where(allowed, scores, MASKED), allowed)


def block_loop(total, size, visit, state):

    def turn_body(turn, inner):
        return visit(inner, turn * size, size)

    return lax.fori_loop(0, total // size, turn_body, state)


def gathered_device(
    tokens,
    doc_ids,
    alibi_slopes,
    ln1_gain,
    ln1_shift,
    qkv_weight,
    qkv_bias,
    out_weight,
    out_bias,
    ln2_gain,
    ln2_shift,
    up_weight,
    up_bias,
    down_weight,
    down_bias,
    cotangent,
):
    half_block = tokens.shape[2]
    width = tokens.shape[3]
    count = 2 * half_block
    heads = alibi_slopes.shape[0]
    head = width // heads
    scale = head ** (-0.5)
    seq_len = count * lax.axis_size("ctx")
    rows_in = tokens.reshape(count, width).astype(jnp.float32)
    doc_rows = doc_ids.reshape(count)
    grad_low = cotangent.reshape(count, width)
    grad_full = grad_low.astype(jnp.float32)
    own_pos = token_positions(
        lax.axis_index("ctx") * count + jnp.arange(count, dtype=jnp.int32), half_block, seq_len
    )
    gain_one, shift_one, w_qkv, b_qkv, w_out, b_out, gain_two, shift_two, b_down = (
        lax.all_gather(ln1_gain, "fsdp", axis=0, tiled=True),
        lax.all_gather(ln1_shift, "fsdp", axis=0, tiled=True),
        lax.all_gather(qkv_weight, "fsdp", axis=0, tiled=True),
        lax.all_gather(qkv_bias, "fsdp", axis=0, tiled=True),
        lax.all_gather(out_weight, "fsdp", axis=0, tiled=True),
        lax.all_gather(out_bias, "fsdp", axis=0, tiled=True),
        lax.all_gather(ln2_gain, "fsdp", axis=0, tiled=True),
        lax.all_gather(ln2_shift, "fsdp", axis=0, tiled=True),
        lax.all_gather(down_bias, "fsdp", axis=0, tiled=True),
    )
    norm_one, norm_one_pull = jax.vjp(
        layer_norm, rows_in, gain_one.astype(jnp.float32), shift_one.astype(jnp.float32)
    )
    h_one = norm_one.astype(jnp.bfloat16)
    joined = project_rows(h_one, w_qkv)
    bias_full = b_qkv.astype(jnp.float32)
    query = (joined[:, :width] + bias_full[:width]).astype(jnp.bfloat16)
    keys = joined[:, width : 2 * width].astype(jnp.bfloat16)
    values = (joined[:, 2 * width :] + bias_full[width:]).astype(jnp.bfloat16)
    query3 = query.reshape(count, heads, head)
    keys3 = keys.reshape(count, heads, head)
    values3 = values.reshape(count, heads, head)
    doc_all = lax.all_gather(doc_rows, "ctx", axis=0, tiled=True)
    start_state = (
        jnp.full((heads, count), MASKED, jnp.float32),
        jnp.zeros((heads, count), jnp.float32),
        jnp.zeros((count, heads, head), jnp.float32),
    )
    key_piece = lax.all_gather(keys, "ctx", axis=0, tiled=True)
    value_piece = lax.all_gather(values, "ctx", axis=0, tiled=True)

    def visit(state, offset, size):
        top, total, accum = state
        key_part = lax.dynamic_slice_in_dim(key_piece, offset, size).reshape(size, heads, head)
        value_part = lax.dynamic_slice_in_dim(value_piece, offset, size).reshape(size, heads, head)
        key_pos = token_positions(offset + jnp.arange(size, dtype=jnp.int32), half_block, seq_len)
        key_doc = lax.dynamic_slice_in_dim(doc_all, offset, size)
        scores, allowed = score_block(
            query3, key_part, own_pos, doc_rows, key_pos, key_doc, alibi_slopes, scale
        )
        new_top = jnp.maximum(top, jnp.max(scores, axis=2))
        weights = jnp.where(allowed, jnp.exp(scores - new_top[:, :, None]), 0.0)
        factor = jnp.exp(top - new_top)
        total = total * factor + jnp.sum(weights, axis=2)
        accum = accum * jnp.transpose(factor)[:, :, None] + jnp.einsum(
            "hqk,khe->qhe",
            weights.astype(jnp.bfloat16),
            value_part,
            preferred_element_type=jnp.float32,
        )
        return (new_top, total, accum)

    top, total, accum = block_loop(key_piece.shape[0], 512, visit, start_state)
    log_total = top + jnp.log(total)
    attended = accum / jnp.transpose(total)[:, :, None]
    mixed = attended.reshape(count, width).astype(jnp.bfloat16)
    resid = rows_in + project_rows(mixed, w_out) + b_out.astype(jnp.float32)
    norm_two, norm_two_pull = jax.vjp(
        layer_norm, resid, gain_two.astype(jnp.float32), shift_two.astype(jnp.float32)
    )
    h_two = norm_two.astype(jnp.bfloat16)
    w_up, b_up, w_down = (
        lax.all_gather(up_weight, "fsdp", axis=0, tiled=True),
        lax.all_gather(up_bias, "fsdp", axis=0, tiled=True),
        lax.all_gather(down_weight, "fsdp", axis=0, tiled=True),
    )
    up = project_rows(h_two, w_up) + b_up.astype(jnp.float32)
    act, gelu_pull = jax.vjp(gelu_tanh, up)
    act_low = act.astype(jnp.bfloat16)
    branch = jnp.dot(act_low, w_down, preferred_element_type=jnp.float32)
    layer_out = resid + branch + b_down.astype(jnp.float32)
    dup = gelu_pull(project_rows(grad_low, w_down))[0].astype(jnp.bfloat16)
    stacked = lax.psum_scatter(
        jnp.concatenate([cross_rows(dup, h_two), cross_rows(act_low, grad_low)], axis=1).astype(
            jnp.bfloat16
        ),
        "fsdp",
        scatter_dimension=0,
        tiled=True,
    ).astype(jnp.float32)
    up_rows_grad = stacked[:, :width]
    down_rows_grad = stacked[:, width:]
    up_bias_term = jnp.sum(dup, axis=0, dtype=jnp.float32)
    dnorm_two = jnp.dot(dup, w_up, preferred_element_type=jnp.float32)
    dresid_norm, gain_two_grad, shift_two_grad = norm_two_pull(dnorm_two)
    dresid = grad_full + dresid_norm
    dbranch = dresid.astype(jnp.bfloat16)
    out_bias_grad = jnp.sum(dbranch, axis=0, dtype=jnp.float32)
    out_weight_grad = cross_rows(dbranch, mixed)
    dmixed = jnp.dot(dbranch, w_out, preferred_element_type=jnp.float32).astype(jnp.bfloat16)
    dmixed3 = dmixed.reshape(count, heads, head)
    delta = jnp.transpose(jnp.sum(dmixed3.astype(jnp.float32) * attended, axis=2))
    query_key_piece = lax.all_gather(keys, "ctx", axis=0, tiled=True)
    query_value_piece = lax.all_gather(values, "ctx", axis=0, tiled=True)

    def visit(accum_grad, offset, size):
        key_part = lax.dynamic_slice_in_dim(query_key_piece, offset, size).reshape(
            size, heads, head
        )
        value_part = lax.dynamic_slice_in_dim(query_value_piece, offset, size).reshape(
            size, heads, head
        )
        key_pos = token_positions(offset + jnp.arange(size, dtype=jnp.int32), half_block, seq_len)
        key_doc = lax.dynamic_slice_in_dim(doc_all, offset, size)
        scores, allowed = score_block(
            query3, key_part, own_pos, doc_rows, key_pos, key_doc, alibi_slopes, scale
        )
        probs = jnp.where(allowed, jnp.exp(scores - log_total[:, :, None]), 0.0)
        dprobs = jnp.einsum("qhe,khe->hqk", dmixed3, value_part, preferred_element_type=jnp.float32)
        dscores = (probs * (dprobs - delta[:, :, None])).astype(jnp.bfloat16)
        return accum_grad + jnp.einsum(
            "hqk,khe->qhe", dscores, key_part, preferred_element_type=jnp.float32
        )

    query_sum = block_loop(
        query_key_piece.shape[0], 512, visit, jnp.zeros((count, heads, head), jnp.float32)
    )
    dquery = (query_sum * scale).reshape(count, width).astype(jnp.bfloat16)
    total_all, delta_all = (
        lax.all_gather(
            jnp.transpose(log_total).astype(jnp.bfloat16), "ctx", axis=0, tiled=True
        ).astype(jnp.float32),
        lax.all_gather(jnp.transpose(delta).astype(jnp.bfloat16), "ctx", axis=0, tiled=True).astype(
            jnp.float32
        ),
    )
    empty = jnp.zeros((count, heads, head), jnp.float32)
    query_piece = lax.all_gather(query, "ctx", axis=0, tiled=True)
    grad_piece = lax.all_gather(dmixed, "ctx", axis=0, tiled=True)

    def visit(state, offset, size):
        dkeys, dvalues = state
        query_part = lax.dynamic_slice_in_dim(query_piece, offset, size).reshape(size, heads, head)
        grad_part = lax.dynamic_slice_in_dim(grad_piece, offset, size).reshape(size, heads, head)
        query_pos = token_positions(offset + jnp.arange(size, dtype=jnp.int32), half_block, seq_len)
        query_doc = lax.dynamic_slice_in_dim(doc_all, offset, size)
        total_part = jnp.transpose(lax.dynamic_slice_in_dim(total_all, offset, size))
        delta_part = jnp.transpose(lax.dynamic_slice_in_dim(delta_all, offset, size))
        scores, allowed = score_block(
            query_part, keys3, query_pos, query_doc, own_pos, doc_rows, alibi_slopes, scale
        )
        probs = jnp.where(allowed, jnp.exp(scores - total_part[:, :, None]), 0.0)
        dvalues = dvalues + jnp.einsum(
            "hqk,qhe->khe",
            probs.astype(jnp.bfloat16),
            grad_part,
            preferred_element_type=jnp.float32,
        )
        dprobs = jnp.einsum("qhe,khe->hqk", grad_part, values3, preferred_element_type=jnp.float32)
        dscores = (probs * (dprobs - delta_part[:, :, None])).astype(jnp.bfloat16)
        dkeys = dkeys + jnp.einsum(
            "hqk,qhe->khe", dscores, query_part, preferred_element_type=jnp.float32
        )
        return (dkeys, dvalues)

    dkeys, dvalues = block_loop(query_piece.shape[0], 512, visit, (empty, empty))
    dkeys_low = (dkeys * scale).reshape(count, width).astype(jnp.bfloat16)
    dvalues_low = dvalues.reshape(count, width).astype(jnp.bfloat16)
    dfused = jnp.concatenate([dquery, dkeys_low, dvalues_low], axis=1)
    qkv_weight_grad = cross_rows(dfused, h_one)
    qkv_bias_grad = jnp.concatenate(
        [
            jnp.sum(dquery, axis=0, dtype=jnp.float32),
            jnp.sum(dvalues_low, axis=0, dtype=jnp.float32),
        ]
    )
    dnorm_one = jnp.dot(dfused, w_qkv, preferred_element_type=jnp.float32)
    dinput_norm, gain_one_grad, shift_one_grad = norm_one_pull(dnorm_one)
    input_grad = (dresid + dinput_norm).astype(jnp.bfloat16).reshape(tokens.shape)
    down_bias_grad = jnp.sum(grad_full, axis=0)
    shares = (
        lax.psum_scatter(
            qkv_weight_grad.astype(jnp.bfloat16), "fsdp", scatter_dimension=0, tiled=True
        ).astype(jnp.float32),
        lax.psum_scatter(
            out_weight_grad.astype(jnp.bfloat16), "fsdp", scatter_dimension=0, tiled=True
        ).astype(jnp.float32),
        lax.psum_scatter(
            qkv_bias_grad.astype(jnp.bfloat16), "fsdp", scatter_dimension=0, tiled=True
        ).astype(jnp.float32),
        lax.psum_scatter(
            out_bias_grad.astype(jnp.bfloat16), "fsdp", scatter_dimension=0, tiled=True
        ).astype(jnp.float32),
        lax.psum_scatter(
            gain_one_grad.astype(jnp.bfloat16), "fsdp", scatter_dimension=0, tiled=True
        ).astype(jnp.float32),
        lax.psum_scatter(
            shift_one_grad.astype(jnp.bfloat16), "fsdp", scatter_dimension=0, tiled=True
        ).astype(jnp.float32),
        lax.psum_scatter(
            gain_two_grad.astype(jnp.bfloat16), "fsdp", scatter_dimension=0, tiled=True
        ).astype(jnp.float32),
        lax.psum_scatter(
            shift_two_grad.astype(jnp.bfloat16), "fsdp", scatter_dimension=0, tiled=True
        ).astype(jnp.float32),
        lax.psum_scatter(
            up_bias_term.astype(jnp.bfloat16), "fsdp", scatter_dimension=0, tiled=True
        ).astype(jnp.float32),
        lax.psum_scatter(
            down_bias_grad.astype(jnp.bfloat16), "fsdp", scatter_dimension=0, tiled=True
        ).astype(jnp.float32),
    )
    totals = (
        lax.psum(shares[0].astype(jnp.bfloat16), "ctx").astype(jnp.float32),
        lax.psum(shares[1].astype(jnp.bfloat16), "ctx").astype(jnp.float32),
        lax.psum(up_rows_grad.astype(jnp.bfloat16), "ctx").astype(jnp.float32),
        lax.psum(down_rows_grad.astype(jnp.bfloat16), "ctx").astype(jnp.float32),
        lax.psum(shares[2].astype(jnp.bfloat16), "ctx").astype(jnp.float32),
        lax.psum(shares[3].astype(jnp.bfloat16), "ctx").astype(jnp.float32),
        lax.psum(shares[4].astype(jnp.bfloat16), "ctx").astype(jnp.float32),
        lax.psum(shares[5].astype(jnp.bfloat16), "ctx").astype(jnp.float32),
        lax.psum(shares[6].astype(jnp.bfloat16), "ctx").astype(jnp.float32),
        lax.psum(shares[7].astype(jnp.bfloat16), "ctx").astype(jnp.float32),
        lax.psum(shares[8].astype(jnp.bfloat16), "ctx").astype(jnp.float32),
        lax.psum(shares[9].astype(jnp.bfloat16), "ctx").astype(jnp.float32),
    )
    return (
        layer_out.astype(jnp.bfloat16).reshape(tokens.shape),
        input_grad,
        totals[6],
        totals[7],
        totals[0],
        totals[4],
        totals[1],
        totals[5],
        totals[8],
        totals[9],
        totals[2],
        totals[10],
        totals[3],
        totals[11],
    )

F32 = jnp.float32
BF16 = jnp.bfloat16
LOG2E = 1.4426950408889634
LN2 = 0.6931471805599453
TILE = 256
DOC_LANES = 48
BACKWARD_ENDS = {j: (3, 7) if j < 3 else (7,) for j in range(8)}
GELU_A = 0.7978845608028654
GELU_B = 0.044715


def dot_nt(a, b):
    return lax.dot_general(a, b, (((1,), (1,)), ((), ())), preferred_element_type=F32)


def dot_nn(a, b):
    return lax.dot_general(a, b, (((1,), (0,)), ((), ())), preferred_element_type=F32)


def dot_tn(a, b):
    return lax.dot_general(a, b, (((0,), (0,)), ((), ())), preferred_element_type=F32)


def kernel_call(body, outs, ins, scratch=(), scalars=1, tied=(), spare=7, cost=0):
    groups = [x if isinstance(x, tuple) else (x,) for x in ins[scalars:]]
    flat = [x for group in groups for x in group]
    joined = [
        pltpu.VMEM((sum(x.shape[0] for x in group), *group[0].shape[1:]), group[0].dtype)
        for group in groups
        if len(group) > 1
    ]
    scratch = [*joined, *scratch]
    room = sum(int(np.prod(x.shape)) * jnp.dtype(x.dtype).itemsize for x in scratch)

    def run(*refs):
        numbers, refs = refs[:scalars], refs[scalars:]
        sources, refs = refs[: len(flat)], refs[len(flat) + len(tied) :]
        targets, refs = refs[: len(outs)], refs[len(outs) :]
        places, refs = list(refs[: len(joined)]), refs[len(joined) :]
        held, at = [], 0
        for group in groups:
            if len(group) == 1:
                held.append(sources[at])
            else:
                held.append(places.pop(0))
                row = 0
                for source in sources[at : at + len(group)]:
                    held[-1][row : row + source.shape[0], :] = source[...]
                    row += source.shape[0]
            at += len(group)
        body(*numbers, *held, *targets, *refs)

    vmem = pl.BlockSpec(memory_space=pltpu.VMEM)
    return pl.pallas_call(
        run,
        out_shape=list(outs),
        in_specs=[pl.BlockSpec(memory_space=pltpu.SMEM)] * scalars
        + [vmem] * len(flat)
        + [pl.BlockSpec(memory_space=pl.ANY)] * len(tied),
        out_specs=[vmem] * len(outs),
        scratch_shapes=scratch,
        compiler_params=pltpu.CompilerParams(vmem_limit_bytes=room + spare * 1024 * 1024),
        cost_estimate=pl.CostEstimate(
            flops=int(cost * 1e9), bytes_accessed=0, transcendentals=0
        ),
    )(*ins[:scalars], *flat, *tied)


def shaped(shape, dtype):
    return jax.ShapeDtypeStruct(shape, dtype)


def lanes_of(shape):
    return lax.broadcasted_iota(jnp.int32, shape, len(shape) - 1)


def three_pieces(v):
    high = v.astype(BF16).astype(F32)
    mid = (v - high).astype(BF16).astype(F32)
    return high, mid, v - high - mid


def normed(v):
    mean = jnp.mean(v, axis=-1, keepdims=True)
    centered = v - mean
    spread = jnp.mean(centered * centered, axis=-1, keepdims=True)
    root = lax.rsqrt(spread + EPS)
    return centered * root, root


def norm_back(dout, unit, root, gain):
    dn = dout * gain
    first = jnp.mean(dn, axis=-1, keepdims=True)
    second = jnp.mean(dn * unit, axis=-1, keepdims=True)
    return root * (dn - first - unit * second)


def block_rows(index, half_block):
    return pl.ds(pl.multiple_of(index * half_block, half_block), half_block)


def prepare_kernel(ids, *refs):
    own, w_ref, out_ref, up_ref, down_ref = refs[0:5]
    vectors, (chunk, pack, piece), places, sems = refs[5:14], refs[14:17], refs[17:31], refs[31]
    c = ids[0]

    def rows(ref, start, count):
        return ref.at[pl.ds(pl.multiple_of(start * count, count), count)]

    sources = [
        own,
        rows(w_ref, ids[5], 128),
        rows(out_ref, c, 32),
        rows(up_ref, c, 128),
        rows(down_ref, c, 128),
        *vectors,
    ]
    copies = [
        pltpu.make_async_copy(a, b, sems.at[i]) for i, (a, b) in enumerate(zip(sources, places))
    ]
    for copy in copies:
        copy.start()
    for copy in copies:
        copy.wait()
    doc, g1, s1, ob, g2, s2, db, qb, ub = places[5:]
    docs = doc[...].astype(F32)
    row = jnp.concatenate([docs[0:1], docs[1:2]], axis=1)
    chunk[256:272, :] = jnp.zeros((16, 1024), BF16)
    chunk[256:272, 0:256] = jnp.broadcast_to(row, (16, 256)).astype(BF16)

    def wide(ref):
        size = ref.shape[0]
        return jnp.broadcast_to(ref[...].astype(F32).reshape(1, size), (8, size))

    first = jnp.concatenate([wide(r) for r in (g1, s1, ob, g2)], axis=1)
    at = lax.broadcasted_iota(jnp.int32, (8, 1024), 0)
    first = jnp.where(at < 4, first, wide(ub))
    second = jnp.concatenate([wide(r) for r in (s2, db, qb)], axis=1)
    small = jnp.concatenate([first, second], axis=0).astype(BF16)
    chunk[0:256, :] = places[0][...]
    pack[0:128, :] = places[1][...]
    pack[128:144, :] = small
    pack[144:176, :] = places[2][...]
    piece[0:128, :] = places[3][...]
    piece[128:256, :] = places[4][...]


def unpack_kernel(ids, p0, p1, p2, p3, w_out, par_out, out_rows, small):
    packs = (p0, p1, p2, p3)
    f = ids[1]
    for k in range(4):
        plane = lax.rem(f + (4 - k), 4)
        small[plane] = packs[k][128:144, :].astype(F32)
        at = pl.multiple_of(plane * 32, 32)
        out_rows[pl.ds(at, 32), :] = packs[k][144:176, :]
        for kind in range(3):

            @pl.when(ids[2 + kind] == plane)
            def _():
                w_out[kind * 128 : (kind + 1) * 128, :] = packs[k][0:128, :]

    rows = [small[p] for p in range(4)]

    def whole(row, start, stop, planes=(0, 1, 2, 3)):
        return jnp.concatenate([rows[p][row * 8 : row * 8 + 1, start:stop] for p in planes], axis=1)

    par_out[0:1, :] = whole(0, 0, 256)
    par_out[1:2, :] = whole(0, 256, 512)
    par_out[2:3, :] = whole(0, 512, 768)
    par_out[3:4, :] = whole(0, 768, 1024)
    par_out[4:5, :] = whole(1, 0, 256)
    par_out[5:6, :] = whole(1, 256, 512)
    par_out[6:7, :] = whole(1, 512, 1024, (0, 1))
    par_out[7:8, :] = whole(1, 512, 1024, (2, 3))
    par_out[8:16, :] = small[f ^ 2][0:8, :]
    par_out[8:9, :] = small[f ^ 2][4:5, :]


def project_kernel(ids, slopes, *refs):
    chunks, (w_ref, par_out, q_out, k_out, v_out, doc_out, h_out) = refs[:8], refs[8:]
    c = ids[0]
    mine = pl.ds(pl.multiple_of(c * 128, 128), 128)
    bias_q = par_out[6:7, mine]
    bias_v = par_out[7:8, mine]
    gain, shift = par_out[0:1, :], par_out[1:2, :]
    weight = w_ref[...]
    lane = lanes_of((256, 128))
    row = lax.broadcasted_iota(jnp.int32, (256, 128), 0)
    eye = (
        lax.broadcasted_iota(jnp.int32, (128, 128), 0) == lanes_of((128, 128))
    ).astype(BF16)
    sub = lax.broadcasted_iota(jnp.int32, (128, 256), 0).astype(F32) - 67.0
    is_doc = (lane >= 67) & (lane < 67 + DOC_LANES)
    low = lane < 64
    for d in range(8):
        cc = c ^ d
        h = (normed(chunks[d][0:256, :].astype(F32))[0] * gain + shift).astype(BF16)
        h_out[d % 2, d // 2] = h
        joined = dot_nt(h, weight)
        query = (joined[:, 0:128] + bias_q) * (LOG2E * 0.125)
        keys = joined[:, 128:256]
        values = joined[:, 256:384] + bias_v
        doc_row = chunks[d][256:272, 0:256].astype(F32)[0:1, :]
        doc_out[pl.ds(cc, 1), :] = doc_row[:, 0:128]
        doc_out[pl.ds(8 + cc, 1), :] = doc_row[:, 128:256]
        one_hot = dot_tn((sub == doc_row).astype(BF16), eye)
        pos = jnp.where(row < 128, cc * 128 + row, 2175 - cc * 128 - row).astype(F32)
        q_aug = jnp.where(lane < 67, 1.0, jnp.where(is_doc, one_hot, 0.0))
        k_tail = jnp.where(is_doc, (1.0 - one_hot) * MASKED, jnp.where(lane < 118, 1.0, 0.0))
        for hh in range(2):
            if hh == 1:
                query, keys, values = (pltpu.roll(t, 64, 1) for t in (query, keys, values))
            high, mid, rest = three_pieces(pos * (slopes[2 * c + hh] * LOG2E))
            k_aug = jnp.where(
                lane == 64, high, jnp.where(lane == 65, mid, jnp.where(lane == 66, rest, k_tail))
            )
            parts = (
                (q_out, jnp.where(low, query, q_aug).astype(BF16)),
                (k_out, jnp.where(low, keys, k_aug).astype(BF16)),
                (v_out, jnp.where(low, values, 1.0).astype(BF16)),
            )
            for ref, value in parts:
                ref[hh, block_rows(cc, 128), :] = value[0:128]
                ref[hh, block_rows(8 + cc, 128), :] = value[128:256]


def tile_start(i):
    return i * TILE if i < 4 else 1024 + (7 - i) * TILE


def tile_rows(i):
    start = jnp.where(i < 4, i * TILE, 1024 + (7 - i) * TILE)
    return pl.ds(pl.multiple_of(start, TILE), TILE)


def tile_docs(docs, i):
    at = tile_start(i) // 128
    return docs[at : at + 2, :]


def count_tiles(flags):
    total = jnp.sum(jnp.where(flags, 1.0, 0.0)).astype(jnp.int32)
    return lax.shift_right_logical(total, 8)


def span(first, last):
    out = []
    if first < 4 and first <= last:
        out.append(slice(first * TILE, (min(last, 3) + 1) * TILE))
    if last >= 4 and first <= last:
        out.append(slice(tile_start(last), tile_start(max(first, 4)) + TILE))
    return out


def attend_kernel(
    ids, docs_ref, q_ref, k_ref, v_ref, q_out, full_out, m0, m1, m2, m3, mixed_out, held
):
    docs = docs_ref[...]
    size = 2 * TILE
    lane = lanes_of((size, 128))
    low = lane < 64
    step_right = lanes_of((size, size)) - lax.broadcasted_iota(jnp.int32, (size, size), 0)

    def widest(scores):
        parts = [scores[:, at : at + 128] for at in range(0, size, 128)]
        return functools.reduce(jnp.maximum, parts)

    def rows_of(i):
        start = jnp.where(i < 2, i * size, 1024 + (3 - i) * size)
        return pl.ds(pl.multiple_of(start, size), size)

    def one_tile(i, carry):
        own = rows_of(i)
        at = jnp.where(i < 2, 4 * i, 8 + 4 * (3 - i))
        first = count_tiles(docs < jnp.min(docs_ref[pl.ds(at, 4), :]))
        first = lax.shift_right_logical(first, 1)
        allowed = jnp.where(i < 2, step_right, -step_right) <= 0
        queries = [q_ref[hh, own, :] for hh in range(2)]
        diagonal = [
            jnp.where(allowed, dot_nt(queries[hh], k_ref[hh, own, :]), MASKED) for hh in range(2)
        ]

        def look(j, tops):
            rows = rows_of(j)
            out = []
            for hh in range(2):
                scores = dot_nt(queries[hh], k_ref[hh, rows, :])
                held[hh, j] = scores
                out.append(jnp.maximum(tops[hh], widest(scores)))
            return tuple(out)

        tops = lax.fori_loop(first, i, look, tuple(widest(s) for s in diagonal))
        tops = [jnp.max(t, axis=1, keepdims=True) for t in tops]

        def gather(j, sums):
            rows = rows_of(j)
            out = []
            for hh in range(2):
                weights = jnp.exp2(held[hh, j] - tops[hh]).astype(BF16)
                out.append(sums[hh] + dot_nn(weights, v_ref[hh, rows, :]))
            return tuple(out)

        start = tuple(
            dot_nn(jnp.exp2(diagonal[hh] - tops[hh]).astype(BF16), v_ref[hh, own, :])
            for hh in range(2)
        )
        sums = lax.fori_loop(first, i, gather, start)
        outs = []
        for hh in range(2):
            total = sums[hh][:, 64:65]
            outs.append(sums[hh] / total)
            high, mid, rest = three_pieces(-(tops[hh] + jnp.log2(total)))
            tail = jnp.where(
                lane == 115,
                high,
                jnp.where(lane == 116, mid, jnp.where(lane == 117, rest, queries[hh].astype(F32))),
            )
            q_out[hh, own, :] = tail.astype(BF16)
        both = jnp.where(low, outs[0], pltpu.roll(outs[1], 64, 1))
        full_out[own, :] = both
        half = jnp.where(i < 2, 0, 128)
        chunk = jnp.where(i < 2, 4 * i, 4 * (3 - i))
        for piece in range(4):
            mixed_out[chunk + piece, pl.ds(pl.multiple_of(half, 128), 128), :] = both[
                piece * 128 : (piece + 1) * 128
            ].astype(BF16)
        return carry

    lax.fori_loop(0, 4, one_tile, 0)
    for e, ref in enumerate((m0, m1, m2, m3)):
        for parity in range(2):
            ref[parity * 256 : (parity + 1) * 256, :] = mixed_out[ids[0] ^ (2 * e + parity)]


def heads_far_kernel(g0, g1, g2, g3, out):
    for e, ref in enumerate((g0, g1, g2, g3)):
        out[e] = ref[256:512, :]


def attend_back_kernel(
    ids, docs_ref, q_ref, k_ref, v_ref, full_ref, g0, g1, g2, g3, g_far, keep, send, grads, dq, dk, dv, all_grads
):
    docs = docs_ref[...]
    lane = lanes_of((256, 128))
    low = lane < 64
    for e, ref in enumerate((g0, g1, g2, g3)):
        all_grads[ids[0] ^ (2 * e)] = ref[0:256, :]
        all_grads[ids[0] ^ (2 * e + 1)] = g_far[e]
    for at in range(8):
        piece = all_grads[at].astype(F32)
        other = jnp.concatenate(
            [
                full_ref[at * 128 : (at + 1) * 128, :],
                full_ref[1024 + at * 128 : 1024 + (at + 1) * 128, :],
            ],
            axis=0,
        )
        product = piece * other
        for hh in range(2):
            delta = jnp.sum(jnp.where(low == (hh == 0), product, 0.0), axis=1, keepdims=True)
            high, mid, rest = three_pieces(-delta)
            tail = jnp.where(
                lane == 64, high, jnp.where(lane == 65, mid, jnp.where(lane == 66, rest, 0.0))
            )
            moved = piece if hh == 0 else pltpu.roll(piece, 64, 1)
            value = jnp.where(low, moved, tail).astype(BF16)
            grads[hh, at * 128 : (at + 1) * 128, :] = value[0:128]
            grads[hh, 1024 + at * 128 : 1024 + (at + 1) * 128, :] = value[128:256]
    dq[...] = jnp.zeros_like(dq)
    down, right = lax.broadcasted_iota(jnp.int32, (TILE, TILE), 0), lanes_of((TILE, TILE))

    def run(j, last):
        own = slice(tile_start(j), tile_start(j) + TILE)
        allowed = (down <= right) if j < 4 else (down >= right)
        places = [own] + span(j + 1, last)

        def head(hh, carry):
            keys, values = k_ref[hh, own, :], v_ref[hh, own, :]
            dk_sum = dv_sum = 0.0
            for at, rows in enumerate(places):
                query, grad = q_ref[hh, rows, :], grads[hh, rows, :]
                probs = jnp.exp2(dot_nt(keys, query))
                if at == 0:
                    probs = jnp.where(allowed, probs, 0.0)
                dscores = (probs * dot_nt(values, grad)).astype(BF16)
                dq[hh, rows, :] += dot_tn(dscores, keys)
                dk_sum += dot_nn(dscores, query)
                dv_sum += dot_nn(probs.astype(BF16), grad)
            dk[hh, own, :] = dk_sum
            dv[hh, own, :] = dv_sum
            return carry

        lax.fori_loop(0, 2, head, 0)

    for j in range(8):
        ends = BACKWARD_ENDS[j]
        within = jnp.sum(jnp.where(docs <= jnp.max(tile_docs(docs, j)), 1.0, 0.0))
        last = lax.shift_right_logical(within.astype(jnp.int32) + (TILE - 1), 8) - 1
        for at, end in enumerate(ends):
            fits = last <= end
            if at:
                fits = fits & (last > ends[at - 1])
            if len(ends) == 1:
                run(j, end)
            else:
                pl.when(fits)(functools.partial(run, j, end))
    for j in range(4):
        for parity, ref in enumerate((keep, send)):
            cc = ids[0] ^ (2 * j + parity)
            for half in range(2):
                rows = block_rows(8 * half + cc, 128)
                at = slice(half * 128, (half + 1) * 128)
                for which, (held, scale) in enumerate(((dq, 0.125), (dk, LN2), (dv, 1.0))):
                    other = pltpu.roll(held[1, rows, :], 64, 1)
                    both = jnp.where(low[0:128], held[0, rows, :], other) * scale
                    ref[j, at, which * 128 : (which + 1) * 128] = both.astype(BF16)


def branch_kernel(ids, chunk, g0, g1, g2, g3, g_far, par, *refs):
    pieces, (w_out, mixed_out, resid_out, h_out) = refs[:8], refs[8:]
    for d in range(8):
        for plane in range(4):
            at = pl.multiple_of(plane * 256 + (ids[0] ^ d) * 32, 32)
            w_out[pl.ds(at, 32), :] = pieces[d][plane * 32 : (plane + 1) * 32, :]
    for e, ref in enumerate((g0, g1, g2, g3)):
        for parity, value in enumerate((ref[0:256, :], g_far[e])):
            at = pl.multiple_of((ids[0] ^ (2 * e + parity)) * 128, 128)
            mixed_out[:, pl.ds(at, 128)] = value
    resid = chunk[0:256, :].astype(F32) + dot_nt(mixed_out[...], w_out[...]) + par[2:3, :]
    resid_out[...] = resid
    h_out[...] = (normed(resid)[0] * par[3:4, :] + par[4:5, :]).astype(BF16)


def feed_step(h, cot, up_w, down_w, bias):
    u = dot_nt(h, up_w) + bias
    grad = dot_nt(cot, down_w)
    square = u * u
    th = jnp.tanh(GELU_A * u * (1.0 + GELU_B * square))
    half = 0.5 * (1.0 + th)
    act = (u * half).astype(BF16)
    slope = half + 0.5 * u * (1.0 - th * th) * (GELU_A * (1.0 + 3.0 * GELU_B * square))
    return act, (grad * slope).astype(BF16)


def feed_kernel(h_ref, cot_ref, up_ref, bias_ref, down_ref, act_out, dup_out, acc, dacc):
    acc[...] = jnp.zeros_like(acc)
    dacc[...] = jnp.zeros_like(dacc)

    def step(t, carry):
        at = pl.ds(pl.multiple_of(t * 256, 256), 256)
        up_w, down_w = up_ref[at, :], down_ref[at, :]
        act, dup = feed_step(h_ref[...], cot_ref[...], up_w, down_w, bias_ref[0:1, at])
        act_out[:, at] = act
        dup_out[:, at] = dup
        acc[...] += dot_nn(act, down_w)
        dacc[...] += dot_nn(dup, up_w)
        return carry

    lax.fori_loop(0, 4, step, 0)


def feed_other_kernel(ids, h_ref, cot_ref, par, acc_in, dacc_in, *refs):
    pieces, (act_out, dup_out, branch, dh, acc, dacc, ups, downs, bias) = refs[:8], refs[8:]
    for d in range(8):
        at = slice(d * 128, (d + 1) * 128)
        ups[at, :] = pieces[d][0:128, :]
        downs[at, :] = pieces[d][128:256, :]
        bias[0:1, at] = par[8:9, pl.ds(pl.multiple_of((ids[0] ^ d) * 128, 128), 128)]
    acc[...] = acc_in[...]
    dacc[...] = dacc_in[...]

    def step(t, carry):
        at = pl.ds(pl.multiple_of(t * 256, 256), 256)
        up_w, down_w = ups[at, :], downs[at, :]
        act, dup = feed_step(h_ref[...], cot_ref[...], up_w, down_w, bias[0:1, at])
        act_out[:, at] = act
        dup_out[:, at] = dup
        acc[...] += dot_nn(act, down_w)
        dacc[...] += dot_nn(dup, up_w)
        return carry

    lax.fori_loop(0, 4, step, 0)
    branch[...] = acc[...].astype(BF16)
    dh[...] = dacc[...].astype(BF16)


def middle_kernel(
    ids, d0, d1, resid_ref, cot_ref, par, w_ref, dresid_out, dbranch_out, m0, m1, m2, m3, sums, held
):
    dh = d0[...].astype(F32) + d1[...].astype(F32)
    unit, root = normed(resid_ref[...])
    cot = cot_ref[...].astype(F32)
    dresid = cot + norm_back(dh, unit, root, par[3:4, :])
    dresid_out[...] = dresid
    dbranch = dresid.astype(BF16)
    dbranch_out[...] = dbranch
    held[...] = dot_nn(dbranch, w_ref[...]).astype(BF16)
    for e, ref in enumerate((m0, m1, m2, m3)):
        for parity in range(2):
            at = pl.multiple_of((ids[0] ^ (2 * e + parity)) * 128, 128)
            ref[parity * 256 : (parity + 1) * 256, :] = held[:, pl.ds(at, 128)]
    sums[...] = jnp.zeros_like(sums)
    sums[0:1, :] = jnp.sum(dbranch.astype(F32), axis=0, keepdims=True)
    sums[1:2, :] = jnp.sum(dh * unit, axis=0, keepdims=True)
    sums[2:3, :] = jnp.sum(dh, axis=0, keepdims=True)
    sums[3:4, :] = jnp.sum(cot, axis=0, keepdims=True)


def feed_weights_kernel(ids, *refs):
    hs, cots, dups, acts, dups_far, acts_far = (refs[2 * i : 2 * i + 2] for i in range(6))
    keep, send, bias, all_rows = refs[12:]
    c = ids[0]

    def product(lefts, at, rights):
        return sum(dot_tn(a[:, at], b[...]) for a, b in zip(lefts, rights)).astype(BF16)

    for t in range(4):
        at = slice(t * 256, (t + 1) * 256)
        for which, (lefts, rights) in enumerate(((dups, hs), (acts, cots))):
            all_rows[which, at, :] = product(lefts, at, rights)
        for which, (lefts, rights) in enumerate(((dups_far, hs), (acts_far, cots))):
            both = product(lefts, at, rights)
            for parity, ref in enumerate((keep, send)):
                place = slice(256 + which * 128, 384 + which * 128)
                ref[t, place, :] = both[parity * 128 : (parity + 1) * 128]
    for e in range(4):
        for parity, ref in enumerate((keep, send)):
            rows = block_rows(c ^ (2 * e + parity), 128)
            ref[e, 0:128, :] = all_rows[0, rows, :]
            ref[e, 128:256, :] = all_rows[1, rows, :]

    def total(refs):
        return sum(jnp.sum(r[...].astype(F32), axis=0, keepdims=True) for r in refs)

    bias[0:1, :] = total(dups)
    far = total(dups_far)
    for d in range(8):
        at = pl.ds(pl.multiple_of((c ^ d) * 128, 128), 128)
        bias[8:9, at] = far[:, d * 128 : (d + 1) * 128]


def out_weights_kernel(ids, dbranch, mixed, keep, send, total):
    for t in range(4):
        at = slice(t * 256, (t + 1) * 256)
        total[at, :] = dot_tn(dbranch[:, at], mixed[...]).astype(BF16)
    for e in range(4):
        for parity, ref in enumerate((keep, send)):
            cc = ids[0] ^ (2 * e + parity)
            for plane in range(4):
                at = pl.multiple_of(plane * 256 + cc * 32, 32)
                ref[e, plane * 32 : (plane + 1) * 32, :] = total[pl.ds(at, 32), :]


def added(*values):
    return sum(v.astype(F32) for v in values).astype(BF16)


def pair_sum_kernel(keep, got, out_keep, out_got, x_out, y_out, own_out):
    def put(target, slot, e, part):
        rows = slice(256 * part, 256 * (part + 1))
        more = slice(64 * part, 64 * (part + 1))
        at = slot * 320
        target[at : at + 256, :] = added(keep[e, rows], got[e, rows])
        target[at + 256 : at + 320, :] = added(out_keep[e, more], out_got[e, more])

    put(x_out, 0, 1, 0)
    put(x_out, 1, 3, 0)
    put(y_out, 0, 2, 1)
    put(y_out, 1, 3, 1)
    put(own_out, 0, 0, 0)
    put(own_out, 1, 0, 1)
    put(own_out, 2, 2, 0)
    put(own_out, 3, 1, 1)


def relay_kernel(own, from_x, from_y, kept, x_out, y_out):
    half = own.shape[0] // 4
    kept[0:half, :] = added(own[0:half, :], from_x[0:half, :])
    y_out[...] = added(own[2 * half : 3 * half, :], from_x[half:, :])
    kept[half:, :] = added(own[half : 2 * half, :], from_y[0:half, :])
    x_out[...] = added(own[3 * half :, :], from_y[half:, :])


def owned_kernel(ids, kept, from_y, from_x, near, far, out_next, out_last, share):
    f = ids[1]
    near[0:256, :] = added(kept[0:256, :], from_y[0:256, :])
    far[0:256, :] = added(kept[320:576, :], from_x[0:256, :])
    share[0:64, :] = added(kept[256:320, :], from_y[256:320, :])
    share[64:128, :] = added(kept[576:640, :], from_x[256:320, :])
    for k, target in enumerate((near, out_next, far, out_last)):
        rows = pl.ds(pl.multiple_of(lax.rem(f + k, 4) * 32, 32), 32)
        if k % 2:
            target[...] = share[rows, :]
        else:
            target[256:288, :] = share[rows, :]


def feed_sum_kernel(near, far, out_next, out_last, out):
    out[0:256, :] = added(near[0:256, :], far[0:256, :])
    outs = (near[256:288, :], far[256:288, :], out_next[...], out_last[...])
    out[256:288, :] = added(*outs)


def slots_kernel(kept, got, near, far):
    near[...] = added(kept[0:144, :], got[0:144, :])
    far[...] = added(kept[144:288, :], got[144:288, :])


def sum_kernel(*refs):
    refs[-1][...] = added(*(r[...] for r in refs[:-1]))


def layer_out_kernel(resid, par, one, two, out):
    out[...] = (resid[...] + par[5:6, :] + one[...].astype(F32) + two[...].astype(F32)).astype(BF16)


def head_weights_kernel(keep, send, h_ref, total):
    for parity, ref in enumerate((keep, send)):
        for j in range(4):
            got = dot_tn(ref[j], h_ref[parity, j])
            if parity == 0 and j == 0:
                total[...] = got
            else:
                total[...] += got


def unproject_kernel(ids, *refs):
    chunks, (near, far, bias_far, w_near, w_far, par, sums, up_sums, wsum) = refs[:4], refs[4:13]
    x_out, y_out, own_out, slots_kept, slots_sent, slots, small = refs[13:]
    c, f = ids[0], ids[1]
    near_w, far_w = w_near[...], w_far[...]
    gain_grad = shift_grad = bias_grad = 0.0
    places = (
        (own_out, 0, own_out, 128),
        (x_out, 0, own_out, 384),
        (own_out, 256, y_out, 0),
        (x_out, 128, y_out, 128),
    )
    for e, chunk in enumerate(chunks):
        grads = near[e]
        unit = normed(chunk[0:256, :].astype(F32))[0]
        share = dot_nn(grads, near_w) + dot_nn(far[e], far_w)
        top, at, bottom, below = places[e]
        top[at : at + 128, :] = share[0:128].astype(BF16)
        bottom[below : below + 128, :] = share[128:256].astype(BF16)
        gain_grad += jnp.sum(share * unit, axis=0, keepdims=True)
        shift_grad += jnp.sum(share, axis=0, keepdims=True)
        bias_grad += jnp.sum(grads.astype(F32) + bias_far[e].astype(F32), axis=0, keepdims=True)
    small[...] = jnp.zeros_like(small)
    for p in range(4):
        at = slice(p * 256, (p + 1) * 256)
        small[p, 0:1, 0:256] = gain_grad[:, at]
        small[p, 0:1, 256:512] = shift_grad[:, at]
        small[p, 0:1, 512:768] = sums[0:1, at]
        small[p, 0:1, 768:1024] = sums[1:2, at]
        small[p, 1:2, 0:256] = sums[2:3, at]
        small[p, 1:2, 256:512] = sums[3:4, at]
        small[p, 1:2, 512:640] = bias_grad[:, 0:128] if p < 2 else bias_grad[:, 256:384]
        up_far = jnp.where(f == p ^ 2, up_sums[8:9, :], 0.0)
        small[p, 2:3, :] = jnp.where(f == p, up_sums[0:1, :], up_far)
        start = pl.multiple_of(ids[6 + p] * 128, 128)
        slots[p, 0:128, :] = wsum[pl.ds(start, 128), :].astype(BF16)
        slots[p, 128:144, :] = small[p].astype(BF16)
    for k in range(2):
        at = slice(k * 144, (k + 1) * 144)
        slots_kept[at, :] = slots[f ^ (2 * k)]
        slots_sent[at, :] = slots[f ^ (2 * k + 1)]


def input_kernel(kept, from_y, from_x, chunk, par, dresid, out):
    moved = jnp.concatenate([from_y[...], from_x[...]], axis=0)
    dh = kept[...].astype(F32) + moved.astype(F32)
    unit, root = normed(chunk[0:256, :].astype(F32))
    out[...] = (dresid[...] + norm_back(dh, unit, root, par[0:1, :])).astype(BF16)


def feed_grads_kernel(ids, *refs, count, first):
    pieces, (up_out, down_out, out_out, place, sems) = refs[:count], refs[-5:]
    copies = []
    for n, piece in enumerate(pieces):
        cc = ids[0] ^ (first + n)
        place[n] = piece[...].astype(F32)
        moves = (
            (place.at[n, 0:128], up_out.at[block_rows(cc, 128)]),
            (place.at[n, 128:256], down_out.at[block_rows(cc, 128)]),
            (place.at[n, 256:288], out_out.at[pl.ds(pl.multiple_of(cc * 32, 32), 32)]),
        )
        for i, (a, b) in enumerate(moves):
            copies.append(pltpu.make_async_copy(a, b, sems.at[3 * n + i]))
            copies[-1].start()
    for copy in copies:
        copy.wait()


def feed_grads_last_kernel(ids, t0, b0, t1, b1, *refs):
    pieces, place = (t0, b0, t1, b1), refs[-2]
    up_out, down_out, out_out, sems = *refs[-5:-2], refs[-1]
    copies = []
    for n in range(2):
        cc = ids[0] ^ (6 + n)
        place[n, 0:144] = pieces[2 * n][...].astype(F32)
        place[n, 144:288] = pieces[2 * n + 1][...].astype(F32)
        moves = (
            (place.at[n, 0:128], up_out.at[block_rows(cc, 128)]),
            (place.at[n, 128:256], down_out.at[block_rows(cc, 128)]),
            (place.at[n, 256:288], out_out.at[pl.ds(pl.multiple_of(cc * 32, 32), 32)]),
        )
        for i, (a, b) in enumerate(moves):
            copies.append(pltpu.make_async_copy(a, b, sems.at[3 * n + i]))
            copies[-1].start()
    for copy in copies:
        copy.wait()


def last_grads_kernel(ids, *refs):
    pieces, (qkv_out, g1, s1, ob, g2, s2, db, ub, bias_out) = refs[:8], refs[8:]
    c, f = ids[0], ids[1]
    total = 0.0
    for d in range(8):
        cc = c ^ d
        place = lax.rem(cc + 24 - 6 * f, 8)

        @pl.when(place < 6)
        def _():
            qkv_out[block_rows(place, 128), :] = pieces[d][0:128, :].astype(F32)

        rows = pieces[d][128:144, :].astype(F32)
        total += rows

        @pl.when(lax.div(cc, 4) == lax.rem(f, 2))
        def _():
            at = pl.multiple_of(lax.rem(cc, 4) * 128, 128)
            bias_out[0:1, pl.ds(at, 128)] = rows[1:2, 512:640]

    for ref, row, start in ((g1, 0, 0), (s1, 0, 256), (ob, 0, 512), (g2, 0, 768), (s2, 1, 0), (db, 1, 256)):
        ref[...] = total[row : row + 1, start : start + 256]
    ub[...] = total[2:3, :]


def per_device(
    tokens,
    doc_ids,
    alibi_slopes,
    ln1_gain,
    ln1_shift,
    qkv_weight,
    qkv_bias,
    out_weight,
    out_bias,
    ln2_gain,
    ln2_shift,
    up_weight,
    up_bias,
    down_weight,
    down_bias,
    cotangent,
):
    c, f = lax.axis_index("ctx"), lax.axis_index("fsdp")
    width = 1024

    def swap(v, d):
        return lax.ppermute(v, "ctx", [(i, i ^ d) for i in range(8)])

    def shift(v, k):
        return lax.ppermute(v, "fsdp", [(i, (i + k) % 4) for i in range(4)])

    def pair(v):
        return lax.ppermute(v, "fsdp", [(i, i ^ 1) for i in range(4)])

    def after(value, *earlier):
        return lax.optimization_barrier((value, earlier))[0]

    def spread(v):
        near = [v] + [swap(v, d) for d in (2, 4, 6)]
        return [t for e in near for t in (e, swap(e, 1))]

    def spread_relayed(v, cut, *earlier):
        from_x, from_y = swap(v, 2), swap(v, 4)
        top, bottom = swap(from_x[:cut], 4), swap(from_y[cut:], 2)
        kept = (v, from_x, from_y, top, bottom)
        pairs = [(p, swap(q, 1)) for p, q in zip(kept, after(kept, top, bottom, *earlier))]
        last = [(pairs[3][side], pairs[4][side]) for side in range(2)]
        return [t for p in pairs[:3] for t in p] + last

    table = np.zeros((32, 16), np.int32)
    for ci in range(8):
        for fi in range(4):
            at = ci * 4 + fi
            table[at, 0:2] = ci, fi
            planes = [(8 * kind + ci) // 6 for kind in range(3)]
            table[at, 2:5] = planes
            for kind in range(3):
                if planes[kind] == fi:
                    table[at, 5] = (8 * kind + ci) % 6
            for k in range(4):
                if k in planes:
                    table[at, 6 + k] = planes.index(k)
    ids = lax.dynamic_index_in_dim(jnp.asarray(table), c * 4 + f, 0, keepdims=False)

    own = tokens.reshape(256, width)
    cot = cotangent.reshape(256, width)
    vectors_in = [ln1_gain, ln1_shift, out_bias, ln2_gain, ln2_shift, down_bias, qkv_bias, up_bias]
    vectors_in = [doc_ids.reshape(2, 128)] + vectors_in
    hbm = pl.BlockSpec(memory_space=pltpu.HBM)
    outs = [shaped((272, width), BF16), shaped((176, width), BF16), shaped((256, width), BF16)]
    sizes = [(size, width) for size in (256, 128, 32, 128, 128)]
    chunk, pack, piece = pl.pallas_call(
        prepare_kernel,
        out_shape=outs,
        in_specs=[pl.BlockSpec(memory_space=pltpu.SMEM)] + [hbm] * 14,
        out_specs=[pl.BlockSpec(memory_space=pltpu.VMEM)] * 3,
        scratch_shapes=[pltpu.VMEM(size, BF16) for size in sizes]
        + [pltpu.VMEM(x.shape, x.dtype) for x in vectors_in]
        + [pltpu.SemaphoreType.DMA((14,))],
        compiler_params=pltpu.CompilerParams(vmem_limit_bytes=58 * 1024 * 1024),
        cost_estimate=pl.CostEstimate(flops=0, bytes_accessed=0, transcendentals=0),
    )(ids, own, qkv_weight, out_weight, up_weight, down_weight, *vectors_in)
    packs = [pack] + [shift(pack, k) for k in (1, 2, 3)]
    w_heads, par, out_rows = kernel_call(
        unpack_kernel,
        [shaped((384, width), BF16), shaped((16, width), F32), shaped((128, width), BF16)],
        [ids, *packs],
        [pltpu.VMEM((4, 16, width), F32)],
        cost=3,
    )
    chunks = spread_relayed(chunk, 128, par)

    heads = shaped((2, 2048, 128), BF16)
    q_one, keys, values, docs, h_one = kernel_call(
        project_kernel,
        [heads, heads, heads, shaped((16, 128), F32), shaped((2, 4, 256, width), BF16)],
        [ids, alibi_slopes, *chunks, w_heads, par],
        scalars=2,
        spare=12,
        cost=0,
    )
    out_near = [out_rows] + [swap(out_rows, d) for d in (2, 4, 6)]
    far_piece = shift(after(piece, packs), 2)
    w_heads_far = swap(w_heads, 1)
    pieces_of_heads = [shaped((512, 128), BF16)] * 4

    def swap_heads(parts):
        got = [parts[0]] + [swap(parts[e], 2 * e) for e in (1, 2, 3)]
        far = kernel_call(heads_far_kernel, [shaped((4, 256, 128), BF16)], got, scalars=0)[0]
        return [*got, swap(far, 1)], far

    q_two, full, *mixed_parts = kernel_call(
        attend_kernel,
        [heads, shaped((2048, 128), F32), *pieces_of_heads],
        [ids, docs, q_one, keys, values],
        [pltpu.VMEM((8, 256, 128), BF16), pltpu.VMEM((2, 4, 2 * TILE, 2 * TILE), F32)],
        spare=14,
        cost=20,
    )
    cot_near = pair(after(cot, full))
    mixed_parts = after(mixed_parts, out_near)
    out_pieces = [t for v in out_near for t in (v, swap(after(v, full), 1))]
    mixed_in, mixed_far = swap_heads(mixed_parts)
    far_piece = after(far_piece, mixed_far)
    rows = shaped((256, width), BF16)
    full_rows = shaped((256, width), F32)
    w_out, mixed, resid, h_two = kernel_call(
        branch_kernel,
        [shaped((width, width), BF16), rows, full_rows, rows],
        [ids, chunk, *mixed_in, par, *out_pieces],
        tied=[w_heads_far, cot_near],
        cost=5,
    )
    h_near = pair(h_two)
    up_row = up_bias.astype(F32).reshape(1, width)

    def feed(h, cots):
        return kernel_call(
            feed_kernel,
            [rows, rows, full_rows, full_rows],
            [h, cots, up_weight, up_row, down_weight],
            scalars=0,
            spare=8,
            cost=5,
        )

    def feed_other(h, cots, accs):
        return kernel_call(
            feed_other_kernel,
            [rows, rows, rows, rows],
            [ids, h, cots, par, *accs, *far_pieces],
            [pltpu.VMEM((256, width), F32)] * 2
            + [pltpu.VMEM((width, width), BF16)] * 2
            + [pltpu.VMEM((8, width), F32)],
            spare=8,
            cost=5,
        )

    act_own, dup_own, *accs_own = feed(h_two, cot)
    far_pieces = spread_relayed(far_piece, 128, act_own)
    act_near, dup_near, *accs_near = feed(h_near, cot_near)
    act_near_far, dup_near_far, branch_near, dh_near = feed_other(h_near, cot_near, accs_near)
    dh_got = pair(dh_near)
    act_own_far, dup_own_far, branch_own, dh_own = feed_other(h_two, after(cot, dh_near), accs_own)
    big = shaped((4, 512, width), BF16)
    keep, send, up_sums = kernel_call(
        feed_weights_kernel,
        [big, big, shaped((16, width), F32)],
        [
            ids,
            h_two,
            h_near,
            cot,
            cot_near,
            dup_own,
            dup_near,
            act_own,
            act_near,
            dup_own_far,
            dup_near_far,
            act_own_far,
            act_near_far,
        ],
        [pltpu.VMEM((2, width, width), BF16)],
        spare=8,
        cost=10,
    )
    dresid, dbranch, *dmixed_parts, sums = kernel_call(
        middle_kernel,
        [full_rows, rows, *pieces_of_heads, shaped((8, width), F32)],
        [ids, dh_own, dh_got, resid, cot, par, w_out],
        [pltpu.VMEM((256, width), BF16)],
        cost=40,
    )
    send = swap(send, 1)
    dmixed_heads, _ = swap_heads(after(dmixed_parts, send))

    def shape(*size):
        return shaped((*size, width), BF16)

    def relay(own_part, x_part, y_part):
        from_x, from_y = swap(x_part, 2), swap(y_part, 4)
        half = own_part.shape[0] // 4
        kept, x_next, y_next = kernel_call(
            relay_kernel,
            [shape(2 * half), shape(half), shape(half)],
            [own_part, from_x, from_y],
            scalars=0,
        )
        return kept, swap(y_next, 4), swap(x_next, 2)

    out_keep, out_send = kernel_call(
        out_weights_kernel,
        [shape(4, 128), shape(4, 128)],
        [ids, dbranch, mixed],
        [pltpu.VMEM((width, width), BF16)],
    )
    x_part, y_part, own_part = kernel_call(
        pair_sum_kernel,
        [shape(640), shape(640), shape(1280)],
        [keep, send, out_keep, swap(out_send, 1)],
        scalars=0,
    )
    feed_kept = relay(own_part, x_part, y_part)
    feed_near, feed_far, out_next, out_last = kernel_call(
        owned_kernel,
        [shape(288), shape(288), shape(32), shape(32)],
        [ids, *feed_kept],
        [pltpu.VMEM((128, width), BF16)],
    )
    branch_got = pair(after(branch_near, dh_got))
    layer_out = kernel_call(
        layer_out_kernel, [rows], [resid, par, branch_own, branch_got], scalars=0
    )[0]

    blocks = shaped((4, 256, 384), BF16)
    near, send = kernel_call(
        attend_back_kernel,
        [blocks, blocks],
        [ids, docs, q_two, keys, values, full, *dmixed_heads],
        [
            pltpu.VMEM((2, 2048, 128), BF16),
            *[pltpu.VMEM((2, 2048, 128), F32)] * 3,
            pltpu.VMEM((8, 256, 128), BF16),
        ],
        spare=14,
        cost=40,
        tied=[own_part, branch_got],
    )
    far = swap(send, 1)
    wsum = kernel_call(
        head_weights_kernel,
        [shaped((384, width), F32)],
        [near, send, h_one],
        scalars=0,
    )[0]
    x_part, y_part, own_part, slots_kept, slots_sent = kernel_call(
        unproject_kernel,
        [shape(256), shape(256), shape(512), shape(288), shape(288)],
        [
            ids,
            *chunks[0::2],
            near,
            far,
            send,
            w_heads,
            w_heads_far,
            par,
            sums,
            up_sums,
            wsum,
        ],
        [pltpu.VMEM((4, 144, width), BF16), pltpu.VMEM((4, 16, width), F32)],
        spare=8,
    )
    slots_near, slots_far = kernel_call(
        slots_kernel,
        [shape(144), shape(144)],
        [slots_kept, pair(slots_sent)],
        scalars=0,
        tied=[feed_kept[0]],
    )
    share_sums = relay(own_part, x_part, y_part)
    input_grad = kernel_call(
        input_kernel, [rows], [*share_sums, chunk, par, dresid], scalars=0, cost=10
    )[0]
    slot_sum = kernel_call(
        sum_kernel,
        [shape(144)],
        [slots_near, shift(slots_far, 2)],
        scalars=0,
        tied=[share_sums[0]],
    )[0]
    last_pieces = spread(slot_sum)
    feed_sum = kernel_call(
        feed_sum_kernel,
        [shape(288)],
        [feed_near, shift(feed_far, 2), shift(out_next, 1), shift(out_last, 3)],
        scalars=0,
        tied=[*last_pieces[2::2], input_grad],
    )[0]
    sizes = [256] * 6 + [1024, 512]
    qkv_grad, *vectors = kernel_call(
        last_grads_kernel,
        [shaped((768, width), F32), *(shaped((1, size), F32) for size in sizes)],
        [ids, *last_pieces],
        spare=14,
        cost=10,
    )
    feed_parts = spread_relayed(feed_sum, 144, qkv_grad)
    vmem, hbm = pl.BlockSpec(memory_space=pltpu.VMEM), pl.BlockSpec(memory_space=pltpu.HBM)

    def write(body, parts, count, before, cost):
        return pl.pallas_call(
            body,
            out_shape=[shaped((width, width), F32)] * 2 + [shaped((256, width), F32)],
            in_specs=[pl.BlockSpec(memory_space=pltpu.SMEM)]
            + [vmem] * len(parts)
            + [hbm] * len(before),
            out_specs=[hbm] * 3,
            input_output_aliases={1 + len(parts) + i: i for i in range(len(before))},
            scratch_shapes=[
                pltpu.VMEM((count, 288, width), F32),
                pltpu.SemaphoreType.DMA((3 * count,)),
            ],
            compiler_params=pltpu.CompilerParams(vmem_limit_bytes=16 * 1024 * 1024),
            cost_estimate=pl.CostEstimate(
                flops=int(cost * 1e9), bytes_accessed=0, transcendentals=0
            ),
        )(ids, *parts, *before)

    body = functools.partial(feed_grads_kernel, count=6, first=0)
    grads = write(body, feed_parts[:6], 6, [], 10)
    tails = [*feed_parts[6], *feed_parts[7]]
    up_grad, down_grad, out_grad = write(feed_grads_last_kernel, tails, 2, grads, 0)
    g1, s1, ob, g2, s2, db, ub, bias_grad = (v.reshape(v.shape[1]) for v in vectors)
    return (
        layer_out.reshape(tokens.shape),
        input_grad.reshape(tokens.shape),
        g1,
        s1,
        qkv_grad,
        bias_grad,
        out_grad,
        ob,
        g2,
        s2,
        up_grad,
        ub,
        down_grad,
        db,
    )


def on_small_slice(mesh, tokens, slopes):
    return (
        mesh.shape["ctx"] == 8
        and mesh.shape["fsdp"] == 4
        and tokens.shape == (4, 2, 1024, 1024)
        and slopes.shape == (16,)
    )


def solution(mesh):
    in_specs = (
        P("fsdp", None, "ctx", None),
        P("fsdp", None, "ctx"),
        P(),
        P("fsdp"),
        P("fsdp"),
        P("fsdp", None),
        P("fsdp"),
        P("fsdp", None),
        P("fsdp"),
        P("fsdp"),
        P("fsdp"),
        P("fsdp", None),
        P("fsdp"),
        P("fsdp", None),
        P("fsdp"),
        P("fsdp", None, "ctx", None),
    )
    out_specs = (
        P("fsdp", None, "ctx", None),
        P("fsdp", None, "ctx", None),
        P("fsdp"),
        P("fsdp"),
        P("fsdp", None),
        P("fsdp"),
        P("fsdp", None),
        P("fsdp"),
        P("fsdp"),
        P("fsdp"),
        P("fsdp", None),
        P("fsdp"),
        P("fsdp", None),
        P("fsdp"),
    )
    def layer(*args):
        body = per_device if on_small_slice(mesh, args[0], args[2]) else gathered_device
        return jax.shard_map(
            body, mesh=mesh, in_specs=in_specs, out_specs=out_specs, check_vma=False
        )(*args)

    return layer
```
